128 devices in a mesh: grp: 8 (over z, core), mem: 16 (over y, x).
Axes of the slice: x: 4, y: 4, z: 4, core: 2. Of those that a mesh axis runs over, the one named last changes fastest.
Arguments:
- forcing: float32 [3, 1024, 4096], P(None, ('grp', 'mem')), may hold values from -6 to 6
- viscosity: float32 [1024, 4096], P(('grp', 'mem')), may hold values from 0.1 to 10
- refinement: int32 [1024], P(('grp', 'mem')), may hold values from 0 to 1
- face_owner: int32 [4096, 1], P(('grp', 'mem')), may hold values from 0 to 15; in each aligned block of 32 rows (0 to 31, 32 to 63, ...) at most 4 rows name the same one
- face_block: int32 [1024, 4], P(('grp', 'mem')), may hold values from 0 to 7
- plane_block: int32 [1024, 2], P(('grp', 'mem')), may hold values from 0 to 7
- hanging: int32 [1024, 6], P(('grp', 'mem')), may hold values 0 or 1
- coarse_solver: float32 [8, 384, 384], P('grp', 'mem'), may hold values from -0.3125 to 0.3125
Outputs:
- velocity: float32 [3, 1024, 4096], P(None, ('grp', 'mem'))
- residual: float32 [3, 1024, 4096], P(None, ('grp', 'mem'))
The draws below stay inside these ranges and needn't reach their ends.
Inputs may be any that keep to these rules, and one draw needn't show every extreme that they name: `face_owner`: among the 32 rows of one device no member appears more than 4 times, and some member appears exactly 4 times.
All inputs are finite; a program needn't handle non-finite values. No bound on the sum of `hanging` on one device may be relied on, other than what follows from the above.
Results may differ from the reference program's by a relative error of at most 0.0001.
Values sent between devices are 32-bit elements; how exact they have to be, the bound alone decides.
A program may use at most 64 MiB of HBM per device.

```python
import math
import jax
import jax.numpy as jnp
import numpy as np
from jax import lax

EDGE = 16
B_DEV = 8
DEG = 3
CELLS = 4096
FACE = 256
BLOCKS = 1024
CAP = 4
NC = 384
N_GRP = 8
N_MEM = 16


def place_ends(values, rng, smallest, top_value):
    place = [jax.random.randint(jax.random.fold_in(rng, axis), (), 0, length) for axis, length in enumerate(values.shape)]
    longest = values.shape.index(max(values.shape))
    next_to = place[:longest] + [(place[longest] + 1) % values.shape[longest]] + place[longest + 1:]
    return values.at[tuple(place)].set(smallest).at[tuple(next_to)].set(top_value)


def level_of(rng, dims, pieces, smallest, largest):
    loudness, own = 1.0, jax.random.fold_in(rng, 6)
    for dim, parts in pieces:
        steps = jnp.exp(jax.random.uniform(jax.random.fold_in(own, dim), (parts,), jnp.float32, smallest / len(pieces), largest / len(pieces)))
        loudness = loudness * jnp.repeat(steps, dims[dim] // parts).reshape([-1 if axis == dim else 1 for axis in range(len(dims))])
    return loudness


def shared_out(stream_key, own, number, rows, amount, top, most, slope):
    order = jax.random.permutation(stream_key, amount)
    crowded, usual = load_shares(amount, rows * top, most, slope, True), load_shares(amount, rows * top, most, slope, False)
    places = jnp.arange(amount)

    def named(lengths, turn):
        used = int((lengths > 0).sum())
        fixed = max(1, used // 4)
        moved = fixed + (places - fixed + turn * (used - fixed)) % max(1, amount - fixed)
        return jnp.zeros((amount,), jnp.int32).at[order[jnp.where(places < fixed, places, moved)]].set(jnp.asarray(lengths, jnp.int32))

    lengths = jnp.where(number % 4 == 0, named(crowded, number // 4), named(usual, number - number // 4 - 1))
    mixed = jax.random.permutation(jax.random.fold_in(own, 3), amount)
    donor, sink = mixed[0:amount // 2 * 2:2], mixed[1:amount // 2 * 2:2]
    margin = jnp.minimum(lengths[donor] - 1, most - lengths[sink]) // 2
    margin = jnp.where((donor == order[0]) | (sink == order[0]) | (lengths[sink] == 0), 0, jnp.maximum(margin, 0))
    moved = jax.random.randint(jax.random.fold_in(own, 4), (amount // 2,), 0, 1 << 20) % (margin + 1)
    lengths = lengths.at[donor].add(-moved).at[sink].add(moved)
    members = jnp.searchsorted(jnp.cumsum(lengths), jnp.arange(rows * top), side="right").astype(jnp.int32)
    grid = members.reshape(top, rows).T
    grid = grid[jax.random.permutation(jax.random.fold_in(own, 1), rows)]
    turn = jax.random.randint(jax.random.fold_in(own, 2), (rows, 1), 0, top)
    return jnp.take_along_axis(grid, (jnp.arange(top)[None, :] + turn) % top, axis=1)


def load_shares(amount, total, reach, skew, full):
    weights = [(1 << 20) // math.isqrt(rank ** skew) + 1 for rank in range(1, amount + 1)]
    largest = reach if full else min(reach, max(-(-total // amount), total * weights[0] // sum(weights)))
    least = 1 if total - largest >= amount - 1 else 0
    holding, surplus = [largest] + [least] * (amount - 1), total - largest - least * (amount - 1)
    while surplus > 0:
        candidates = [i for i in range(1, amount) if holding[i] < largest] or [i for i in range(1, amount) if holding[i] < reach]
        pool, remaining = sum([weights[i] for i in candidates]), surplus
        for i in candidates:
            addition = min(reach - holding[i], max(1, remaining * weights[i] // pool), surplus)
            holding[i] = holding[i] + addition
            surplus = surplus - addition
    return np.array(holding)


def centred(key, shape, deviation, reach, shards=(), kind=jnp.bfloat16):
    values = deviation * jax.random.normal(key, shape, jnp.float32)
    if shards:
        values = values * level_of(key, shape, shards, -0.22, 0.18)
    return jnp.clip(values, -reach, reach).astype(kind)


def setup_inputs(seed: int = 0) -> dict:
    seeds = jax.random.split(jax.random.key(seed), 9)
    forcing = centred(seeds[0], (3, BLOCKS, CELLS), 1.0, 6.0, ((1, 128),), jnp.float32)
    viscosity = jnp.clip(jnp.exp(math.log(10.0) - 4.6051702 * jax.random.uniform(seeds[1], (BLOCKS, CELLS), jnp.float32) ** level_of(seeds[1], (BLOCKS, CELLS), ((0, 128),), -0.2, 0.2)), 0.1, 10.0)
    refinement = place_ends(jax.random.randint(seeds[2], (BLOCKS,), 0, 2), jax.random.fold_in(seeds[2], 1), 0, 1).astype(jnp.int32)
    face_owner_keys = jax.random.split(jax.random.fold_in(seeds[3], 1), (4 * BLOCKS) // (4 * B_DEV))
    face_owner_turns = jax.random.permutation(jax.random.fold_in(seeds[3], 3), (4 * BLOCKS) // (4 * B_DEV))
    face_owner = jax.vmap(lambda own, number: shared_out(jax.random.fold_in(seeds[3], 2), own, number, 4 * B_DEV, N_MEM, 1, CAP, 2))(face_owner_keys, face_owner_turns).reshape((4 * BLOCKS, 1))
    face_block = place_ends(jax.random.randint(seeds[4], (BLOCKS, 4), 0, B_DEV), jax.random.fold_in(seeds[4], 1), 0, B_DEV - 1).astype(jnp.int32)
    plane_block = place_ends(jax.random.randint(seeds[5], (BLOCKS, 2), 0, B_DEV), jax.random.fold_in(seeds[5], 1), 0, B_DEV - 1).astype(jnp.int32)
    hanging = place_ends((jax.random.randint(seeds[6], (BLOCKS, 6), 0, 4) < 1).astype(jnp.int32), jax.random.fold_in(seeds[6], 1), 0, 1)
    coarse_solver = centred(seeds[7], (N_GRP, NC, NC), NC ** -0.5, 0.3125, ((0, 8), (1, 16)), jnp.float32)
    return {"forcing": forcing, "viscosity": viscosity, "refinement": refinement, "face_owner": face_owner, "face_block": face_block, "plane_block": plane_block, "hanging": hanging, "coarse_solver": coarse_solver}


MASS_TERM = 1.0
LOWER_BOUND = 0.25
UPPER_BOUND = 2.0

def face_set(values):
    leading = values.shape[:-1]
    cube_view = values.reshape(leading + (EDGE, EDGE, EDGE))
    return [cube_view[..., 0].reshape(leading + (FACE,)), cube_view[..., EDGE - 1].reshape(leading + (FACE,)), cube_view[..., :, 0, :].reshape(leading + (FACE,)), cube_view[..., :, EDGE - 1, :].reshape(leading + (FACE,)), cube_view[..., 0, :, :].reshape(leading + (FACE,)), cube_view[..., EDGE - 1, :, :].reshape(leading + (FACE,))]

def coarsen(plane_vals):
    leading = plane_vals.shape[:-1]
    squares = plane_vals.reshape(leading + (EDGE // 2, 2, EDGE // 2, 2))
    average = lax.optimization_barrier(jnp.mean(squares, axis=(-3, -1), keepdims=True))
    return jnp.broadcast_to(average, squares.shape).reshape(leading + (FACE,))

def spread(plane_vals):
    leading = plane_vals.shape[:-1]
    shaped = plane_vals.reshape(leading + (EDGE, 1, EDGE))
    return jnp.broadcast_to(shaped, leading + (EDGE, EDGE, EDGE)).reshape(leading + (CELLS,))

def beside(values, ghosts):
    leading = values.shape[:-1]
    cell_index = jnp.arange(CELLS, dtype=jnp.int32)
    along_k = cell_index % EDGE
    along_j = cell_index // EDGE % EDGE
    zero_one = jnp.zeros(leading + (1,), jnp.float32)
    zero_row = jnp.zeros(leading + (EDGE,), jnp.float32)
    return [jnp.where(along_k == 0, jnp.repeat(ghosts[0], EDGE, axis=-1), jnp.concatenate([zero_one, values[..., :-1]], axis=-1)), jnp.where(along_k == EDGE - 1, jnp.repeat(ghosts[1], EDGE, axis=-1), jnp.concatenate([values[..., 1:], zero_one], axis=-1)), jnp.where(along_j == 0, spread(ghosts[2]), jnp.concatenate([zero_row, values[..., :-EDGE]], axis=-1)), jnp.where(along_j == EDGE - 1, spread(ghosts[3]), jnp.concatenate([values[..., EDGE:], zero_row], axis=-1)), jnp.concatenate([ghosts[4], values[..., :-FACE]], axis=-1), jnp.concatenate([values[..., FACE:], ghosts[5]], axis=-1)]

def reference(forcing, viscosity, refinement, face_owner, face_block, plane_block, hanging, coarse_solver):
    effective = viscosity * jnp.exp2(-refinement.astype(jnp.float32))[:, None]
    stride = N_MEM * B_DEV
    block_ids = jnp.arange(BLOCKS, dtype=jnp.int32)
    group_base = block_ids // stride * stride
    local_idx = block_ids % B_DEV
    owners = face_owner.reshape(BLOCKS, 4)
    sources = [group_base + owners[:, direction] * B_DEV + face_block[:, direction] for direction in range(4)]
    lower_src = jnp.clip(block_ids - stride - local_idx + plane_block[:, 0], 0, BLOCKS - 1).astype(jnp.int32)
    upper_src = jnp.clip(block_ids + stride - local_idx + plane_block[:, 1], 0, BLOCKS - 1).astype(jnp.int32)
    lower_valid = block_ids >= stride
    upper_valid = block_ids < BLOCKS - stride

    def ghost_set(stacked):
        planes = face_set(stacked)
        result = []
        for direction in range(4):
            result.append(planes[direction ^ 1][:, sources[direction]])
        result.append(jnp.where(lower_valid[None, :, None], planes[5][:, lower_src], 0.0))
        result.append(jnp.where(upper_valid[None, :, None], planes[4][:, upper_src], 0.0))
        return [jnp.where(hanging[:, direction][None, :, None] == 1, coarsen(result[direction]), result[direction]) for direction in range(6)]
    nearby_eff = beside(effective[None], ghost_set(effective[None]))
    weights = [0.5 * (effective + nearby_eff[direction][0]) for direction in range(6)]
    diagonal = MASS_TERM * effective
    for direction in range(6):
        diagonal = diagonal + weights[direction]

    def operate(values):
        nearby = beside(values, ghost_set(values))
        applied = diagonal * values
        for direction in range(6):
            applied = applied - weights[direction] * nearby[direction]
        return applied
    midpoint = 0.5 * (UPPER_BOUND + LOWER_BOUND)
    half_width = 0.5 * (UPPER_BOUND - LOWER_BOUND)
    sigma_ratio = midpoint / half_width

    def smooth(solution, residual):
        rho_now = 1.0 / sigma_ratio
        step_dir = residual / (diagonal * midpoint)
        for sweep_index in range(DEG):
            solution = solution + step_dir
            residual = residual - operate(step_dir)
            if sweep_index < DEG - 1:
                rho_next = 1.0 / (2.0 * sigma_ratio - rho_now)
                step_dir = rho_next * rho_now * step_dir + 2.0 * rho_next / half_width * (residual / diagonal)
                rho_now = rho_next
        return (solution, residual)
    solution, residual = smooth(jnp.zeros_like(forcing), forcing)
    coarse_vec = (lax.optimization_barrier(jnp.sum(residual, axis=-1)) / math.sqrt(CELLS)).T.reshape(N_GRP, NC)
    correction = jnp.einsum('gij,gj->gi', coarse_solver, coarse_vec, precision=lax.Precision.HIGHEST)
    lifted = jnp.broadcast_to(correction.reshape(BLOCKS, 3).T[:, :, None], forcing.shape)
    solution = solution + lifted
    residual = residual - operate(lifted)
    solution, residual = smooth(solution, residual)
    return (solution, residual)
```

```python
import functools
import math

import jax
import jax.numpy as jnp
from jax import lax
from jax.experimental import pallas as pl
from jax.experimental.pallas import tpu as pltpu
from jax.sharding import PartitionSpec as P

MESH = pl.DeviceIdType.MESH
EDGE = 16
DEG = 3
CELLS = 4096
FACE = 256
LANES = 128
CAP = 4
MASS_TERM = 1.0
LOWER_BOUND = 0.25
UPPER_BOUND = 2.0
SWEEPS = 2 * DEG
F32 = jnp.float32
BF16 = jnp.bfloat16
REQUEST, EFFECTIVE, CORRECTION = 0, 1, 2


def chebyshev():
    theta = 0.5 * (UPPER_BOUND + LOWER_BOUND)
    delta = 0.5 * (UPPER_BOUND - LOWER_BOUND)
    sigma = theta / delta
    rho = 1.0 / sigma
    steps = [(0.0, 1.0 / theta)]
    for _ in range(DEG - 1):
        rho_next = 1.0 / (2.0 * sigma - rho)
        steps.append((rho_next * rho, 2.0 * rho_next / delta))
        rho = rho_next
    return steps


def by_step(step, values):
    result = jnp.float32(values[-1])
    for place in range(len(values) - 2, -1, -1):
        result = jnp.where(step == place, jnp.float32(values[place]), result)
    return result


def iota(shape, dim):
    return lax.broadcasted_iota(jnp.int32, shape, dim)


def turn(x, shift):
    shift = shift % LANES
    return x if shift == 0 else pltpu.roll(x, shift, 1)


def part(i, v):
    return pl.ds(i * FACE + v * LANES, LANES)


def pick(one_hot, values):
    high = values.astype(BF16)
    rest = values - high.astype(F32)
    middle = rest.astype(BF16)
    low = (rest - middle.astype(F32)).astype(BF16)

    def product(piece):
        return jnp.dot(one_hot, piece, preferred_element_type=F32)

    return product(high) + (product(middle) + product(low))


def coarsen(x):
    lane = iota(x.shape, 1)
    x = x + jnp.where(lane % 2 == 0, turn(x, -1), turn(x, 1))
    x = x + jnp.where(lane // EDGE % 2 == 0, turn(x, -EDGE), turn(x, EDGE))
    return 0.25 * x


def extract(read):
    lane = iota((8, LANES), 1)
    in_row, row = lane % EDGE, lane // EDGE
    zero = jnp.zeros((8, LANES), F32)
    faces = {(v, d): zero for v in range(2) for d in range(4)}
    for i in range(EDGE):
        halves = (read(i, 0), read(i, 1))
        for v in range(2):
            moved = turn(halves[v], i)
            faces[v, 0] = jnp.where(in_row == i, moved, faces[v, 0])
            faces[v, 1] = jnp.where(in_row == (i - 1) % EDGE, moved, faces[v, 1])
        v = i // 8
        moved = turn(jnp.where(lane < EDGE, halves[0], halves[1]), i % 8 * EDGE)
        faces[v, 2] = jnp.where(row == i % 8, moved, faces[v, 2])
        faces[v, 3] = jnp.where(row == (i - 1) % 8, moved, faces[v, 3])
    for v in range(2):
        faces[v, 1] = turn(faces[v, 1], -(EDGE - 1))
        faces[v, 3] = turn(faces[v, 3], EDGE)
    return faces


def tables(owner, face_block, plane_block, hanging, members, has_lower, has_upper):
    wide = members * 8
    rows, columns = iota((32, 32), 0), iota((32, 32), 1)
    given = 4 * (rows % 8) + rows // 8
    given_t = 4 * (columns % 8) + columns // 8
    across = jnp.sum(jnp.where(rows == columns, owner, 0), axis=0, keepdims=True)
    owner_col = jnp.sum(jnp.where(columns == given, across, 0), axis=1, keepdims=True)
    owner_row = jnp.sum(jnp.where(rows == given_t, owner, 0), axis=0, keepdims=True)
    same = owner_col == owner_row
    rank_col = jnp.sum(jnp.where(same & (columns < rows), 1, 0), axis=1, keepdims=True)
    rank_row = jnp.sum(jnp.where(same & (rows < columns), 1, 0), axis=0, keepdims=True)

    def spread(table, first, groups, of_row):
        tall = jnp.concatenate([table] * groups, axis=0)
        mask = iota(tall.shape, 1) == first + of_row(iota(tall.shape, 0))
        return jnp.sum(jnp.where(mask, tall, 0), axis=1, keepdims=True)

    block_col = spread(face_block, 0, 4, lambda r: r // 8)
    side = iota((32, 1), 0) // 8
    wanted = (side + 1 - 2 * (side % 2)) * 8 + block_col
    slot_col = owner_col * 8 + rank_col
    slot_row = owner_row * 8 + rank_row

    def ones(mask):
        return jnp.where(mask, 1.0, 0.0).astype(BF16)

    lanes = iota((32, wide), 1)
    unpack = jnp.concatenate([ones(lanes == slot_col + CAP * v) for v in range(2)], axis=0)
    slots = iota((wide, 32), 0)
    unpack_t = jnp.concatenate([ones(slots == slot_row + CAP * v) for v in range(2)], axis=1)
    lanes = iota((32, LANES), 1)
    source = jnp.concatenate([ones(lanes == wanted + 32 * v) for v in range(2)], axis=0)
    request = jnp.dot(unpack_t, source, preferred_element_type=F32)
    plane_col = spread(plane_block, 0, 4, lambda r: r // 16)
    which = iota((32, 32), 0) // 16
    inside = jnp.where(which == 0, has_lower, has_upper) == 1
    plane_pick = ones((columns == rows // 8 * 8 + plane_col) & inside)
    lift_pick = ones(iota((32, wide), 1) == owner_col * 8 + block_col)
    near_hang = spread(hanging, 0, 4, lambda r: r // 8)
    plane_hang = spread(hanging, 4, 4, lambda r: r // 16)
    near_hang = jnp.broadcast_to(near_hang.astype(F32), (32, LANES))
    plane_hang = jnp.broadcast_to(plane_hang.astype(F32), (32, LANES))
    return unpack, request, plane_pick, lift_pick, near_hang, plane_hang


def kernel(
    n_grp,
    n_mem,
    forcing,
    viscosity,
    refinement,
    face_owner,
    face_block,
    plane_block,
    hanging,
    coarse_solver,
    velocity,
    residual,
    effective,
    weight_k,
    weight_j,
    weight_i,
    ghost_k,
    ghost_j,
    diagonal,
    inverse,
    step_dir,
    faces,
    ghosts,
    plane_ghosts,
    hang_near,
    hang_plane,
    unpack_mat,
    pack_mat,
    plane_mat,
    lift_mat,
    solver_rows,
    out_big,
    in_big,
    out_small,
    in_small,
    out_plane,
    in_plane,
    send_big,
    recv_big,
    send_small,
    recv_small,
    send_plane,
    recv_plane,
):
    grp, mem = lax.axis_index("grp"), lax.axis_index("mem")
    above = lax.rem(grp + 1, n_grp)
    below = lax.rem(grp + n_grp - 1, n_grp)
    n_coarse = n_mem * 24
    groups_of_lanes = -(-n_coarse // LANES)
    wide = n_mem * 8
    COARSE = SWEEPS

    barrier = pltpu.get_barrier_semaphore()
    for offset in range(1, n_mem):
        pl.semaphore_signal(
            barrier, inc=1, device_id={"mem": lax.rem(mem + offset, n_mem)}, device_id_type=MESH
        )
    for other in (above, below):
        pl.semaphore_signal(barrier, inc=1, device_id={"grp": other}, device_id_type=MESH)

    lane = iota((8, LANES), 1)
    in_row = lane % EDGE
    first_k, last_k = in_row == 0, in_row == EDGE - 1
    first_row, last_row = lane < EDGE, lane >= LANES - EDGE

    def send(outgoing, incoming, which, send_sem, recv_sem):
        for offset in range(1, n_mem):
            to = lax.rem(mem + offset, n_mem)
            pltpu.make_async_remote_copy(
                src_ref=outgoing.at[which, to],
                dst_ref=incoming.at[which, mem],
                send_sem=send_sem.at[which],
                recv_sem=recv_sem.at[which],
                device_id={"mem": to},
                device_id_type=MESH,
            ).start()

    def all_of(buffer, which, sem):
        span = buffer.at[which, pl.ds(0, n_mem - 1)]
        pltpu.make_async_copy(span, span, sem.at[which]).wait()

    def plane_copy(which, side):
        return pltpu.make_async_remote_copy(
            src_ref=out_plane.at[which, side],
            dst_ref=in_plane.at[which, side],
            send_sem=send_plane.at[which, side],
            recv_sem=recv_plane.at[which, side],
            device_id={"grp": above if side == 0 else below},
            device_id_type=MESH,
        )

    unpack, request, plane_pick, lift_pick, near_hang, plane_hang = tables(
        face_owner[...],
        face_block[...],
        plane_block[...],
        hanging[...],
        n_mem,
        jnp.where(grp > 0, 1, 0),
        jnp.where(grp < n_grp - 1, 1, 0),
    )
    unpack_mat[...] = unpack
    plane_mat[...] = plane_pick
    lift_mat[...] = lift_pick
    hang_near[...] = near_hang
    hang_plane[...] = plane_hang
    out_small[REQUEST] = request.reshape(n_mem, 8, LANES)

    pl.semaphore_wait(barrier, n_mem - 1 + 2)

    send(out_small, in_small, REQUEST, send_small, recv_small)
    in_small[REQUEST, mem] = out_small[REQUEST, mem]

    block_row = iota((8, LANES), 0)
    level = jnp.zeros((8, LANES), jnp.int32)
    for b in range(8):
        level = jnp.where(block_row == b, refinement[b], level)
    scale = 1.0 / jnp.left_shift(jnp.ones_like(level), level).astype(F32)
    for i in range(EDGE):
        for v in range(2):
            effective[:, part(i, v)] = viscosity[:, part(i, v)] * scale

    def send_planes(which, channels, read):
        for c in range(channels):
            for v in range(2):
                out_plane[which, 0, c, pl.ds(8 * v, 8), :] = read(c, EDGE - 1, v)
                out_plane[which, 1, c, pl.ds(8 * v, 8), :] = read(c, 0, v)
        for side in range(2):
            plane_copy(which, side).start()

    for side in range(2):
        for c in range(1, 3):
            out_plane[SWEEPS, side, c] = jnp.zeros((16, LANES), F32)
    send_planes(SWEEPS, 1, lambda c, i, v: effective[:, part(i, v)])
    found = extract(lambda i, v: effective[:, part(i, v)])
    for (v, d), register in found.items():
        faces[0, pl.ds(v * 32 + d * 8, 8), :] = register

    all_of(in_small, REQUEST, recv_small)
    pack_mat[...] = in_small[REQUEST].reshape(wide, LANES)[:, :64].astype(BF16)
    out_small[EFFECTIVE] = pick(pack_mat[...], faces[0]).reshape(n_mem, 8, LANES)
    send(out_small, in_small, EFFECTIVE, send_small, recv_small)
    in_small[EFFECTIVE, mem] = out_small[EFFECTIVE, mem]

    rows, columns = iota((24, 24), 0), iota((24, 24), 1)
    reorder = jnp.where(columns == 3 * (rows % 8) + rows // 8, 1.0, 0.0).astype(BF16)
    solver_rows[:, pl.ds(0, n_coarse)] = pick(reorder, coarse_solver[0])
    if n_coarse % LANES:
        spare = groups_of_lanes * LANES - n_coarse
        solver_rows[:, pl.ds(n_coarse, spare)] = jnp.zeros((24, spare), F32)
    for c in range(3):
        for i in range(EDGE):
            for v in range(2):
                residual[c, :, part(i, v)] = forcing[c, :, part(i, v)]
                velocity[c, :, part(i, v)] = jnp.zeros((8, LANES), F32)
                step_dir[c, :, part(i, v)] = jnp.zeros((8, LANES), F32)
    for i in range(EDGE):
        own = [effective[:, part(i, v)] for v in range(2)]
        back = [turn(x, EDGE) for x in own]
        ahead = [turn(x, -EDGE) for x in own]
        for v in range(2):
            x = own[v]
            lower_k = jnp.where(first_k, 0.0, 0.5 * (x + turn(x, 1)))
            upper_k = jnp.where(last_k, 0.0, 0.5 * (x + turn(x, -1)))
            if v == 0:
                lower_j = jnp.where(first_row, 0.0, 0.5 * (x + back[0]))
                upper_j = 0.5 * (x + jnp.where(last_row, ahead[1], ahead[0]))
            else:
                lower_j = 0.5 * (x + jnp.where(first_row, back[0], back[1]))
                upper_j = jnp.where(last_row, 0.0, 0.5 * (x + ahead[1]))
            weight_k[0, :, part(i, v)] = lower_k
            weight_k[1, :, part(i, v)] = upper_k
            weight_j[0, :, part(i, v)] = lower_j
            weight_j[1, :, part(i, v)] = upper_j
            if i > 0:
                weight_i[:, part(i, v)] = 0.5 * (x + effective[:, part(i - 1, v)])
            diagonal[:, part(i, v)] = MASS_TERM * x + lower_k + upper_k + lower_j + upper_j

    def settle(values, hang):
        return jnp.where(hang == 1.0, coarsen(values), values)

    def side_by_side(buffer, channels):
        return jnp.concatenate([buffer(c) for c in range(channels)], axis=1)

    def receive_planes(which, channels):
        for side in range(2):
            plane_copy(which, side).wait_recv()
        arrived = side_by_side(
            lambda c: in_plane[which, :, c].reshape(32, LANES), channels
        )
        picked = pick(plane_mat[...], arrived)
        for c in range(channels):
            plane_ghosts[c] = settle(picked[:, c * LANES : (c + 1) * LANES], hang_plane[...])

    def unpack_near(arrived, channels):
        picked = pick(unpack_mat[...], arrived)
        for c in range(channels):
            for v in range(2):
                ghosts[c, pl.ds(32 * v, 32), :] = settle(
                    picked[32 * v : 32 * v + 32, c * LANES : (c + 1) * LANES], hang_near[...]
                )

    def ghost(c, d, v):
        return ghosts[c, pl.ds(v * 32 + d * 8, 8), :]

    def plane_ghost(c, side, v):
        return plane_ghosts[c, pl.ds(side * 16 + v * 8, 8), :]

    def k_ghost(c, i, v):
        return jnp.where(first_k, turn(ghost(c, 0, v), -i), turn(ghost(c, 1, v), EDGE - 1 - i))

    def j_ghost(c, i, v):
        shift = -(i % 8) * EDGE
        if v == 0:
            return turn(ghost(c, 2, i // 8), shift)
        return turn(ghost(c, 3, i // 8), LANES - EDGE + shift)

    receive_planes(SWEEPS, 1)
    for v in range(2):
        weight_i[:, part(0, v)] = 0.5 * (effective[:, part(0, v)] + plane_ghost(0, 0, v))
        weight_i[:, part(EDGE, v)] = 0.5 * (effective[:, part(EDGE - 1, v)] + plane_ghost(0, 1, v))
    all_of(in_small, EFFECTIVE, recv_small)
    unpack_near(in_small[EFFECTIVE].reshape(wide, LANES), 1)
    for i in range(EDGE):
        for v in range(2):
            x = effective[:, part(i, v)]
            at_k = jnp.where(first_k | last_k, 0.5 * (x + k_ghost(0, i, v)), 0.0)
            edge = first_row if v == 0 else last_row
            at_j = jnp.where(edge, 0.5 * (x + j_ghost(0, i, v)), 0.0)
            ghost_k[:, part(i, v)] = at_k
            ghost_j[:, part(i, v)] = at_j
            whole = (
                diagonal[:, part(i, v)]
                + (weight_i[:, part(i, v)] + weight_i[:, part(i + 1, v)])
                + (at_k + at_j)
            )
            diagonal[:, part(i, v)] = whole
            inverse[:, part(i, v)] = 1.0 / whole

    steps = chebyshev()

    def coarse_level():
        totals = []
        for c in range(3):
            total = jnp.zeros((8, LANES), F32)
            for i in range(EDGE):
                for v in range(2):
                    total = total + residual[c, :, part(i, v)]
            totals.append(jnp.sum(total, axis=1, keepdims=True) / math.sqrt(CELLS))
        for q in range(groups_of_lanes):
            place = lane + q * LANES - 24 * mem - 3 * block_row
            mine = jnp.zeros((8, LANES), F32)
            for c in range(3):
                mine = jnp.where(place == c, totals[c], mine)
            for m in range(n_mem):
                out_big[COARSE, m, q] = mine
        for q in range(groups_of_lanes, 3):
            for m in range(n_mem):
                out_big[COARSE, m, q] = jnp.zeros((8, LANES), F32)
        send(out_big, in_big, COARSE, send_big, recv_big)
        in_big[COARSE, mem] = out_big[COARSE, mem]
        all_of(in_big, COARSE, recv_big)
        products = [jnp.zeros((8, LANES), F32)] * 3
        for q in range(groups_of_lanes):
            vector = in_big[COARSE, 0, q]
            for m in range(1, n_mem):
                vector = vector + in_big[COARSE, m, q]
            vector = jnp.sum(vector, axis=0, keepdims=True)
            for c in range(3):
                products[c] = products[c] + solver_rows[
                    pl.ds(8 * c, 8), pl.ds(q * LANES, LANES)
                ] * vector
        own = [jnp.sum(products[c], axis=1, keepdims=True) for c in range(3)]
        tile = jnp.zeros((8, LANES), F32)
        for c in range(3):
            tile = jnp.where(lane == c, own[c], tile)
        for m in range(n_mem):
            out_small[CORRECTION, m] = tile
        send(out_small, in_small, CORRECTION, send_small, recv_small)
        in_small[CORRECTION, mem] = tile
        for side in range(2):
            for c in range(3):
                out_plane[SWEEPS + 1, side, c] = jnp.concatenate([tile, tile], axis=0)
            plane_copy(SWEEPS + 1, side).start()
        for side in range(2):
            plane_copy(SWEEPS + 1, side).wait_recv()
        far = pick(plane_mat[...], in_plane[SWEEPS + 1, :, 0].reshape(32, LANES))
        all_of(in_small, CORRECTION, recv_small)
        near = pick(lift_mat[...], in_small[CORRECTION].reshape(wide, LANES))
        for c in range(3):
            mine = jnp.broadcast_to(own[c], (8, LANES))

            def difference(values, start):
                return mine - jnp.broadcast_to(values[start : start + 8, c : c + 1], (8, LANES))

            gap = [difference(near, 8 * d) for d in range(4)]
            gap_lower, gap_upper = difference(far, 0), difference(far, 16)
            gap_k = jnp.where(first_k, gap[0], gap[1])
            for i in range(EDGE):
                for v in range(2):
                    change = MASS_TERM * effective[:, part(i, v)] * mine
                    change = change + ghost_k[:, part(i, v)] * gap_k
                    change = change + ghost_j[:, part(i, v)] * gap[2 + v]
                    if i == 0:
                        change = change + weight_i[:, part(0, v)] * gap_lower
                    if i == EDGE - 1:
                        change = change + weight_i[:, part(EDGE, v)] * gap_upper
                    residual[c, :, part(i, v)] = residual[c, :, part(i, v)] - change
                    velocity[c, :, part(i, v)] = velocity[c, :, part(i, v)] + mine

    def sweep(t, carry):
        @pl.when(t == DEG)
        def _():
            coarse_level()

        step = lax.rem(t, DEG)
        keep = by_step(step, [first for first, _ in steps])
        gain = by_step(step, [second for _, second in steps])

        @pl.loop(0, 3)
        def _(c):
            for i in range(EDGE):
                for v in range(2):
                    step_dir[c, :, part(i, v)] = keep * step_dir[c, :, part(i, v)] + gain * (
                        residual[c, :, part(i, v)] * inverse[:, part(i, v)]
                    )
            found = extract(lambda i, v: step_dir[c, :, part(i, v)])
            for (v, d), register in found.items():
                faces[c, pl.ds(v * 32 + d * 8, 8), :] = register

        packed = pick(pack_mat[...], side_by_side(lambda c: faces[c], 3))
        for c in range(3):
            out_big[t, :, c] = packed[:, c * LANES : (c + 1) * LANES].reshape(n_mem, 8, LANES)
        send(out_big, in_big, t, send_big, recv_big)
        send_planes(t, 3, lambda c, i, v: step_dir[c, :, part(i, v)])
        in_big[t, mem] = out_big[t, mem]

        @pl.loop(0, 3)
        def _(c):
            for i in range(EDGE):
                own = [step_dir[c, :, part(i, v)] for v in range(2)]
                back = [turn(x, EDGE) for x in own]
                ahead = [turn(x, -EDGE) for x in own]
                for v in range(2):
                    x = own[v]
                    if v == 0:
                        lower_j, upper_j = back[0], jnp.where(last_row, ahead[1], ahead[0])
                    else:
                        lower_j, upper_j = jnp.where(first_row, back[0], back[1]), ahead[1]
                    change = weight_k[0, :, part(i, v)] * turn(x, 1)
                    change = change + weight_k[1, :, part(i, v)] * turn(x, -1)
                    change = change + weight_j[0, :, part(i, v)] * lower_j
                    change = change + weight_j[1, :, part(i, v)] * upper_j
                    if i > 0:
                        change = change + weight_i[:, part(i, v)] * step_dir[c, :, part(i - 1, v)]
                    if i < EDGE - 1:
                        change = change + weight_i[:, part(i + 1, v)] * step_dir[
                            c, :, part(i + 1, v)
                        ]
                    residual[c, :, part(i, v)] = residual[c, :, part(i, v)] - (
                        diagonal[:, part(i, v)] * x - change
                    )
                    velocity[c, :, part(i, v)] = velocity[c, :, part(i, v)] + x

        receive_planes(t, 3)
        for c in range(3):
            for v in range(2):
                for i, side in ((0, 0), (EDGE - 1, 1)):
                    residual[c, :, part(i, v)] = residual[c, :, part(i, v)] + weight_i[
                        :, part(i + side, v)
                    ] * plane_ghost(c, side, v)
        all_of(in_big, t, recv_big)
        unpack_near(side_by_side(lambda c: in_big[t, :, c].reshape(wide, LANES), 3), 3)

        @pl.loop(0, 3)
        def _(c):
            for i in range(EDGE):
                for v in range(2):
                    change = ghost_k[:, part(i, v)] * k_ghost(c, i, v)
                    change = change + ghost_j[:, part(i, v)] * j_ghost(c, i, v)
                    residual[c, :, part(i, v)] = residual[c, :, part(i, v)] + change

        return carry

    lax.fori_loop(0, SWEEPS, sweep, 0)

    for t in range(SWEEPS + 1):
        all_of(out_big, t, send_big)
    for t in range(3):
        all_of(out_small, t, send_small)
    for t in range(SWEEPS + 2):
        for side in range(2):
            plane_copy(t, side).wait_send()


def solution(mesh):
    n_grp, n_mem = mesh.shape["grp"], mesh.shape["mem"]
    wide = n_mem * 8

    def local(*args):
        field = pltpu.VMEM((8, CELLS), F32)
        vmem = pl.BlockSpec(memory_space=pltpu.VMEM)
        smem = pl.BlockSpec(memory_space=pltpu.SMEM)
        forcing = args[0]
        dma = pltpu.SemaphoreType.DMA
        return pl.pallas_call(
            functools.partial(kernel, n_grp, n_mem),
            out_shape=[jax.ShapeDtypeStruct(forcing.shape, F32)] * 2,
            in_specs=[vmem, vmem, smem, vmem, vmem, vmem, vmem, vmem],
            out_specs=[vmem, vmem],
            scratch_shapes=[
                field,
                pltpu.VMEM((2, 8, CELLS), F32),
                pltpu.VMEM((2, 8, CELLS), F32),
                pltpu.VMEM((8, CELLS + FACE), F32),
                field,
                field,
                field,
                field,
                pltpu.VMEM((3, 8, CELLS), F32),
                pltpu.VMEM((3, 64, LANES), F32),
                pltpu.VMEM((3, 64, LANES), F32),
                pltpu.VMEM((3, 32, LANES), F32),
                pltpu.VMEM((32, LANES), F32),
                pltpu.VMEM((32, LANES), F32),
                pltpu.VMEM((64, wide), BF16),
                pltpu.VMEM((wide, 64), BF16),
                pltpu.VMEM((32, 32), BF16),
                pltpu.VMEM((32, wide), BF16),
                pltpu.VMEM((24, -(-n_mem * 24 // LANES) * LANES), F32),
                pltpu.VMEM((SWEEPS + 1, n_mem, 3, 8, LANES), F32),
                pltpu.VMEM((SWEEPS + 1, n_mem, 3, 8, LANES), F32),
                pltpu.VMEM((3, n_mem, 8, LANES), F32),
                pltpu.VMEM((3, n_mem, 8, LANES), F32),
                pltpu.VMEM((SWEEPS + 2, 2, 3, 16, LANES), F32),
                pltpu.VMEM((SWEEPS + 2, 2, 3, 16, LANES), F32),
                dma((SWEEPS + 1,)),
                dma((SWEEPS + 1,)),
                dma((3,)),
                dma((3,)),
                dma((SWEEPS + 2, 2)),
                dma((SWEEPS + 2, 2)),
            ],
            compiler_params=pltpu.CompilerParams(
                collective_id=0, has_side_effects=True, vmem_limit_bytes=32 * 1024 * 1024
            ),
            name="vcycle",
        )(*args)

    in_specs = (
        P(None, ("grp", "mem"), None),
        P(("grp", "mem"), None),
        P(("grp", "mem")),
        P(("grp", "mem"), None),
        P(("grp", "mem"), None),
        P(("grp", "mem"), None),
        P(("grp", "mem"), None),
        P("grp", "mem", None),
    )
    out_specs = (P(None, ("grp", "mem"), None), P(None, ("grp", "mem"), None))
    return jax.shard_map(local, mesh=mesh, in_specs=in_specs, out_specs=out_specs, check_vma=False)
```

```python
import functools
import math

import jax
import jax.numpy as jnp
from jax import lax
from jax.experimental import pallas as pl
from jax.experimental.pallas import tpu as pltpu
from jax.sharding import PartitionSpec as P

MESH = pl.DeviceIdType.MESH
EDGE = 16
DEG = 3
CELLS = 4096
FACE = 256
LANES = 128
CAP = 4
MASS_TERM = 1.0
LOWER_BOUND = 0.25
UPPER_BOUND = 2.0
SWEEPS = 2 * DEG
F32 = jnp.float32
BF16 = jnp.bfloat16
REQUEST, CORRECTION = 0, 1


def chebyshev():
    theta = 0.5 * (UPPER_BOUND + LOWER_BOUND)
    delta = 0.5 * (UPPER_BOUND - LOWER_BOUND)
    sigma = theta / delta
    rho = 1.0 / sigma
    steps = [(0.0, 1.0 / theta)]
    for _ in range(DEG - 1):
        rho_next = 1.0 / (2.0 * sigma - rho)
        steps.append((rho_next * rho, 2.0 * rho_next / delta))
        rho = rho_next
    return steps


def far_first(members):
    tall = members // 4

    def hops(offset):
        dy, dx = offset
        return min(dy, tall - dy) + min(dx, 4 - dx)

    others = [(dy, dx) for dy in range(tall) for dx in range(4) if (dy, dx) != (0, 0)]
    return sorted(others, key=hops, reverse=True)


def by_step(step, values):
    result = jnp.float32(values[-1])
    for place in range(len(values) - 2, -1, -1):
        result = jnp.where(step == place, jnp.float32(values[place]), result)
    return result


def iota(shape, dim):
    return lax.broadcasted_iota(jnp.int32, shape, dim)


def turn(x, shift):
    shift = shift % LANES
    return x if shift == 0 else pltpu.roll(x, shift, 1)


def part(i, v):
    return pl.ds(i * FACE + v * LANES, LANES)


def parts(values):
    high = values.astype(BF16)
    rest = values - high.astype(F32)
    middle = rest.astype(BF16)
    low = (rest - middle.astype(F32)).astype(BF16)
    return jnp.concatenate([high, middle, low], axis=0)


def thrice(one_hot):
    return jnp.concatenate([one_hot] * 3, axis=1)


def pick(one_hot_thrice, values):
    return jnp.dot(one_hot_thrice, parts(values), preferred_element_type=F32)


def coarsen(x):
    lane = iota(x.shape, 1)
    x = x + jnp.where(lane % 2 == 0, turn(x, -1), turn(x, 1))
    x = x + jnp.where(lane // EDGE % 2 == 0, turn(x, -EDGE), turn(x, EDGE))
    return 0.25 * x


def extract(read):
    lane = iota((8, LANES), 1)
    in_row, row = lane % EDGE, lane // EDGE
    zero = jnp.zeros((8, LANES), F32)
    faces = {(v, d): zero for v in range(2) for d in range(4)}
    for i in range(EDGE):
        halves = (read(i, 0), read(i, 1))
        for v in range(2):
            moved = turn(halves[v], i)
            faces[v, 0] = jnp.where(in_row == i, moved, faces[v, 0])
            faces[v, 1] = jnp.where(in_row == (i - 1) % EDGE, moved, faces[v, 1])
        v = i // 8
        moved = turn(jnp.where(lane < EDGE, halves[0], halves[1]), i % 8 * EDGE)
        faces[v, 2] = jnp.where(row == i % 8, moved, faces[v, 2])
        faces[v, 3] = jnp.where(row == (i - 1) % 8, moved, faces[v, 3])
    for v in range(2):
        faces[v, 1] = turn(faces[v, 1], -(EDGE - 1))
        faces[v, 3] = turn(faces[v, 3], EDGE)
    return faces


def tables(owner, face_block, plane_block, hanging, members, has_lower, has_upper):
    wide = members * 8
    rows, columns = iota((32, 32), 0), iota((32, 32), 1)
    given = 4 * (rows % 8) + rows // 8
    given_t = 4 * (columns % 8) + columns // 8
    owner_col = jnp.sum(jnp.where(columns == given, owner, 0), axis=1, keepdims=True)
    own_col = jnp.sum(jnp.where(rows == columns, owner, 0), axis=1, keepdims=True)
    owner_row = jnp.sum(jnp.where(rows == given_t, own_col, 0), axis=0, keepdims=True)
    same = owner_col == owner_row
    rank_col = jnp.sum(jnp.where(same & (columns < rows), 1, 0), axis=1, keepdims=True)
    rank_row = jnp.sum(jnp.where(same & (rows < columns), 1, 0), axis=0, keepdims=True)

    def spread(table, first, of_row):
        tall = jnp.concatenate([table] * 4, axis=0)
        mask = iota(tall.shape, 1) == first + of_row(iota(tall.shape, 0))
        return jnp.sum(jnp.where(mask, tall, 0), axis=1, keepdims=True)

    def spread_t(table, per):
        lanes, which = iota((32, 8), 1), iota((32, 8), 0)
        tall = jnp.zeros((32, 8), jnp.int32)
        for d in range(table.shape[0]):
            tall = jnp.where(which // per == d, table[d : d + 1], tall)
        return jnp.sum(jnp.where(lanes == which % 8, tall, 0), axis=1, keepdims=True)

    block_col = spread_t(face_block, 8)
    side = iota((32, 1), 0) // 8
    wanted = (side + 1 - 2 * (side % 2)) * 8 + block_col
    slot_col = owner_col * 8 + rank_col
    slot_row = owner_row * 8 + rank_row

    def ones(mask):
        return jnp.where(mask, 1.0, 0.0).astype(BF16)

    lanes = iota((32, wide), 1)
    unpack = jnp.concatenate([ones(lanes == slot_col + CAP * v) for v in range(2)], axis=0)
    slots = iota((wide, 32), 0)
    unpack_t = jnp.concatenate([ones(slots == slot_row + CAP * v) for v in range(2)], axis=1)
    lanes = iota((32, LANES), 1)
    source = jnp.concatenate([ones(lanes % 64 == wanted + 32 * v) for v in range(2)], axis=0)
    request = jnp.dot(unpack_t, source, preferred_element_type=F32)
    lanes = iota((32, members * 64), 1)
    face_pick = jnp.concatenate(
        [ones(lanes == owner_col * 64 + wanted + 32 * v) for v in range(2)], axis=0
    )
    plane_col = spread_t(plane_block, 16)
    which = iota((32, 32), 0) // 16
    inside = jnp.where(which == 0, has_lower, has_upper) == 1
    plane_pick = ones((columns == rows // 8 * 8 + plane_col) & inside)
    lift_pick = ones(iota((32, wide), 1) == owner_col * 8 + block_col)
    near_hang = spread(hanging, 0, lambda r: r // 8)
    plane_hang = spread(hanging, 4, lambda r: r // 16)
    near_hang = jnp.broadcast_to(near_hang.astype(F32), (32, LANES))
    plane_hang = jnp.broadcast_to(plane_hang.astype(F32), (32, LANES))
    return (
        thrice(unpack),
        request,
        thrice(face_pick),
        thrice(plane_pick),
        thrice(lift_pick),
        near_hang,
        plane_hang,
    )


def kernel(
    n_grp,
    n_mem,
    forcing_hbm,
    viscosity_hbm,
    solver_hbm,
    refinement,
    face_owner,
    face_block,
    plane_block,
    hanging,
    result,
    effective,
    solver,
    weight_k,
    weight_j,
    weight_i,
    ghost_k,
    ghost_j,
    diagonal,
    inverse,
    step_dir,
    faces,
    ghosts,
    plane_ghosts,
    hang_near,
    hang_plane,
    unpack_mat,
    pack_mat,
    plane_mat,
    lift_mat,
    face_mat,
    solver_rows,
    out_face,
    in_face,
    out_big,
    in_big,
    out_small,
    in_small,
    out_plane,
    in_plane,
    send_big,
    recv_big,
    send_small,
    recv_small,
    send_plane,
    recv_plane,
    send_face,
    recv_face,
    load_sem,
):
    velocity, residual = result.at[0], result.at[1]
    grp, mem = lax.axis_index("grp"), lax.axis_index("mem")
    above = lax.rem(grp + 1, n_grp)
    below = lax.rem(grp + n_grp - 1, n_grp)
    n_coarse = n_mem * 24
    groups_of_lanes = -(-n_coarse // LANES)
    wide = n_mem * 8
    COARSE = SWEEPS

    mem_y, mem_x = lax.div(mem, 4), lax.rem(mem, 4)
    peers = [
        lax.rem(mem_y + dy, n_mem // 4) * 4 + lax.rem(mem_x + dx, 4) for dy, dx in far_first(n_mem)
    ]
    barrier = pltpu.get_barrier_semaphore()
    for to in peers:
        pl.semaphore_signal(barrier, inc=1, device_id={"mem": to}, device_id_type=MESH)
    for other in (above, below):
        pl.semaphore_signal(barrier, inc=1, device_id={"grp": other}, device_id_type=MESH)

    loads = [
        pltpu.make_async_copy(viscosity_hbm, effective, load_sem.at[0]),
        pltpu.make_async_copy(forcing_hbm, residual, load_sem.at[1]),
        pltpu.make_async_copy(solver_hbm.at[0], solver, load_sem.at[2]),
    ]
    for load in loads:
        load.start()

    lane = iota((8, LANES), 1)
    in_row = lane % EDGE
    row = lane // EDGE
    first_k, last_k = in_row == 0, in_row == EDGE - 1
    first_row, last_row = lane < EDGE, lane >= LANES - EDGE

    def send(outgoing, incoming, which, send_sem, recv_sem):
        for to in peers:
            pltpu.make_async_remote_copy(
                src_ref=outgoing.at[which, to],
                dst_ref=incoming.at[which, mem],
                send_sem=send_sem.at[which],
                recv_sem=recv_sem.at[which],
                device_id={"mem": to},
                device_id_type=MESH,
            ).start()

    def all_of(buffer, which, sem):
        span = buffer.at[which, pl.ds(0, n_mem - 1)]
        pltpu.make_async_copy(span, span, sem.at[which]).wait()

    def plane_copy(which, side):
        return pltpu.make_async_remote_copy(
            src_ref=out_plane.at[which, side],
            dst_ref=in_plane.at[which, side],
            send_sem=send_plane.at[which, side],
            recv_sem=recv_plane.at[which, side],
            device_id={"grp": above if side == 0 else below},
            device_id_type=MESH,
        )

    unpack, request, face_pick, plane_pick, lift_pick, near_hang, plane_hang = tables(
        face_owner[...],
        face_block[...],
        plane_block[...],
        hanging[...],
        n_mem,
        jnp.where(grp > 0, 1, 0),
        jnp.where(grp < n_grp - 1, 1, 0),
    )
    unpack_mat[...] = unpack
    face_mat[...] = face_pick
    plane_mat[...] = plane_pick
    lift_mat[...] = lift_pick
    hang_near[...] = near_hang
    hang_plane[...] = plane_hang
    out_small[REQUEST] = request.reshape(n_mem, 8, LANES)

    block_row = iota((8, LANES), 0)
    level = jnp.sum(
        jnp.where(iota((8, 8), 0) == iota((8, 8), 1), refinement[...], 0), axis=1, keepdims=True
    )
    level = jnp.broadcast_to(level, (8, LANES))
    scale = 1.0 / jnp.left_shift(jnp.ones_like(level), level).astype(F32)
    loads[0].wait()
    for i in range(EDGE):
        for v in range(2):
            effective[:, part(i, v)] = effective[:, part(i, v)] * scale

    def send_planes(which, channels, read):
        for c in range(channels):
            for v in range(2):
                out_plane[which, 0, c, pl.ds(8 * v, 8), :] = read(c, EDGE - 1, v)
                out_plane[which, 1, c, pl.ds(8 * v, 8), :] = read(c, 0, v)
        for side in range(2):
            plane_copy(which, side).start()

    for side in range(2):
        for c in range(1, 3):
            out_plane[SWEEPS, side, c] = jnp.zeros((16, LANES), F32)
    found = extract(lambda i, v: effective[:, part(i, v)])
    for (v, d), register in found.items():
        out_face[pl.ds(v * 32 + d * 8, 8), :] = register

    pl.semaphore_wait(barrier, n_mem - 1 + 2)

    for to in peers:
        pltpu.make_async_remote_copy(
            src_ref=out_face,
            dst_ref=in_face.at[mem],
            send_sem=send_face,
            recv_sem=recv_face,
            device_id={"mem": to},
            device_id_type=MESH,
        ).start()
    send_planes(SWEEPS, 1, lambda c, i, v: effective[:, part(i, v)])
    send(out_small, in_small, REQUEST, send_small, recv_small)
    in_face[mem] = out_face[...]
    in_small[REQUEST, mem] = out_small[REQUEST, mem]

    loads[1].wait()
    loads[2].wait()
    rows, columns = iota((24, 24), 0), iota((24, 24), 1)
    reorder = jnp.where(columns == 3 * (rows % 8) + rows // 8, 1.0, 0.0).astype(BF16)
    solver_rows[:, pl.ds(0, n_coarse)] = pick(thrice(reorder), solver[...])
    if n_coarse % LANES:
        spare = groups_of_lanes * LANES - n_coarse
        solver_rows[:, pl.ds(n_coarse, spare)] = jnp.zeros((24, spare), F32)
    for c in range(3):
        for i in range(EDGE):
            for v in range(2):
                velocity[c, :, part(i, v)] = jnp.zeros((8, LANES), F32)
                step_dir[c, :, part(i, v)] = jnp.zeros((8, LANES), F32)
    for i in range(EDGE):
        own = [effective[:, part(i, v)] for v in range(2)]
        back = [turn(x, EDGE) for x in own]
        ahead = [turn(x, -EDGE) for x in own]
        for v in range(2):
            x = own[v]
            lower_k = jnp.where(first_k, 0.0, 0.5 * (x + turn(x, 1)))
            upper_k = jnp.where(last_k, 0.0, 0.5 * (x + turn(x, -1)))
            if v == 0:
                lower_j = jnp.where(first_row, 0.0, 0.5 * (x + back[0]))
                upper_j = 0.5 * (x + jnp.where(last_row, ahead[1], ahead[0]))
            else:
                lower_j = 0.5 * (x + jnp.where(first_row, back[0], back[1]))
                upper_j = jnp.where(last_row, 0.0, 0.5 * (x + ahead[1]))
            weight_k[0, :, part(i, v)] = lower_k
            weight_k[1, :, part(i, v)] = upper_k
            weight_j[0, :, part(i, v)] = lower_j
            weight_j[1, :, part(i, v)] = upper_j
            if i > 0:
                weight_i[:, part(i, v)] = 0.5 * (x + effective[:, part(i - 1, v)])
            diagonal[:, part(i, v)] = MASS_TERM * x + lower_k + upper_k + lower_j + upper_j

    def settle(values, hang):
        return jnp.where(hang == 1.0, coarsen(values), values)

    def side_by_side(buffer, channels):
        return jnp.concatenate([buffer(c) for c in range(channels)], axis=1)

    def receive_planes(which, channels):
        for side in range(2):
            plane_copy(which, side).wait_recv()
        arrived = side_by_side(
            lambda c: in_plane[which, :, c].reshape(32, LANES), channels
        )
        picked = pick(plane_mat[...], arrived)
        for c in range(channels):
            plane_ghosts[c] = settle(picked[:, c * LANES : (c + 1) * LANES], hang_plane[...])

    def unpack_near(matrix, arrived, channels):
        picked = pick(matrix, arrived)
        for c in range(channels):
            for v in range(2):
                ghosts[c, pl.ds(32 * v, 32), :] = settle(
                    picked[32 * v : 32 * v + 32, c * LANES : (c + 1) * LANES], hang_near[...]
                )

    def ghost(c, d, v):
        return ghosts[c, pl.ds(v * 32 + d * 8, 8), :]

    def plane_ghost(c, side, v):
        return plane_ghosts[c, pl.ds(side * 16 + v * 8, 8), :]

    def near_ghosts(c):
        lower_k = [ghost(c, 0, v) for v in range(2)]
        upper_k = [turn(ghost(c, 1, v), EDGE - 1) for v in range(2)]
        lower_j = [ghost(c, 2, v) for v in range(2)]
        upper_j = [turn(ghost(c, 3, v), LANES - EDGE) for v in range(2)]

        def at_k(i, v):
            return turn(jnp.where(in_row == i, lower_k[v], upper_k[v]), -i)

        def at_j(i):
            both = jnp.where(row == i % 8, lower_j[i // 8], upper_j[i // 8])
            return turn(both, -(i % 8) * EDGE)

        return at_k, at_j

    receive_planes(SWEEPS, 1)
    for v in range(2):
        weight_i[:, part(0, v)] = 0.5 * (effective[:, part(0, v)] + plane_ghost(0, 0, v))
        weight_i[:, part(EDGE, v)] = 0.5 * (effective[:, part(EDGE - 1, v)] + plane_ghost(0, 1, v))
    span = in_face.at[pl.ds(0, n_mem - 1)]
    pltpu.make_async_copy(span, span, recv_face).wait()
    unpack_near(face_mat[...], in_face[...].reshape(n_mem * 64, LANES), 1)
    k_ghost, j_ghost = near_ghosts(0)
    for i in range(EDGE):
        beside_j = j_ghost(i)
        for v in range(2):
            x = effective[:, part(i, v)]
            at_k = jnp.where(first_k | last_k, 0.5 * (x + k_ghost(i, v)), 0.0)
            edge = first_row if v == 0 else last_row
            at_j = jnp.where(edge, 0.5 * (x + beside_j), 0.0)
            ghost_k[:, part(i, v)] = at_k
            ghost_j[:, part(i, v)] = at_j
            whole = (
                diagonal[:, part(i, v)]
                + (weight_i[:, part(i, v)] + weight_i[:, part(i + 1, v)])
                + (at_k + at_j)
            )
            diagonal[:, part(i, v)] = whole
            inverse[:, part(i, v)] = 1.0 / whole

    steps = chebyshev()
    ghosts[...] = jnp.zeros(ghosts.shape, F32)
    plane_ghosts[...] = jnp.zeros(plane_ghosts.shape, F32)
    all_of(in_small, REQUEST, recv_small)
    request = in_small[REQUEST].reshape(wide, LANES)
    pack_mat[...] = jnp.concatenate([request, request[:, :64]], axis=1).astype(BF16)

    def across_faces(c):
        k_ghost, j_ghost = near_ghosts(c)

        def new(i):
            beside_j = j_ghost(i)
            result = []
            for v in range(2):
                change = ghost_k[:, part(i, v)] * k_ghost(i, v)
                change = change + ghost_j[:, part(i, v)] * beside_j
                if i == 0:
                    change = change + weight_i[:, part(0, v)] * plane_ghost(c, 0, v)
                if i == EDGE - 1:
                    change = change + weight_i[:, part(EDGE, v)] * plane_ghost(c, 1, v)
                result.append(residual[c, :, part(i, v)] + change)
            return result

        return new

    def coarse_level():
        totals = []
        for c in range(3):
            total = jnp.zeros((8, LANES), F32)
            new = across_faces(c)
            for i in range(EDGE):
                for v, value in enumerate(new(i)):
                    residual[c, :, part(i, v)] = value
                    total = total + value
            totals.append(jnp.sum(total, axis=1, keepdims=True) / math.sqrt(CELLS))
        for q in range(groups_of_lanes):
            place = lane + q * LANES - 24 * mem - 3 * block_row
            mine = jnp.zeros((8, LANES), F32)
            for c in range(3):
                mine = jnp.where(place == c, totals[c], mine)
            for m in range(n_mem):
                out_big[COARSE, m, q] = mine
        for q in range(groups_of_lanes, 3):
            for m in range(n_mem):
                out_big[COARSE, m, q] = jnp.zeros((8, LANES), F32)
        send(out_big, in_big, COARSE, send_big, recv_big)
        in_big[COARSE, mem] = out_big[COARSE, mem]
        all_of(in_big, COARSE, recv_big)
        products = [jnp.zeros((8, LANES), F32)] * 3
        for q in range(groups_of_lanes):
            vector = in_big[COARSE, 0, q]
            for m in range(1, n_mem):
                vector = vector + in_big[COARSE, m, q]
            vector = jnp.sum(vector, axis=0, keepdims=True)
            for c in range(3):
                products[c] = products[c] + solver_rows[
                    pl.ds(8 * c, 8), pl.ds(q * LANES, LANES)
                ] * vector
        own = [jnp.sum(products[c], axis=1, keepdims=True) for c in range(3)]
        tile = jnp.zeros((8, LANES), F32)
        for c in range(3):
            tile = jnp.where(lane == c, own[c], tile)
        for m in range(n_mem):
            out_small[CORRECTION, m] = tile
        send(out_small, in_small, CORRECTION, send_small, recv_small)
        in_small[CORRECTION, mem] = tile
        for side in range(2):
            for c in range(3):
                out_plane[SWEEPS + 1, side, c] = jnp.concatenate([tile, tile], axis=0)
            plane_copy(SWEEPS + 1, side).start()
        for side in range(2):
            plane_copy(SWEEPS + 1, side).wait_recv()
        far = pick(plane_mat[...], in_plane[SWEEPS + 1, :, 0].reshape(32, LANES))
        all_of(in_small, CORRECTION, recv_small)
        near = pick(lift_mat[...], in_small[CORRECTION].reshape(wide, LANES))
        for c in range(3):
            mine = jnp.broadcast_to(own[c], (8, LANES))

            def difference(values, start):
                return mine - jnp.broadcast_to(values[start : start + 8, c : c + 1], (8, LANES))

            gap = [difference(near, 8 * d) for d in range(4)]
            gap_lower, gap_upper = difference(far, 0), difference(far, 16)
            gap_k = jnp.where(first_k, gap[0], gap[1])
            for i in range(EDGE):
                for v in range(2):
                    change = MASS_TERM * effective[:, part(i, v)] * mine
                    change = change + ghost_k[:, part(i, v)] * gap_k
                    change = change + ghost_j[:, part(i, v)] * gap[2 + v]
                    if i == 0:
                        change = change + weight_i[:, part(0, v)] * gap_lower
                    if i == EDGE - 1:
                        change = change + weight_i[:, part(EDGE, v)] * gap_upper
                    residual[c, :, part(i, v)] = residual[c, :, part(i, v)] - change
                    velocity[c, :, part(i, v)] = velocity[c, :, part(i, v)] + mine
        ghosts[...] = jnp.zeros(ghosts.shape, F32)
        plane_ghosts[...] = jnp.zeros(plane_ghosts.shape, F32)

    def sweep(t, carry):
        @pl.when(t == DEG)
        def _():
            coarse_level()

        step = lax.rem(t, DEG)
        keep = by_step(step, [first for first, _ in steps])
        gain = by_step(step, [second for _, second in steps])

        for c in range(3):
            new = across_faces(c)
            moved = {}

            def step_of(i, v):
                if v == 0:
                    for half, value in enumerate(new(i)):
                        residual[c, :, part(i, half)] = value
                        ahead = keep * step_dir[c, :, part(i, half)] + gain * (
                            value * inverse[:, part(i, half)]
                        )
                        step_dir[c, :, part(i, half)] = ahead
                        moved[i, half] = ahead
                return moved[i, v]

            for (v, d), register in extract(step_of).items():
                faces[c, pl.ds(v * 32 + d * 8, 8), :] = register

        packed = pick(pack_mat[...], side_by_side(lambda c: faces[c], 3))
        for c in range(3):
            out_big[t, :, c] = packed[:, c * LANES : (c + 1) * LANES].reshape(n_mem, 8, LANES)
        send(out_big, in_big, t, send_big, recv_big)
        send_planes(t, 3, lambda c, i, v: step_dir[c, :, part(i, v)])
        in_big[t, mem] = out_big[t, mem]

        @pl.loop(0, 3)
        def _(c):
            for i in range(EDGE):
                own = [step_dir[c, :, part(i, v)] for v in range(2)]
                back = [turn(x, EDGE) for x in own]
                ahead = [turn(x, -EDGE) for x in own]
                for v in range(2):
                    x = own[v]
                    if v == 0:
                        lower_j, upper_j = back[0], jnp.where(last_row, ahead[1], ahead[0])
                    else:
                        lower_j, upper_j = jnp.where(first_row, back[0], back[1]), ahead[1]
                    change = weight_k[0, :, part(i, v)] * turn(x, 1)
                    change = change + weight_k[1, :, part(i, v)] * turn(x, -1)
                    change = change + weight_j[0, :, part(i, v)] * lower_j
                    change = change + weight_j[1, :, part(i, v)] * upper_j
                    if i > 0:
                        change = change + weight_i[:, part(i, v)] * step_dir[c, :, part(i - 1, v)]
                    if i < EDGE - 1:
                        change = change + weight_i[:, part(i + 1, v)] * step_dir[
                            c, :, part(i + 1, v)
                        ]
                    residual[c, :, part(i, v)] = residual[c, :, part(i, v)] - (
                        diagonal[:, part(i, v)] * x - change
                    )
                    velocity[c, :, part(i, v)] = velocity[c, :, part(i, v)] + x

        receive_planes(t, 3)
        all_of(in_big, t, recv_big)
        unpack_near(
            unpack_mat[...],
            side_by_side(lambda c: in_big[t, :, c].reshape(wide, LANES), 3),
            3,
        )
        return carry

    lax.fori_loop(0, SWEEPS, sweep, 0)
    for c in range(3):
        new = across_faces(c)
        for i in range(EDGE):
            for v, value in enumerate(new(i)):
                residual[c, :, part(i, v)] = value

    span = in_face.at[pl.ds(0, n_mem - 1)]
    pltpu.make_async_copy(span, span, send_face).wait()
    for t in range(SWEEPS + 1):
        all_of(out_big, t, send_big)
    for t in (REQUEST, CORRECTION):
        all_of(out_small, t, send_small)
    for t in range(SWEEPS + 2):
        for side in range(2):
            plane_copy(t, side).wait_send()


def solution(mesh):
    n_grp, n_mem = mesh.shape["grp"], mesh.shape["mem"]
    wide = n_mem * 8

    def local(
        forcing,
        viscosity,
        refinement,
        face_owner,
        face_block,
        plane_block,
        hanging,
        coarse_solver,
    ):
        field = pltpu.VMEM((8, CELLS), F32)
        vmem = pl.BlockSpec(memory_space=pltpu.VMEM)
        hbm = pl.BlockSpec(memory_space=pltpu.HBM)
        dma = pltpu.SemaphoreType.DMA
        both = pl.pallas_call(
            functools.partial(kernel, n_grp, n_mem),
            out_shape=jax.ShapeDtypeStruct((2, *forcing.shape), F32),
            in_specs=[hbm] * 3 + [vmem] * 5,
            out_specs=vmem,
            scratch_shapes=[
                field,
                pltpu.VMEM((24, n_mem * 24), F32),
                pltpu.VMEM((2, 8, CELLS), F32),
                pltpu.VMEM((2, 8, CELLS), F32),
                pltpu.VMEM((8, CELLS + FACE), F32),
                field,
                field,
                field,
                field,
                pltpu.VMEM((3, 8, CELLS), F32),
                pltpu.VMEM((3, 64, LANES), F32),
                pltpu.VMEM((3, 64, LANES), F32),
                pltpu.VMEM((3, 32, LANES), F32),
                pltpu.VMEM((32, LANES), F32),
                pltpu.VMEM((32, LANES), F32),
                pltpu.VMEM((64, 3 * wide), BF16),
                pltpu.VMEM((wide, 192), BF16),
                pltpu.VMEM((32, 96), BF16),
                pltpu.VMEM((32, 3 * wide), BF16),
                pltpu.VMEM((64, 3 * n_mem * 64), BF16),
                pltpu.VMEM((24, -(-n_mem * 24 // LANES) * LANES), F32),
                pltpu.VMEM((64, LANES), F32),
                pltpu.VMEM((n_mem, 64, LANES), F32),
                pltpu.VMEM((SWEEPS + 1, n_mem, 3, 8, LANES), F32),
                pltpu.VMEM((SWEEPS + 1, n_mem, 3, 8, LANES), F32),
                pltpu.VMEM((2, n_mem, 8, LANES), F32),
                pltpu.VMEM((2, n_mem, 8, LANES), F32),
                pltpu.VMEM((SWEEPS + 2, 2, 3, 16, LANES), F32),
                pltpu.VMEM((SWEEPS + 2, 2, 3, 16, LANES), F32),
                dma((SWEEPS + 1,)),
                dma((SWEEPS + 1,)),
                dma((2,)),
                dma((2,)),
                dma((SWEEPS + 2, 2)),
                dma((SWEEPS + 2, 2)),
                dma,
                dma,
                dma((3,)),
            ],
            compiler_params=pltpu.CompilerParams(
                collective_id=0, has_side_effects=True, vmem_limit_bytes=56 * 1024 * 1024
            ),
            name="vcycle",
        )(
            forcing,
            viscosity,
            coarse_solver,
            refinement.reshape(1, 8),
            face_owner.reshape(1, 32),
            face_block.T,
            plane_block.T,
            hanging,
        )
        return both[0], both[1]

    in_specs = (
        P(None, ("grp", "mem"), None),
        P(("grp", "mem"), None),
        P(("grp", "mem")),
        P(("grp", "mem"), None),
        P(("grp", "mem"), None),
        P(("grp", "mem"), None),
        P(("grp", "mem"), None),
        P("grp", "mem", None),
    )
    out_specs = (P(None, ("grp", "mem"), None), P(None, ("grp", "mem"), None))
    return jax.shard_map(local, mesh=mesh, in_specs=in_specs, out_specs=out_specs, check_vma=False)
```

```python
import functools
import math

import jax
import jax.numpy as jnp
from jax import lax
from jax.experimental import pallas as pl
from jax.experimental.pallas import tpu as pltpu
from jax.sharding import PartitionSpec as P

MESH = pl.DeviceIdType.MESH
EDGE = 16
DEG = 3
CELLS = 4096
FACE = 256
LANES = 128
CAP = 4
MASS_TERM = 1.0
LOWER_BOUND = 0.25
UPPER_BOUND = 2.0
SWEEPS = 2 * DEG
F32 = jnp.float32
BF16 = jnp.bfloat16


def chebyshev():
    theta = 0.5 * (UPPER_BOUND + LOWER_BOUND)
    delta = 0.5 * (UPPER_BOUND - LOWER_BOUND)
    sigma = theta / delta
    rho = 1.0 / sigma
    steps = [(0.0, 1.0 / theta)]
    for _ in range(DEG - 1):
        rho_next = 1.0 / (2.0 * sigma - rho)
        steps.append((rho_next * rho, 2.0 * rho_next / delta))
        rho = rho_next
    return steps


def far_first(members):
    tall = members // 4

    def hops(offset):
        dy, dx = offset
        return min(dy, tall - dy) + min(dx, 4 - dx)

    others = [(dy, dx) for dy in range(tall) for dx in range(4) if (dy, dx) != (0, 0)]
    return sorted(others, key=hops, reverse=True)


def by_step(step, values):
    result = jnp.float32(values[-1])
    for place in range(len(values) - 2, -1, -1):
        result = jnp.where(step == place, jnp.float32(values[place]), result)
    return result


def iota(shape, dim):
    return lax.broadcasted_iota(jnp.int32, shape, dim)


def turn(x, shift):
    shift = shift % LANES
    return x if shift == 0 else pltpu.roll(x, shift, 1)


def part(i, v):
    return pl.ds(i * FACE + v * LANES, LANES)


def parts(values):
    high = values.astype(BF16)
    rest = values - high.astype(F32)
    middle = rest.astype(BF16)
    low = (rest - middle.astype(F32)).astype(BF16)
    return jnp.concatenate([high, middle, low], axis=0)


def thrice(one_hot):
    return jnp.concatenate([one_hot] * 3, axis=1)


def pick(one_hot_thrice, values):
    return jnp.dot(one_hot_thrice, parts(values), preferred_element_type=F32)


def coarsen(x):
    lane = iota(x.shape, 1)
    x = x + jnp.where(lane % 2 == 0, turn(x, -1), turn(x, 1))
    x = x + jnp.where(lane // EDGE % 2 == 0, turn(x, -EDGE), turn(x, EDGE))
    return 0.25 * x


def extract(read):
    lane = iota((8, LANES), 1)
    in_row, row = lane % EDGE, lane // EDGE
    zero = jnp.zeros((8, LANES), F32)
    faces = {(v, d): zero for v in range(2) for d in range(4)}
    for i in range(EDGE):
        halves = (read(i, 0), read(i, 1))
        for v in range(2):
            moved = turn(halves[v], i)
            faces[v, 0] = jnp.where(in_row == i, moved, faces[v, 0])
            faces[v, 1] = jnp.where(in_row == (i - 1) % EDGE, moved, faces[v, 1])
        v = i // 8
        moved = turn(jnp.where(lane < EDGE, halves[0], halves[1]), i % 8 * EDGE)
        faces[v, 2] = jnp.where(row == i % 8, moved, faces[v, 2])
        faces[v, 3] = jnp.where(row == (i - 1) % 8, moved, faces[v, 3])
    for v in range(2):
        faces[v, 1] = turn(faces[v, 1], -(EDGE - 1))
        faces[v, 3] = turn(faces[v, 3], EDGE)
    return faces


def tables(owner, face_block, plane_block, hanging, members, has_lower, has_upper):
    wide = members * 8
    rows, columns = iota((32, 32), 0), iota((32, 32), 1)
    given = 4 * (rows % 8) + rows // 8
    given_t = 4 * (columns % 8) + columns // 8
    owner_col = jnp.sum(jnp.where(columns == given, owner, 0), axis=1, keepdims=True)
    own_col = jnp.sum(jnp.where(rows == columns, owner, 0), axis=1, keepdims=True)
    owner_row = jnp.sum(jnp.where(rows == given_t, own_col, 0), axis=0, keepdims=True)
    same = owner_col == owner_row
    rank_col = jnp.sum(jnp.where(same & (columns < rows), 1, 0), axis=1, keepdims=True)
    rank_row = jnp.sum(jnp.where(same & (rows < columns), 1, 0), axis=0, keepdims=True)

    def spread(table, first, of_row):
        tall = jnp.concatenate([table] * 4, axis=0)
        mask = iota(tall.shape, 1) == first + of_row(iota(tall.shape, 0))
        return jnp.sum(jnp.where(mask, tall, 0), axis=1, keepdims=True)

    def spread_t(table, per):
        lanes, which = iota((32, 8), 1), iota((32, 8), 0)
        tall = jnp.zeros((32, 8), jnp.int32)
        for d in range(table.shape[0]):
            tall = jnp.where(which // per == d, table[d : d + 1], tall)
        return jnp.sum(jnp.where(lanes == which % 8, tall, 0), axis=1, keepdims=True)

    block_col = spread_t(face_block, 8)
    side = iota((32, 1), 0) // 8
    wanted = (side + 1 - 2 * (side % 2)) * 8 + block_col
    slot_col = owner_col * 8 + rank_col
    slot_row = owner_row * 8 + rank_row

    def ones(mask):
        return jnp.where(mask, 1.0, 0.0).astype(BF16)

    lanes = iota((32, wide), 1)
    unpack = jnp.concatenate([ones(lanes == slot_col + CAP * v) for v in range(2)], axis=0)
    slots = iota((wide, 32), 0)
    unpack_t = jnp.concatenate([ones(slots == slot_row + CAP * v) for v in range(2)], axis=1)
    lanes = iota((32, LANES), 1)
    source = jnp.concatenate([ones(lanes % 64 == wanted + 32 * v) for v in range(2)], axis=0)
    request = jnp.dot(unpack_t, source, preferred_element_type=F32)
    plane_col = spread_t(plane_block, 16)
    which = iota((32, 32), 0) // 16
    inside = jnp.where(which == 0, has_lower, has_upper) == 1
    plane_pick = ones((columns == rows // 8 * 8 + plane_col) & inside)
    lanes, which = iota((8, 8), 1), iota((8, 8), 0)
    far_pick = []
    for d, exists in enumerate((has_lower, has_upper)):
        chosen = plane_block[d : d + 1]
        chosen = jnp.sum(jnp.where(lanes == which, chosen, 0), axis=1, keepdims=True)
        far_pick.append(jnp.where((lanes == chosen) & (exists == 1), 1.0, 0.0))
    lift_pick = ones(iota((32, wide), 1) == owner_col * 8 + block_col)
    near_hang = spread(hanging, 0, lambda r: r // 8)
    plane_hang = spread(hanging, 4, lambda r: r // 16)
    near_hang = jnp.broadcast_to(near_hang.astype(F32), (32, LANES))
    plane_hang = jnp.broadcast_to(plane_hang.astype(F32), (32, LANES))
    return (
        thrice(unpack),
        request,
        thrice(plane_pick),
        thrice(lift_pick),
        far_pick,
        near_hang,
        plane_hang,
    )


def kernel(
    n_grp,
    n_mem,
    forcing_hbm,
    viscosity_hbm,
    solver_hbm,
    refinement,
    face_owner,
    face_block,
    plane_block,
    hanging,
    owner_scalar,
    block_scalar,
    result,
    velocity,
    residual,
    effective,
    solver,
    weight_k,
    weight_j,
    weight_i,
    ghost_k,
    ghost_j,
    diagonal,
    inverse,
    step_dir,
    faces,
    ghosts,
    plane_ghosts,
    hang_near,
    hang_plane,
    unpack_mat,
    pack_mat,
    plane_mat,
    lift_mat,
    far_mat,
    solver_rows,
    in_solver,
    in_far_solver,
    near_rows,
    far_rows,
    out_vector,
    in_vector,
    out_face,
    in_face,
    out_big,
    in_big,
    out_request,
    in_request,
    out_plane,
    in_plane,
    send_big,
    recv_big,
    send_request,
    recv_request,
    send_plane,
    recv_plane,
    send_face,
    recv_face,
    send_solver,
    recv_solver,
    send_far,
    recv_far,
    send_vector,
    recv_vector,
    load_sem,
    store_sem,
):
    grp, mem = lax.axis_index("grp"), lax.axis_index("mem")
    above = lax.rem(grp + 1, n_grp)
    below = lax.rem(grp + n_grp - 1, n_grp)
    n_coarse = n_mem * 24
    groups_of_lanes = n_coarse // LANES
    wide = n_mem * 8

    mem_y, mem_x = lax.div(mem, 4), lax.rem(mem, 4)
    peers = [
        lax.rem(mem_y + dy, n_mem // 4) * 4 + lax.rem(mem_x + dx, 4) for dy, dx in far_first(n_mem)
    ]
    barrier = pltpu.get_barrier_semaphore()
    for to in peers:
        pl.semaphore_signal(barrier, inc=1, device_id={"mem": to}, device_id_type=MESH)
    for other in (above, below):
        for to in [*peers, mem]:
            pl.semaphore_signal(
                barrier, inc=1, device_id={"grp": other, "mem": to}, device_id_type=MESH
            )

    loads = [
        pltpu.make_async_copy(viscosity_hbm, effective, load_sem.at[0]),
        pltpu.make_async_copy(forcing_hbm, residual, load_sem.at[1]),
        pltpu.make_async_copy(solver_hbm.at[0], solver, load_sem.at[2]),
    ]
    for load in loads:
        load.start()

    def store(place):
        source = (velocity, residual)[place]
        return pltpu.make_async_copy(source, result.at[place], store_sem.at[place])

    lane = iota((8, LANES), 1)
    in_row = lane % EDGE
    row = lane // EDGE
    first_k, last_k = in_row == 0, in_row == EDGE - 1
    first_row, last_row = lane < EDGE, lane >= LANES - EDGE

    def send(outgoing, incoming, send_sem, recv_sem):
        for to in peers:
            pltpu.make_async_remote_copy(
                src_ref=outgoing.at[to],
                dst_ref=incoming.at[mem],
                send_sem=send_sem,
                recv_sem=recv_sem,
                device_id={"mem": to},
                device_id_type=MESH,
            ).start()

    def wait_for(buffer, sem, count=n_mem - 1):
        span = buffer.at[pl.ds(0, count)]
        pltpu.make_async_copy(span, span, sem).wait()

    def plane_copy(which, side):
        return pltpu.make_async_remote_copy(
            src_ref=out_plane.at[which, side],
            dst_ref=in_plane.at[which, side],
            send_sem=send_plane.at[which, side],
            recv_sem=recv_plane.at[which, side],
            device_id={"grp": above if side == 0 else below},
            device_id_type=MESH,
        )

    def far_solver(c, side):
        return pltpu.make_async_remote_copy(
            src_ref=solver_rows.at[c],
            dst_ref=in_far_solver.at[c, side],
            send_sem=send_far.at[c, side],
            recv_sem=recv_far.at[c, side],
            device_id={"grp": above if side == 0 else below},
            device_id_type=MESH,
        )

    block_row = iota((8, LANES), 0)
    level = jnp.sum(
        jnp.where(iota((8, 8), 0) == iota((8, 8), 1), refinement[...], 0), axis=1, keepdims=True
    )
    level = jnp.broadcast_to(level, (8, LANES))
    scale = 1.0 / jnp.left_shift(jnp.ones_like(level), level).astype(F32)
    loads[0].wait()
    for i in range(EDGE):
        for v in range(2):
            effective[:, part(i, v)] = effective[:, part(i, v)] * scale

    def send_planes(which, channels, read):
        for c in range(channels):
            for v in range(2):
                out_plane[which, 0, c, pl.ds(8 * v, 8), :] = read(c, EDGE - 1, v)
                out_plane[which, 1, c, pl.ds(8 * v, 8), :] = read(c, 0, v)
        for side in range(2):
            plane_copy(which, side).start()

    for side in range(2):
        for c in range(1, 3):
            out_plane[SWEEPS, side, c] = jnp.zeros((16, LANES), F32)
    found = extract(lambda i, v: effective[:, part(i, v)])
    for (v, d), register in found.items():
        out_face[pl.ds(v * 32 + d * 8, 8), :] = register

    pl.semaphore_wait(barrier, n_mem - 1 + 2 * n_mem)

    for to in peers:
        pltpu.make_async_remote_copy(
            src_ref=out_face,
            dst_ref=in_face.at[mem],
            send_sem=send_face,
            recv_sem=recv_face,
            device_id={"mem": to},
            device_id_type=MESH,
        ).start()
    send_planes(SWEEPS, 1, lambda c, i, v: effective[:, part(i, v)])
    in_face[mem] = out_face[...]
    unpack, request, plane_pick, lift_pick, far_pick, near_hang, plane_hang = tables(
        face_owner[...],
        face_block[...],
        plane_block[...],
        hanging[...],
        n_mem,
        jnp.where(grp > 0, 1, 0),
        jnp.where(grp < n_grp - 1, 1, 0),
    )
    unpack_mat[...] = unpack
    plane_mat[...] = plane_pick
    lift_mat[...] = lift_pick
    for side in range(2):
        far_mat[side] = far_pick[side]
    hang_near[...] = near_hang
    hang_plane[...] = plane_hang
    out_request[...] = request.reshape(n_mem, 8, LANES)
    send(out_request, in_request, send_request, recv_request)
    in_request[mem] = out_request[mem]

    loads[1].wait()
    loads[2].wait()
    rows, columns = iota((24, 24), 0), iota((24, 24), 1)
    reorder = jnp.where(columns == 3 * (rows % 8) + rows // 8, 1.0, 0.0).astype(BF16)
    ordered = pick(thrice(reorder), solver[...])
    for c in range(3):
        solver_rows[c] = ordered[8 * c : 8 * c + 8]
    for c in range(3):
        for i in range(EDGE):
            for v in range(2):
                velocity[c, :, part(i, v)] = jnp.zeros((8, LANES), F32)
                step_dir[c, :, part(i, v)] = jnp.zeros((8, LANES), F32)
    for i in range(EDGE):
        own = [effective[:, part(i, v)] for v in range(2)]
        back = [turn(x, EDGE) for x in own]
        ahead = [turn(x, -EDGE) for x in own]
        for v in range(2):
            x = own[v]
            lower_k = jnp.where(first_k, 0.0, 0.5 * (x + turn(x, 1)))
            upper_k = jnp.where(last_k, 0.0, 0.5 * (x + turn(x, -1)))
            if v == 0:
                lower_j = jnp.where(first_row, 0.0, 0.5 * (x + back[0]))
                upper_j = 0.5 * (x + jnp.where(last_row, ahead[1], ahead[0]))
            else:
                lower_j = 0.5 * (x + jnp.where(first_row, back[0], back[1]))
                upper_j = jnp.where(last_row, 0.0, 0.5 * (x + ahead[1]))
            weight_k[0, :, part(i, v)] = lower_k
            weight_k[1, :, part(i, v)] = upper_k
            weight_j[0, :, part(i, v)] = lower_j
            weight_j[1, :, part(i, v)] = upper_j
            if i > 0:
                weight_i[:, part(i, v)] = 0.5 * (x + effective[:, part(i - 1, v)])
            diagonal[:, part(i, v)] = MASS_TERM * x + lower_k + upper_k + lower_j + upper_j

    def settle(values, hang):
        return jnp.where(hang == 1.0, coarsen(values), values)

    def side_by_side(buffer, channels):
        return jnp.concatenate([buffer(c) for c in range(channels)], axis=1)

    def receive_planes(which, channels):
        for side in range(2):
            plane_copy(which, side).wait_recv()
        arrived = side_by_side(
            lambda c: in_plane[which, :, c].reshape(32, LANES), channels
        )
        picked = pick(plane_mat[...], arrived)
        for c in range(channels):
            plane_ghosts[c] = settle(picked[:, c * LANES : (c + 1) * LANES], hang_plane[...])

    def unpack_near(matrix, arrived, channels):
        picked = pick(matrix, arrived)
        for c in range(channels):
            for v in range(2):
                ghosts[c, pl.ds(32 * v, 32), :] = settle(
                    picked[32 * v : 32 * v + 32, c * LANES : (c + 1) * LANES], hang_near[...]
                )

    def ghost(c, d, v):
        return ghosts[c, pl.ds(v * 32 + d * 8, 8), :]

    def plane_ghost(c, side, v):
        return plane_ghosts[c, pl.ds(side * 16 + v * 8, 8), :]

    def near_ghosts(c):
        lower_k = [ghost(c, 0, v) for v in range(2)]
        upper_k = [turn(ghost(c, 1, v), EDGE - 1) for v in range(2)]
        lower_j = [ghost(c, 2, v) for v in range(2)]
        upper_j = [turn(ghost(c, 3, v), LANES - EDGE) for v in range(2)]

        def at_k(i, v):
            return turn(jnp.where(in_row == i, lower_k[v], upper_k[v]), -i)

        def at_j(i):
            both = jnp.where(row == i % 8, lower_j[i // 8], upper_j[i // 8])
            return turn(both, -(i % 8) * EDGE)

        return at_k, at_j

    receive_planes(SWEEPS, 1)
    for v in range(2):
        weight_i[:, part(0, v)] = 0.5 * (effective[:, part(0, v)] + plane_ghost(0, 0, v))
        weight_i[:, part(EDGE, v)] = 0.5 * (effective[:, part(EDGE - 1, v)] + plane_ghost(0, 1, v))
    wait_for(in_face, recv_face)
    for d in range(4):
        for b in range(8):
            owner = owner_scalar[0, 4 * b + d]
            wanted = (d + 1 - 2 * (d % 2)) * 8 + block_scalar[d, b]
            for v in range(2):
                ghosts[0, pl.ds(v * 32 + d * 8 + b, 1), :] = in_face[
                    owner, pl.ds(v * 32 + wanted, 1), :
                ]
    for v in range(2):
        ghosts[0, pl.ds(32 * v, 32), :] = settle(ghosts[0, pl.ds(32 * v, 32), :], hang_near[...])
    k_ghost, j_ghost = near_ghosts(0)
    for i in range(EDGE):
        beside_j = j_ghost(i)
        for v in range(2):
            x = effective[:, part(i, v)]
            at_k = jnp.where(first_k | last_k, 0.5 * (x + k_ghost(i, v)), 0.0)
            edge = first_row if v == 0 else last_row
            at_j = jnp.where(edge, 0.5 * (x + beside_j), 0.0)
            ghost_k[:, part(i, v)] = at_k
            ghost_j[:, part(i, v)] = at_j
            whole = (
                diagonal[:, part(i, v)]
                + (weight_i[:, part(i, v)] + weight_i[:, part(i + 1, v)])
                + (at_k + at_j)
            )
            diagonal[:, part(i, v)] = whole
            inverse[:, part(i, v)] = 1.0 / whole

    steps = chebyshev()
    ghosts[...] = jnp.zeros(ghosts.shape, F32)
    plane_ghosts[...] = jnp.zeros(plane_ghosts.shape, F32)
    wait_for(in_request, recv_request)
    request = in_request[...].reshape(wide, LANES)
    pack_mat[...] = jnp.concatenate([request, request[:, :64]], axis=1).astype(BF16)

    def across_faces(c):
        k_ghost, j_ghost = near_ghosts(c)

        def new(i):
            beside_j = j_ghost(i)
            result = []
            for v in range(2):
                change = ghost_k[:, part(i, v)] * k_ghost(i, v)
                change = change + ghost_j[:, part(i, v)] * beside_j
                if i == 0:
                    change = change + weight_i[:, part(0, v)] * plane_ghost(c, 0, v)
                if i == EDGE - 1:
                    change = change + weight_i[:, part(EDGE, v)] * plane_ghost(c, 1, v)
                result.append(residual[c, :, part(i, v)] + change)
            return result

        return new

    def coarse_level():
        totals = []
        for c in range(3):
            total = jnp.zeros((8, LANES), F32)
            new = across_faces(c)
            for i in range(EDGE):
                for v, value in enumerate(new(i)):
                    residual[c, :, part(i, v)] = value
                    total = total + value
            totals.append(jnp.sum(total, axis=1, keepdims=True) / math.sqrt(CELLS))
        chunks = []
        for q in range(groups_of_lanes):
            place = lane + q * LANES - 24 * mem - 3 * block_row
            mine = jnp.zeros((8, LANES), F32)
            for c in range(3):
                mine = jnp.where(place == c, totals[c], mine)
            chunks.append(jnp.sum(mine, axis=0, keepdims=True))
        tile = jnp.zeros((8, LANES), F32)
        for q in range(groups_of_lanes):
            tile = jnp.where(block_row == q, chunks[q], tile)
        out_vector[...] = tile

        def send_vector_to(other, to, slot):
            pltpu.make_async_remote_copy(
                src_ref=out_vector,
                dst_ref=in_vector.at[slot, mem],
                send_sem=send_vector.at[slot],
                recv_sem=recv_vector.at[slot],
                device_id={"grp": other, "mem": to},
                device_id_type=MESH,
            ).start()

        for to in peers:
            send_vector_to(above, to, 1)
            send_vector_to(below, to, 2)
            send_vector_to(grp, to, 0)
        send_vector_to(above, mem, 1)
        send_vector_to(below, mem, 2)
        in_vector[0, mem] = tile

        for c in range(3):
            wait_for(in_solver.at[c], recv_solver.at[c])
            in_solver[c, mem] = solver_rows[c]
            near_rows[c] = pick(lift_mat[...], in_solver[c].reshape(wide, n_coarse))
            for side in range(2):
                far_solver(c, side).wait_recv()
                source = in_far_solver[c, side]
                chosen = jnp.zeros((8, n_coarse), F32)
                for b in range(8):
                    wants = far_mat[side][:, b : b + 1]
                    chosen = jnp.where(wants == 1.0, source[b : b + 1], chosen)
                far_rows[c, side] = chosen

        def vector_of(slot):
            whole = in_vector[slot, 0]
            for m in range(1, n_mem):
                whole = whole + in_vector[slot, m]
            return [jnp.broadcast_to(whole[q : q + 1], (8, LANES)) for q in range(groups_of_lanes)]

        def correction(rows, vector):
            product = rows[:, :LANES] * vector[0]
            for q in range(1, groups_of_lanes):
                product = product + rows[:, q * LANES : (q + 1) * LANES] * vector[q]
            return jnp.broadcast_to(jnp.sum(product, axis=1, keepdims=True), (8, LANES))

        for side in range(2):
            wait_for(in_vector.at[1 + side], recv_vector.at[1 + side], n_mem)
        far_vectors = [vector_of(1), vector_of(2)]
        wait_for(in_vector.at[0], recv_vector.at[0])
        vector = vector_of(0)
        for c in range(3):
            mine = correction(solver_rows[c], vector)
            gap = [
                mine - correction(near_rows[c, pl.ds(8 * d, 8), :], vector) for d in range(4)
            ]
            gap_lower, gap_upper = [
                mine - correction(far_rows[c, side], far_vectors[side]) for side in range(2)
            ]
            gap_k = jnp.where(first_k, gap[0], gap[1])
            for i in range(EDGE):
                for v in range(2):
                    change = MASS_TERM * effective[:, part(i, v)] * mine
                    change = change + ghost_k[:, part(i, v)] * gap_k
                    change = change + ghost_j[:, part(i, v)] * gap[2 + v]
                    if i == 0:
                        change = change + weight_i[:, part(0, v)] * gap_lower
                    if i == EDGE - 1:
                        change = change + weight_i[:, part(EDGE, v)] * gap_upper
                    residual[c, :, part(i, v)] = residual[c, :, part(i, v)] - change
                    velocity[c, :, part(i, v)] = velocity[c, :, part(i, v)] + mine
        ghosts[...] = jnp.zeros(ghosts.shape, F32)
        plane_ghosts[...] = jnp.zeros(plane_ghosts.shape, F32)

    def sweep(t, carry):
        @pl.when(t == DEG)
        def _():
            coarse_level()

        step = lax.rem(t, DEG)
        keep = by_step(step, [first for first, _ in steps])
        gain = by_step(step, [second for _, second in steps])

        for c in range(3):
            new = across_faces(c)
            moved = {}

            def step_of(i, v):
                if v == 0:
                    for half, value in enumerate(new(i)):
                        residual[c, :, part(i, half)] = value
                        ahead = keep * step_dir[c, :, part(i, half)] + gain * (
                            value * inverse[:, part(i, half)]
                        )
                        step_dir[c, :, part(i, half)] = ahead
                        moved[i, half] = ahead
                return moved[i, v]

            for (v, d), register in extract(step_of).items():
                faces[c, pl.ds(v * 32 + d * 8, 8), :] = register

        packed = pick(pack_mat[...], side_by_side(lambda c: faces[c], 3))
        for c in range(3):
            out_big[t, :, c] = packed[:, c * LANES : (c + 1) * LANES].reshape(n_mem, 8, LANES)
        send(out_big.at[t], in_big.at[t], send_big.at[t], recv_big.at[t])
        send_planes(t, 3, lambda c, i, v: step_dir[c, :, part(i, v)])

        @pl.when(t < DEG)
        def _():
            for to in peers:
                pltpu.make_async_remote_copy(
                    src_ref=solver_rows.at[t],
                    dst_ref=in_solver.at[t, mem],
                    send_sem=send_solver.at[t],
                    recv_sem=recv_solver.at[t],
                    device_id={"mem": to},
                    device_id_type=MESH,
                ).start()
            for side in range(2):
                far_solver(t, side).start()

        in_big[t, mem] = out_big[t, mem]

        @pl.loop(0, 3)
        def _(c):
            for i in range(EDGE):
                own = [step_dir[c, :, part(i, v)] for v in range(2)]
                back = [turn(x, EDGE) for x in own]
                ahead = [turn(x, -EDGE) for x in own]
                for v in range(2):
                    x = own[v]
                    if v == 0:
                        lower_j, upper_j = back[0], jnp.where(last_row, ahead[1], ahead[0])
                    else:
                        lower_j, upper_j = jnp.where(first_row, back[0], back[1]), ahead[1]
                    change = weight_k[0, :, part(i, v)] * turn(x, 1)
                    change = change + weight_k[1, :, part(i, v)] * turn(x, -1)
                    change = change + weight_j[0, :, part(i, v)] * lower_j
                    change = change + weight_j[1, :, part(i, v)] * upper_j
                    if i > 0:
                        change = change + weight_i[:, part(i, v)] * step_dir[c, :, part(i - 1, v)]
                    if i < EDGE - 1:
                        change = change + weight_i[:, part(i + 1, v)] * step_dir[
                            c, :, part(i + 1, v)
                        ]
                    residual[c, :, part(i, v)] = residual[c, :, part(i, v)] - (
                        diagonal[:, part(i, v)] * x - change
                    )
                    velocity[c, :, part(i, v)] = velocity[c, :, part(i, v)] + x

        @pl.when(t == SWEEPS - 1)
        def _():
            store(0).start()

        receive_planes(t, 3)
        wait_for(in_big.at[t], recv_big.at[t])
        unpack_near(
            unpack_mat[...],
            side_by_side(lambda c: in_big[t, :, c].reshape(wide, LANES), 3),
            3,
        )
        return carry

    lax.fori_loop(0, SWEEPS, sweep, 0)
    for c in range(3):
        new = across_faces(c)
        for i in range(EDGE):
            for v, value in enumerate(new(i)):
                residual[c, :, part(i, v)] = value

    store(1).start()
    wait_for(in_face, send_face)
    for t in range(SWEEPS):
        wait_for(out_big.at[t], send_big.at[t])
    for t in range(DEG):
        wait_for(in_solver.at[t], send_solver.at[t])
        for side in range(2):
            far_solver(t, side).wait_send()
    wait_for(in_vector.at[0], send_vector.at[0])
    for side in range(2):
        wait_for(in_vector.at[1 + side], send_vector.at[1 + side], n_mem)
    wait_for(out_request, send_request)
    for t in range(SWEEPS + 1):
        for side in range(2):
            plane_copy(t, side).wait_send()
    for place in range(2):
        store(place).wait()


def solution(mesh):
    n_grp, n_mem = mesh.shape["grp"], mesh.shape["mem"]
    wide = n_mem * 8

    def local(
        forcing,
        viscosity,
        refinement,
        face_owner,
        face_block,
        plane_block,
        hanging,
        coarse_solver,
    ):
        field = pltpu.VMEM((8, CELLS), F32)
        vmem = pl.BlockSpec(memory_space=pltpu.VMEM)
        hbm = pl.BlockSpec(memory_space=pltpu.HBM)
        smem = pl.BlockSpec(memory_space=pltpu.SMEM)
        dma = pltpu.SemaphoreType.DMA
        both = pl.pallas_call(
            functools.partial(kernel, n_grp, n_mem),
            out_shape=jax.ShapeDtypeStruct((2, *forcing.shape), F32),
            in_specs=[hbm] * 3 + [vmem] * 5 + [smem] * 2,
            out_specs=hbm,
            scratch_shapes=[
                pltpu.VMEM((3, 8, CELLS), F32),
                pltpu.VMEM((3, 8, CELLS), F32),
                field,
                pltpu.VMEM((24, n_mem * 24), F32),
                pltpu.VMEM((2, 8, CELLS), F32),
                pltpu.VMEM((2, 8, CELLS), F32),
                pltpu.VMEM((8, CELLS + FACE), F32),
                field,
                field,
                field,
                field,
                pltpu.VMEM((3, 8, CELLS), F32),
                pltpu.VMEM((3, 64, LANES), F32),
                pltpu.VMEM((3, 64, LANES), F32),
                pltpu.VMEM((3, 32, LANES), F32),
                pltpu.VMEM((32, LANES), F32),
                pltpu.VMEM((32, LANES), F32),
                pltpu.VMEM((64, 3 * wide), BF16),
                pltpu.VMEM((wide, 192), BF16),
                pltpu.VMEM((32, 96), BF16),
                pltpu.VMEM((32, 3 * wide), BF16),
                pltpu.VMEM((2, 8, 8), F32),
                pltpu.VMEM((3, 8, n_mem * 24), F32),
                pltpu.VMEM((3, n_mem, 8, n_mem * 24), F32),
                pltpu.VMEM((3, 2, 8, n_mem * 24), F32),
                pltpu.VMEM((3, 32, n_mem * 24), F32),
                pltpu.VMEM((3, 2, 8, n_mem * 24), F32),
                pltpu.VMEM((8, LANES), F32),
                pltpu.VMEM((3, n_mem, 8, LANES), F32),
                pltpu.VMEM((64, LANES), F32),
                pltpu.VMEM((n_mem, 64, LANES), F32),
                pltpu.VMEM((SWEEPS, n_mem, 3, 8, LANES), F32),
                pltpu.VMEM((SWEEPS, n_mem, 3, 8, LANES), F32),
                pltpu.VMEM((n_mem, 8, LANES), F32),
                pltpu.VMEM((n_mem, 8, LANES), F32),
                pltpu.VMEM((SWEEPS + 1, 2, 3, 16, LANES), F32),
                pltpu.VMEM((SWEEPS + 1, 2, 3, 16, LANES), F32),
                dma((SWEEPS,)),
                dma((SWEEPS,)),
                dma,
                dma,
                dma((SWEEPS + 1, 2)),
                dma((SWEEPS + 1, 2)),
                dma,
                dma,
                dma((DEG,)),
                dma((DEG,)),
                dma((DEG, 2)),
                dma((DEG, 2)),
                dma((3,)),
                dma((3,)),
                dma((3,)),
                dma((2,)),
            ],
            compiler_params=pltpu.CompilerParams(
                collective_id=0, has_side_effects=True, vmem_limit_bytes=56 * 1024 * 1024
            ),
            name="vcycle",
        )(
            forcing,
            viscosity,
            coarse_solver,
            refinement.reshape(1, 8),
            face_owner.reshape(1, 32),
            face_block.T,
            plane_block.T,
            hanging,
            face_owner.reshape(1, 32),
            face_block.T,
        )
        return both[0], both[1]

    in_specs = (
        P(None, ("grp", "mem"), None),
        P(("grp", "mem"), None),
        P(("grp", "mem")),
        P(("grp", "mem"), None),
        P(("grp", "mem"), None),
        P(("grp", "mem"), None),
        P(("grp", "mem"), None),
        P("grp", "mem", None),
    )
    out_specs = (P(None, ("grp", "mem"), None), P(None, ("grp", "mem"), None))
    return jax.shard_map(local, mesh=mesh, in_specs=in_specs, out_specs=out_specs, check_vma=False)
```

```python
import functools
import math

import jax
import jax.numpy as jnp
from jax import lax
from jax.experimental import pallas as pl
from jax.experimental.pallas import tpu as pltpu
from jax.sharding import PartitionSpec as P

MESH = pl.DeviceIdType.MESH
EDGE = 16
DEG = 3
CELLS = 4096
FACE = 256
LANES = 128
CAP = 4
MASS_TERM = 1.0
LOWER_BOUND = 0.25
UPPER_BOUND = 2.0
SWEEPS = 2 * DEG
F32 = jnp.float32
BF16 = jnp.bfloat16


def chebyshev():
    theta = 0.5 * (UPPER_BOUND + LOWER_BOUND)
    delta = 0.5 * (UPPER_BOUND - LOWER_BOUND)
    sigma = theta / delta
    rho = 1.0 / sigma
    steps = [(0.0, 1.0 / theta)]
    for _ in range(DEG - 1):
        rho_next = 1.0 / (2.0 * sigma - rho)
        steps.append((rho_next * rho, 2.0 * rho_next / delta))
        rho = rho_next
    return steps


def far_first(members):
    tall = members // 4

    def hops(offset):
        dy, dx = offset
        return min(dy, tall - dy) + min(dx, 4 - dx)

    others = [(dy, dx) for dy in range(tall) for dx in range(4) if (dy, dx) != (0, 0)]
    return sorted(others, key=hops, reverse=True)


def by_step(step, values):
    result = jnp.float32(values[-1])
    for place in range(len(values) - 2, -1, -1):
        result = jnp.where(step == place, jnp.float32(values[place]), result)
    return result


def iota(shape, dim):
    return lax.broadcasted_iota(jnp.int32, shape, dim)


def turn(x, shift):
    shift = shift % LANES
    return x if shift == 0 else pltpu.roll(x, shift, 1)


def part(i, v):
    return pl.ds(i * FACE + v * LANES, LANES)


def parts(values):
    high = values.astype(BF16)
    rest = values - high.astype(F32)
    middle = rest.astype(BF16)
    low = (rest - middle.astype(F32)).astype(BF16)
    return jnp.concatenate([high, middle, low], axis=0)


def thrice(one_hot):
    return jnp.concatenate([one_hot] * 3, axis=1)


def pick(one_hot_thrice, values):
    return jnp.dot(one_hot_thrice, parts(values), preferred_element_type=F32)


def coarsen(x):
    lane = iota(x.shape, 1)
    x = x + jnp.where(lane % 2 == 0, turn(x, -1), turn(x, 1))
    x = x + jnp.where(lane // EDGE % 2 == 0, turn(x, -EDGE), turn(x, EDGE))
    return 0.25 * x


def extract(read):
    lane = iota((8, LANES), 1)
    in_row, row = lane % EDGE, lane // EDGE
    zero = jnp.zeros((8, LANES), F32)
    faces = {(v, d): zero for v in range(2) for d in range(4)}
    for i in range(EDGE):
        halves = (read(i, 0), read(i, 1))
        for v in range(2):
            moved = turn(halves[v], i)
            faces[v, 0] = jnp.where(in_row == i, moved, faces[v, 0])
            faces[v, 1] = jnp.where(in_row == (i - 1) % EDGE, moved, faces[v, 1])
        v = i // 8
        moved = turn(jnp.where(lane < EDGE, halves[0], halves[1]), i % 8 * EDGE)
        faces[v, 2] = jnp.where(row == i % 8, moved, faces[v, 2])
        faces[v, 3] = jnp.where(row == (i - 1) % 8, moved, faces[v, 3])
    for v in range(2):
        faces[v, 1] = turn(faces[v, 1], -(EDGE - 1))
        faces[v, 3] = turn(faces[v, 3], EDGE)
    return faces


def tables(owner, face_block, plane_block, hanging, members, has_lower, has_upper):
    wide = members * 8
    rows, columns = iota((32, 32), 0), iota((32, 32), 1)
    given = 4 * (rows % 8) + rows // 8
    given_t = 4 * (columns % 8) + columns // 8
    owner_col = jnp.sum(jnp.where(columns == given, owner, 0), axis=1, keepdims=True)
    own_col = jnp.sum(jnp.where(rows == columns, owner, 0), axis=1, keepdims=True)
    owner_row = jnp.sum(jnp.where(rows == given_t, own_col, 0), axis=0, keepdims=True)
    same = owner_col == owner_row
    rank_col = jnp.sum(jnp.where(same & (columns < rows), 1, 0), axis=1, keepdims=True)
    rank_row = jnp.sum(jnp.where(same & (rows < columns), 1, 0), axis=0, keepdims=True)

    def spread(table, first, of_row):
        tall = jnp.concatenate([table] * 4, axis=0)
        mask = iota(tall.shape, 1) == first + of_row(iota(tall.shape, 0))
        return jnp.sum(jnp.where(mask, tall, 0), axis=1, keepdims=True)

    def spread_t(table, per):
        lanes, which = iota((32, 8), 1), iota((32, 8), 0)
        tall = jnp.zeros((32, 8), jnp.int32)
        for d in range(table.shape[0]):
            tall = jnp.where(which // per == d, table[d : d + 1], tall)
        return jnp.sum(jnp.where(lanes == which % 8, tall, 0), axis=1, keepdims=True)

    block_col = spread_t(face_block, 8)
    side = iota((32, 1), 0) // 8
    wanted = (side + 1 - 2 * (side % 2)) * 8 + block_col
    slot_col = owner_col * 8 + rank_col
    slot_row = owner_row * 8 + rank_row

    def ones(mask):
        return jnp.where(mask, 1.0, 0.0).astype(BF16)

    lanes = iota((32, wide), 1)
    unpack = jnp.concatenate([ones(lanes == slot_col + CAP * v) for v in range(2)], axis=0)
    slots = iota((wide, 32), 0)
    unpack_t = jnp.concatenate([ones(slots == slot_row + CAP * v) for v in range(2)], axis=1)
    lanes = iota((32, LANES), 1)
    source = jnp.concatenate([ones(lanes % 64 == wanted + 32 * v) for v in range(2)], axis=0)
    request = jnp.dot(unpack_t, source, preferred_element_type=F32)
    plane_col = spread_t(plane_block, 16)
    which = iota((32, 32), 0) // 16
    inside = jnp.where(which == 0, has_lower, has_upper) == 1
    plane_pick = ones((columns == rows // 8 * 8 + plane_col) & inside)
    lanes, which = iota((8, 8), 1), iota((8, 8), 0)
    far_pick = []
    for d, exists in enumerate((has_lower, has_upper)):
        chosen = plane_block[d : d + 1]
        chosen = jnp.sum(jnp.where(lanes == which, chosen, 0), axis=1, keepdims=True)
        far_pick.append(jnp.where((lanes == chosen) & (exists == 1), 1.0, 0.0))
    lift_pick = ones(iota((32, wide), 1) == owner_col * 8 + block_col)
    near_hang = spread(hanging, 0, lambda r: r // 8)
    plane_hang = spread(hanging, 4, lambda r: r // 16)
    near_hang = jnp.broadcast_to(near_hang.astype(F32), (32, LANES))
    plane_hang = jnp.broadcast_to(plane_hang.astype(F32), (32, LANES))
    return (
        thrice(unpack),
        request,
        thrice(plane_pick),
        thrice(lift_pick),
        far_pick,
        near_hang,
        plane_hang,
    )


def kernel(
    n_grp,
    n_mem,
    forcing_hbm,
    viscosity_hbm,
    solver_hbm,
    refinement,
    face_owner,
    face_block,
    plane_block,
    hanging,
    owner_scalar,
    block_scalar,
    result,
    velocity,
    residual,
    effective,
    solver,
    weight_k,
    weight_j,
    weight_i,
    ghost_k,
    ghost_j,
    diagonal,
    inverse,
    step_dir,
    faces,
    ghosts,
    plane_ghosts,
    hang_near,
    hang_plane,
    unpack_mat,
    pack_mat,
    plane_mat,
    lift_mat,
    far_mat,
    solver_rows,
    in_solver,
    in_far_solver,
    near_rows,
    far_rows,
    out_vector,
    in_vector,
    out_face,
    in_face,
    out_big,
    in_big,
    out_request,
    in_request,
    out_plane,
    in_plane,
    send_big,
    recv_big,
    send_request,
    recv_request,
    send_plane,
    recv_plane,
    send_face,
    recv_face,
    send_solver,
    recv_solver,
    send_far,
    recv_far,
    send_vector,
    recv_vector,
    load_sem,
    store_sem,
):
    grp, mem = lax.axis_index("grp"), lax.axis_index("mem")
    above = lax.rem(grp + 1, n_grp)
    below = lax.rem(grp + n_grp - 1, n_grp)
    n_coarse = n_mem * 24
    groups_of_lanes = n_coarse // LANES
    wide = n_mem * 8

    mem_y, mem_x = lax.div(mem, 4), lax.rem(mem, 4)
    peers = [
        lax.rem(mem_y + dy, n_mem // 4) * 4 + lax.rem(mem_x + dx, 4) for dy, dx in far_first(n_mem)
    ]
    barrier = pltpu.get_barrier_semaphore()
    for to in peers:
        pl.semaphore_signal(barrier, inc=1, device_id={"mem": to}, device_id_type=MESH)
    for other in (above, below):
        pl.semaphore_signal(barrier, inc=1, device_id={"grp": other}, device_id_type=MESH)

    loads = [
        pltpu.make_async_copy(viscosity_hbm, effective, load_sem.at[0]),
        pltpu.make_async_copy(forcing_hbm, residual, load_sem.at[1]),
        pltpu.make_async_copy(solver_hbm.at[0], solver, load_sem.at[2]),
    ]
    for load in loads:
        load.start()

    def store(place):
        source = (velocity, residual)[place]
        return pltpu.make_async_copy(source, result.at[place], store_sem.at[place])

    lane = iota((8, LANES), 1)
    in_row = lane % EDGE
    row = lane // EDGE
    first_k, last_k = in_row == 0, in_row == EDGE - 1
    first_row, last_row = lane < EDGE, lane >= LANES - EDGE

    def send(outgoing, incoming, send_sem, recv_sem):
        for to in peers:
            pltpu.make_async_remote_copy(
                src_ref=outgoing.at[to],
                dst_ref=incoming.at[mem],
                send_sem=send_sem,
                recv_sem=recv_sem,
                device_id={"mem": to},
                device_id_type=MESH,
            ).start()

    def wait_for(buffer, sem, count=n_mem - 1):
        span = buffer.at[pl.ds(0, count)]
        pltpu.make_async_copy(span, span, sem).wait()

    def plane_copy(which, side):
        return pltpu.make_async_remote_copy(
            src_ref=out_plane.at[which, side],
            dst_ref=in_plane.at[which, side],
            send_sem=send_plane.at[which, side],
            recv_sem=recv_plane.at[which, side],
            device_id={"grp": above if side == 0 else below},
            device_id_type=MESH,
        )

    def far_solver(c, side):
        return pltpu.make_async_remote_copy(
            src_ref=solver_rows.at[c],
            dst_ref=in_far_solver.at[c, side],
            send_sem=send_far.at[c, side],
            recv_sem=recv_far.at[c, side],
            device_id={"grp": above if side == 0 else below},
            device_id_type=MESH,
        )

    block_row = iota((8, LANES), 0)
    level = jnp.sum(
        jnp.where(iota((8, 8), 0) == iota((8, 8), 1), refinement[...], 0), axis=1, keepdims=True
    )
    level = jnp.broadcast_to(level, (8, LANES))
    scale = 1.0 / jnp.left_shift(jnp.ones_like(level), level).astype(F32)
    loads[0].wait()
    for i in range(EDGE):
        for v in range(2):
            effective[:, part(i, v)] = effective[:, part(i, v)] * scale

    def send_planes(which, channels, read):
        for c in range(channels):
            for v in range(2):
                out_plane[which, 0, c, pl.ds(8 * v, 8), :] = read(c, EDGE - 1, v)
                out_plane[which, 1, c, pl.ds(8 * v, 8), :] = read(c, 0, v)
        for side in range(2):
            plane_copy(which, side).start()

    for side in range(2):
        for c in range(1, 3):
            out_plane[SWEEPS, side, c] = jnp.zeros((16, LANES), F32)
    found = extract(lambda i, v: effective[:, part(i, v)])
    for (v, d), register in found.items():
        out_face[pl.ds(v * 32 + d * 8, 8), :] = register

    pl.semaphore_wait(barrier, n_mem - 1 + 2)

    for to in peers:
        pltpu.make_async_remote_copy(
            src_ref=out_face,
            dst_ref=in_face.at[mem],
            send_sem=send_face,
            recv_sem=recv_face,
            device_id={"mem": to},
            device_id_type=MESH,
        ).start()
    send_planes(SWEEPS, 1, lambda c, i, v: effective[:, part(i, v)])
    in_face[mem] = out_face[...]
    unpack, request, plane_pick, lift_pick, far_pick, near_hang, plane_hang = tables(
        face_owner[...],
        face_block[...],
        plane_block[...],
        hanging[...],
        n_mem,
        jnp.where(grp > 0, 1, 0),
        jnp.where(grp < n_grp - 1, 1, 0),
    )
    unpack_mat[...] = unpack
    plane_mat[...] = plane_pick
    lift_mat[...] = lift_pick
    for side in range(2):
        far_mat[side] = far_pick[side]
    hang_near[...] = near_hang
    hang_plane[...] = plane_hang
    out_request[...] = request.reshape(n_mem, 8, LANES)
    send(out_request, in_request, send_request, recv_request)
    in_request[mem] = out_request[mem]

    loads[1].wait()
    loads[2].wait()
    rows, columns = iota((24, 24), 0), iota((24, 24), 1)
    reorder = jnp.where(columns == 3 * (rows % 8) + rows // 8, 1.0, 0.0).astype(BF16)
    ordered = pick(thrice(reorder), solver[...])
    for c in range(3):
        solver_rows[c] = ordered[8 * c : 8 * c + 8]
    for c in range(3):
        for i in range(EDGE):
            for v in range(2):
                velocity[c, :, part(i, v)] = jnp.zeros((8, LANES), F32)
                step_dir[c, :, part(i, v)] = jnp.zeros((8, LANES), F32)
    for i in range(EDGE):
        own = [effective[:, part(i, v)] for v in range(2)]
        back = [turn(x, EDGE) for x in own]
        ahead = [turn(x, -EDGE) for x in own]
        for v in range(2):
            x = own[v]
            lower_k = jnp.where(first_k, 0.0, 0.5 * (x + turn(x, 1)))
            upper_k = jnp.where(last_k, 0.0, 0.5 * (x + turn(x, -1)))
            if v == 0:
                lower_j = jnp.where(first_row, 0.0, 0.5 * (x + back[0]))
                upper_j = 0.5 * (x + jnp.where(last_row, ahead[1], ahead[0]))
            else:
                lower_j = 0.5 * (x + jnp.where(first_row, back[0], back[1]))
                upper_j = jnp.where(last_row, 0.0, 0.5 * (x + ahead[1]))
            weight_k[0, :, part(i, v)] = lower_k
            weight_k[1, :, part(i, v)] = upper_k
            weight_j[0, :, part(i, v)] = lower_j
            weight_j[1, :, part(i, v)] = upper_j
            if i > 0:
                weight_i[:, part(i, v)] = 0.5 * (x + effective[:, part(i - 1, v)])
            diagonal[:, part(i, v)] = MASS_TERM * x + lower_k + upper_k + lower_j + upper_j

    def settle(values, hang):
        return jnp.where(hang == 1.0, coarsen(values), values)

    def side_by_side(buffer, channels):
        return jnp.concatenate([buffer(c) for c in range(channels)], axis=1)

    def receive_planes(which, channels):
        for side in range(2):
            plane_copy(which, side).wait_recv()
        arrived = side_by_side(
            lambda c: in_plane[which, :, c].reshape(32, LANES), channels
        )
        picked = pick(plane_mat[...], arrived)
        for c in range(channels):
            plane_ghosts[c] = settle(picked[:, c * LANES : (c + 1) * LANES], hang_plane[...])

    def unpack_near(matrix, arrived, channels):
        picked = pick(matrix, arrived)
        for c in range(channels):
            for v in range(2):
                ghosts[c, pl.ds(32 * v, 32), :] = settle(
                    picked[32 * v : 32 * v + 32, c * LANES : (c + 1) * LANES], hang_near[...]
                )

    def ghost(c, d, v):
        return ghosts[c, pl.ds(v * 32 + d * 8, 8), :]

    def plane_ghost(c, side, v):
        return plane_ghosts[c, pl.ds(side * 16 + v * 8, 8), :]

    def near_ghosts(c):
        lower_k = [ghost(c, 0, v) for v in range(2)]
        upper_k = [turn(ghost(c, 1, v), EDGE - 1) for v in range(2)]
        lower_j = [ghost(c, 2, v) for v in range(2)]
        upper_j = [turn(ghost(c, 3, v), LANES - EDGE) for v in range(2)]

        def at_k(i, v):
            return turn(jnp.where(in_row == i, lower_k[v], upper_k[v]), -i)

        def at_j(i):
            both = jnp.where(row == i % 8, lower_j[i // 8], upper_j[i // 8])
            return turn(both, -(i % 8) * EDGE)

        return at_k, at_j

    receive_planes(SWEEPS, 1)
    for v in range(2):
        weight_i[:, part(0, v)] = 0.5 * (effective[:, part(0, v)] + plane_ghost(0, 0, v))
        weight_i[:, part(EDGE, v)] = 0.5 * (effective[:, part(EDGE - 1, v)] + plane_ghost(0, 1, v))
    wait_for(in_face, recv_face)
    for d in range(4):
        for b in range(8):
            owner = owner_scalar[0, 4 * b + d]
            wanted = (d + 1 - 2 * (d % 2)) * 8 + block_scalar[d, b]
            for v in range(2):
                ghosts[0, pl.ds(v * 32 + d * 8 + b, 1), :] = in_face[
                    owner, pl.ds(v * 32 + wanted, 1), :
                ]
    for v in range(2):
        ghosts[0, pl.ds(32 * v, 32), :] = settle(ghosts[0, pl.ds(32 * v, 32), :], hang_near[...])
    k_ghost, j_ghost = near_ghosts(0)
    for i in range(EDGE):
        beside_j = j_ghost(i)
        for v in range(2):
            x = effective[:, part(i, v)]
            at_k = jnp.where(first_k | last_k, 0.5 * (x + k_ghost(i, v)), 0.0)
            edge = first_row if v == 0 else last_row
            at_j = jnp.where(edge, 0.5 * (x + beside_j), 0.0)
            ghost_k[:, part(i, v)] = at_k
            ghost_j[:, part(i, v)] = at_j
            whole = (
                diagonal[:, part(i, v)]
                + (weight_i[:, part(i, v)] + weight_i[:, part(i + 1, v)])
                + (at_k + at_j)
            )
            diagonal[:, part(i, v)] = whole
            inverse[:, part(i, v)] = 1.0 / whole

    steps = chebyshev()
    ghosts[...] = jnp.zeros(ghosts.shape, F32)
    plane_ghosts[...] = jnp.zeros(plane_ghosts.shape, F32)
    wait_for(in_request, recv_request)
    request = in_request[...].reshape(wide, LANES)
    pack_mat[...] = jnp.concatenate([request, request[:, :64]], axis=1).astype(BF16)

    def across_faces(c):
        k_ghost, j_ghost = near_ghosts(c)

        def new(i):
            beside_j = j_ghost(i)
            result = []
            for v in range(2):
                change = ghost_k[:, part(i, v)] * k_ghost(i, v)
                change = change + ghost_j[:, part(i, v)] * beside_j
                if i == 0:
                    change = change + weight_i[:, part(0, v)] * plane_ghost(c, 0, v)
                if i == EDGE - 1:
                    change = change + weight_i[:, part(EDGE, v)] * plane_ghost(c, 1, v)
                result.append(residual[c, :, part(i, v)] + change)
            return result

        return new

    def coarse_level():
        totals = []
        for c in range(3):
            total = jnp.zeros((8, LANES), F32)
            new = across_faces(c)
            for i in range(EDGE):
                for v, value in enumerate(new(i)):
                    residual[c, :, part(i, v)] = value
                    total = total + value
            totals.append(jnp.sum(total, axis=1, keepdims=True) / math.sqrt(CELLS))
        chunks = []
        for q in range(groups_of_lanes):
            place = lane + q * LANES - 24 * mem - 3 * block_row
            mine = jnp.zeros((8, LANES), F32)
            for c in range(3):
                mine = jnp.where(place == c, totals[c], mine)
            chunks.append(jnp.sum(mine, axis=0, keepdims=True))
        tile = jnp.zeros((8, LANES), F32)
        for q in range(groups_of_lanes):
            tile = jnp.where(block_row == q, chunks[q], tile)
        out_vector[...] = tile

        def send_vector_to(other, to, slot):
            pltpu.make_async_remote_copy(
                src_ref=out_vector,
                dst_ref=in_vector.at[slot, mem],
                send_sem=send_vector.at[slot],
                recv_sem=recv_vector.at[slot],
                device_id={"grp": other, "mem": to},
                device_id_type=MESH,
            ).start()

        for to in peers:
            send_vector_to(above, to, 1)
            send_vector_to(below, to, 2)
            send_vector_to(grp, to, 0)
        send_vector_to(above, mem, 1)
        send_vector_to(below, mem, 2)
        in_vector[0, mem] = tile

        for c in range(3):
            wait_for(in_solver.at[c], recv_solver.at[c])
            in_solver[c, mem] = solver_rows[c]
            near_rows[c] = pick(lift_mat[...], in_solver[c].reshape(wide, n_coarse))
            for side in range(2):
                far_solver(c, side).wait_recv()
                source = in_far_solver[c, side]
                chosen = jnp.zeros((8, n_coarse), F32)
                for b in range(8):
                    wants = far_mat[side][:, b : b + 1]
                    chosen = jnp.where(wants == 1.0, source[b : b + 1], chosen)
                far_rows[c, side] = chosen

        def vector_of(slot):
            whole = in_vector[slot, 0]
            for m in range(1, n_mem):
                whole = whole + in_vector[slot, m]
            return [jnp.broadcast_to(whole[q : q + 1], (8, LANES)) for q in range(groups_of_lanes)]

        def correction(rows, vector):
            product = rows[:, :LANES] * vector[0]
            for q in range(1, groups_of_lanes):
                product = product + rows[:, q * LANES : (q + 1) * LANES] * vector[q]
            return jnp.broadcast_to(jnp.sum(product, axis=1, keepdims=True), (8, LANES))

        for side in range(2):
            wait_for(in_vector.at[1 + side], recv_vector.at[1 + side], n_mem)
        far_vectors = [vector_of(1), vector_of(2)]
        wait_for(in_vector.at[0], recv_vector.at[0])
        vector = vector_of(0)
        for c in range(3):
            mine = correction(solver_rows[c], vector)
            gap = [
                mine - correction(near_rows[c, pl.ds(8 * d, 8), :], vector) for d in range(4)
            ]
            gap_lower, gap_upper = [
                mine - correction(far_rows[c, side], far_vectors[side]) for side in range(2)
            ]
            gap_k = jnp.where(first_k, gap[0], gap[1])
            for i in range(EDGE):
                for v in range(2):
                    change = MASS_TERM * effective[:, part(i, v)] * mine
                    change = change + ghost_k[:, part(i, v)] * gap_k
                    change = change + ghost_j[:, part(i, v)] * gap[2 + v]
                    if i == 0:
                        change = change + weight_i[:, part(0, v)] * gap_lower
                    if i == EDGE - 1:
                        change = change + weight_i[:, part(EDGE, v)] * gap_upper
                    residual[c, :, part(i, v)] = residual[c, :, part(i, v)] - change
                    velocity[c, :, part(i, v)] = velocity[c, :, part(i, v)] + mine
        ghosts[...] = jnp.zeros(ghosts.shape, F32)
        plane_ghosts[...] = jnp.zeros(plane_ghosts.shape, F32)

    def sweep(t, carry):
        @pl.when(t == DEG)
        def _():
            coarse_level()

        step = lax.rem(t, DEG)
        keep = by_step(step, [first for first, _ in steps])
        gain = by_step(step, [second for _, second in steps])

        for c in range(3):
            new = across_faces(c)
            moved = {}

            def step_of(i, v):
                if v == 0:
                    for half, value in enumerate(new(i)):
                        residual[c, :, part(i, half)] = value
                        ahead = keep * step_dir[c, :, part(i, half)] + gain * (
                            value * inverse[:, part(i, half)]
                        )
                        step_dir[c, :, part(i, half)] = ahead
                        moved[i, half] = ahead
                return moved[i, v]

            for (v, d), register in extract(step_of).items():
                faces[c, pl.ds(v * 32 + d * 8, 8), :] = register

        packed = pick(pack_mat[...], side_by_side(lambda c: faces[c], 3))
        for c in range(3):
            out_big[t, :, c] = packed[:, c * LANES : (c + 1) * LANES].reshape(n_mem, 8, LANES)
        send(out_big.at[t], in_big.at[t], send_big.at[t], recv_big.at[t])
        send_planes(t, 3, lambda c, i, v: step_dir[c, :, part(i, v)])

        @pl.when(t < DEG)
        def _():
            for to in peers:
                pltpu.make_async_remote_copy(
                    src_ref=solver_rows.at[t],
                    dst_ref=in_solver.at[t, mem],
                    send_sem=send_solver.at[t],
                    recv_sem=recv_solver.at[t],
                    device_id={"mem": to},
                    device_id_type=MESH,
                ).start()
            for side in range(2):
                far_solver(t, side).start()

        in_big[t, mem] = out_big[t, mem]

        @pl.loop(0, 3)
        def _(c):
            for i in range(EDGE):
                own = [step_dir[c, :, part(i, v)] for v in range(2)]
                back = [turn(x, EDGE) for x in own]
                ahead = [turn(x, -EDGE) for x in own]
                for v in range(2):
                    x = own[v]
                    if v == 0:
                        lower_j, upper_j = back[0], jnp.where(last_row, ahead[1], ahead[0])
                    else:
                        lower_j, upper_j = jnp.where(first_row, back[0], back[1]), ahead[1]
                    change = weight_k[0, :, part(i, v)] * turn(x, 1)
                    change = change + weight_k[1, :, part(i, v)] * turn(x, -1)
                    change = change + weight_j[0, :, part(i, v)] * lower_j
                    change = change + weight_j[1, :, part(i, v)] * upper_j
                    if i > 0:
                        change = change + weight_i[:, part(i, v)] * step_dir[c, :, part(i - 1, v)]
                    if i < EDGE - 1:
                        change = change + weight_i[:, part(i + 1, v)] * step_dir[
                            c, :, part(i + 1, v)
                        ]
                    residual[c, :, part(i, v)] = residual[c, :, part(i, v)] - (
                        diagonal[:, part(i, v)] * x - change
                    )
                    velocity[c, :, part(i, v)] = velocity[c, :, part(i, v)] + x

        @pl.when(t == SWEEPS - 1)
        def _():
            store(0).start()

        receive_planes(t, 3)
        wait_for(in_big.at[t], recv_big.at[t])
        unpack_near(
            unpack_mat[...],
            side_by_side(lambda c: in_big[t, :, c].reshape(wide, LANES), 3),
            3,
        )
        return carry

    lax.fori_loop(0, SWEEPS, sweep, 0)
    for c in range(3):
        new = across_faces(c)
        for i in range(EDGE):
            for v, value in enumerate(new(i)):
                residual[c, :, part(i, v)] = value

    store(1).start()
    wait_for(in_face, send_face)
    for t in range(SWEEPS):
        wait_for(out_big.at[t], send_big.at[t])
    for t in range(DEG):
        wait_for(in_solver.at[t], send_solver.at[t])
        for side in range(2):
            far_solver(t, side).wait_send()
    wait_for(in_vector.at[0], send_vector.at[0])
    for side in range(2):
        wait_for(in_vector.at[1 + side], send_vector.at[1 + side], n_mem)
    wait_for(out_request, send_request)
    for t in range(SWEEPS + 1):
        for side in range(2):
            plane_copy(t, side).wait_send()
    for place in range(2):
        store(place).wait()


def solution(mesh):
    n_grp, n_mem = mesh.shape["grp"], mesh.shape["mem"]
    wide = n_mem * 8

    def local(
        forcing,
        viscosity,
        refinement,
        face_owner,
        face_block,
        plane_block,
        hanging,
        coarse_solver,
    ):
        field = pltpu.VMEM((8, CELLS), F32)
        vmem = pl.BlockSpec(memory_space=pltpu.VMEM)
        hbm = pl.BlockSpec(memory_space=pltpu.HBM)
        smem = pl.BlockSpec(memory_space=pltpu.SMEM)
        dma = pltpu.SemaphoreType.DMA
        both = pl.pallas_call(
            functools.partial(kernel, n_grp, n_mem),
            out_shape=jax.ShapeDtypeStruct((2, *forcing.shape), F32),
            in_specs=[hbm] * 3 + [vmem] * 5 + [smem] * 2,
            out_specs=hbm,
            scratch_shapes=[
                pltpu.VMEM((3, 8, CELLS), F32),
                pltpu.VMEM((3, 8, CELLS), F32),
                field,
                pltpu.VMEM((24, n_mem * 24), F32),
                pltpu.VMEM((2, 8, CELLS), F32),
                pltpu.VMEM((2, 8, CELLS), F32),
                pltpu.VMEM((8, CELLS + FACE), F32),
                field,
                field,
                field,
                field,
                pltpu.VMEM((3, 8, CELLS), F32),
                pltpu.VMEM((3, 64, LANES), F32),
                pltpu.VMEM((3, 64, LANES), F32),
                pltpu.VMEM((3, 32, LANES), F32),
                pltpu.VMEM((32, LANES), F32),
                pltpu.VMEM((32, LANES), F32),
                pltpu.VMEM((64, 3 * wide), BF16),
                pltpu.VMEM((wide, 192), BF16),
                pltpu.VMEM((32, 96), BF16),
                pltpu.VMEM((32, 3 * wide), BF16),
                pltpu.VMEM((2, 8, 8), F32),
                pltpu.VMEM((3, 8, n_mem * 24), F32),
                pltpu.VMEM((3, n_mem, 8, n_mem * 24), F32),
                pltpu.VMEM((3, 2, 8, n_mem * 24), F32),
                pltpu.VMEM((3, 32, n_mem * 24), F32),
                pltpu.VMEM((3, 2, 8, n_mem * 24), F32),
                pltpu.VMEM((8, LANES), F32),
                pltpu.VMEM((3, n_mem, 8, LANES), F32),
                pltpu.VMEM((64, LANES), F32),
                pltpu.VMEM((n_mem, 64, LANES), F32),
                pltpu.VMEM((SWEEPS, n_mem, 3, 8, LANES), F32),
                pltpu.VMEM((SWEEPS, n_mem, 3, 8, LANES), F32),
                pltpu.VMEM((n_mem, 8, LANES), F32),
                pltpu.VMEM((n_mem, 8, LANES), F32),
                pltpu.VMEM((SWEEPS + 1, 2, 3, 16, LANES), F32),
                pltpu.VMEM((SWEEPS + 1, 2, 3, 16, LANES), F32),
                dma((SWEEPS,)),
                dma((SWEEPS,)),
                dma,
                dma,
                dma((SWEEPS + 1, 2)),
                dma((SWEEPS + 1, 2)),
                dma,
                dma,
                dma((DEG,)),
                dma((DEG,)),
                dma((DEG, 2)),
                dma((DEG, 2)),
                dma((3,)),
                dma((3,)),
                dma((3,)),
                dma((2,)),
            ],
            compiler_params=pltpu.CompilerParams(
                collective_id=0, has_side_effects=True, vmem_limit_bytes=56 * 1024 * 1024
            ),
            name="vcycle",
        )(
            forcing,
            viscosity,
            coarse_solver,
            refinement.reshape(1, 8),
            face_owner.reshape(1, 32),
            face_block.T,
            plane_block.T,
            hanging,
            face_owner.reshape(1, 32),
            face_block.T,
        )
        return both[0], both[1]

    in_specs = (
        P(None, ("grp", "mem"), None),
        P(("grp", "mem"), None),
        P(("grp", "mem")),
        P(("grp", "mem"), None),
        P(("grp", "mem"), None),
        P(("grp", "mem"), None),
        P(("grp", "mem"), None),
        P("grp", "mem", None),
    )
    out_specs = (P(None, ("grp", "mem"), None), P(None, ("grp", "mem"), None))
    return jax.shard_map(local, mesh=mesh, in_specs=in_specs, out_specs=out_specs, check_vma=False)
```

```python
import functools
import math

import jax
import jax.numpy as jnp
from jax import lax
from jax.experimental import pallas as pl
from jax.experimental.pallas import tpu as pltpu
from jax.sharding import PartitionSpec as P

MESH = pl.DeviceIdType.MESH
EDGE = 16
DEG = 3
CELLS = 4096
FACE = 256
LANES = 128
CAP = 4
MASS_TERM = 1.0
LOWER_BOUND = 0.25
UPPER_BOUND = 2.0
SWEEPS = 2 * DEG
GROUPS = ((0, 1, 2),)
F32 = jnp.float32
BF16 = jnp.bfloat16


def chebyshev():
    theta = 0.5 * (UPPER_BOUND + LOWER_BOUND)
    delta = 0.5 * (UPPER_BOUND - LOWER_BOUND)
    sigma = theta / delta
    rho = 1.0 / sigma
    steps = [(0.0, 1.0 / theta)]
    for _ in range(DEG - 1):
        rho_next = 1.0 / (2.0 * sigma - rho)
        steps.append((rho_next * rho, 2.0 * rho_next / delta))
        rho = rho_next
    return steps


def far_first(members):
    tall = members // 4

    def hops(offset):
        dy, dx = offset
        return min(dy, tall - dy) + min(dx, 4 - dx)

    others = [(dy, dx) for dy in range(tall) for dx in range(4) if (dy, dx) != (0, 0)]
    return sorted(others, key=hops, reverse=True)


def by_step(step, values):
    result = jnp.float32(values[-1])
    for place in range(len(values) - 2, -1, -1):
        result = jnp.where(step == place, jnp.float32(values[place]), result)
    return result


def iota(shape, dim):
    return lax.broadcasted_iota(jnp.int32, shape, dim)


def turn(x, shift):
    shift = shift % LANES
    return x if shift == 0 else pltpu.roll(x, shift, 1)


def part(i, v):
    return pl.ds(i * FACE + v * LANES, LANES)


def parts(values):
    high = values.astype(BF16)
    rest = values - high.astype(F32)
    middle = rest.astype(BF16)
    low = (rest - middle.astype(F32)).astype(BF16)
    return jnp.concatenate([high, middle, low], axis=0)


def thrice(one_hot):
    return jnp.concatenate([one_hot] * 3, axis=1)


def pick(one_hot_thrice, values):
    return jnp.dot(one_hot_thrice, parts(values), preferred_element_type=F32)


def coarsen(x):
    lane = iota(x.shape, 1)
    x = x + jnp.where(lane % 2 == 0, turn(x, -1), turn(x, 1))
    x = x + jnp.where(lane // EDGE % 2 == 0, turn(x, -EDGE), turn(x, EDGE))
    return 0.25 * x


def extract(read):
    lane = iota((8, LANES), 1)
    in_row, row = lane % EDGE, lane // EDGE
    zero = jnp.zeros((8, LANES), F32)
    faces = {(v, d): zero for v in range(2) for d in range(4)}
    for i in range(EDGE):
        halves = (read(i, 0), read(i, 1))
        for v in range(2):
            moved = turn(halves[v], i)
            faces[v, 0] = jnp.where(in_row == i, moved, faces[v, 0])
            faces[v, 1] = jnp.where(in_row == (i - 1) % EDGE, moved, faces[v, 1])
        v = i // 8
        moved = turn(jnp.where(lane < EDGE, halves[0], halves[1]), i % 8 * EDGE)
        faces[v, 2] = jnp.where(row == i % 8, moved, faces[v, 2])
        faces[v, 3] = jnp.where(row == (i - 1) % 8, moved, faces[v, 3])
    for v in range(2):
        faces[v, 1] = turn(faces[v, 1], -(EDGE - 1))
        faces[v, 3] = turn(faces[v, 3], EDGE)
    return faces


def tables(owner, face_block, plane_block, hanging, members, has_lower, has_upper):
    wide = members * 8
    rows, columns = iota((32, 32), 0), iota((32, 32), 1)
    given = 4 * (rows % 8) + rows // 8
    given_t = 4 * (columns % 8) + columns // 8
    owner_col = jnp.sum(jnp.where(columns == given, owner, 0), axis=1, keepdims=True)
    own_col = jnp.sum(jnp.where(rows == columns, owner, 0), axis=1, keepdims=True)
    owner_row = jnp.sum(jnp.where(rows == given_t, own_col, 0), axis=0, keepdims=True)
    same = owner_col == owner_row
    rank_col = jnp.sum(jnp.where(same & (columns < rows), 1, 0), axis=1, keepdims=True)
    rank_row = jnp.sum(jnp.where(same & (rows < columns), 1, 0), axis=0, keepdims=True)

    def spread(table, first, of_row):
        tall = jnp.concatenate([table] * 4, axis=0)
        mask = iota(tall.shape, 1) == first + of_row(iota(tall.shape, 0))
        return jnp.sum(jnp.where(mask, tall, 0), axis=1, keepdims=True)

    def spread_t(table, per):
        lanes, which = iota((32, 8), 1), iota((32, 8), 0)
        tall = jnp.zeros((32, 8), jnp.int32)
        for d in range(table.shape[0]):
            tall = jnp.where(which // per == d, table[d : d + 1], tall)
        return jnp.sum(jnp.where(lanes == which % 8, tall, 0), axis=1, keepdims=True)

    block_col = spread_t(face_block, 8)
    side = iota((32, 1), 0) // 8
    wanted = (side + 1 - 2 * (side % 2)) * 8 + block_col
    slot_col = owner_col * 8 + rank_col
    slot_row = owner_row * 8 + rank_row

    def ones(mask):
        return jnp.where(mask, 1.0, 0.0).astype(BF16)

    lanes = iota((32, wide), 1)
    unpack = jnp.concatenate([ones(lanes == slot_col + CAP * v) for v in range(2)], axis=0)
    slots = iota((wide, 32), 0)
    unpack_t = jnp.concatenate([ones(slots == slot_row + CAP * v) for v in range(2)], axis=1)
    lanes = iota((32, LANES), 1)
    source = jnp.concatenate([ones(lanes % 64 == wanted + 32 * v) for v in range(2)], axis=0)
    request = jnp.dot(unpack_t, source, preferred_element_type=F32)
    plane_col = spread_t(plane_block, 16)
    which = iota((32, 32), 0) // 16
    inside = jnp.where(which == 0, has_lower, has_upper) == 1
    plane_pick = ones((columns == rows // 8 * 8 + plane_col) & inside)
    lanes, which = iota((8, 8), 1), iota((8, 8), 0)
    far_pick = []
    for d, exists in enumerate((has_lower, has_upper)):
        chosen = plane_block[d : d + 1]
        chosen = jnp.sum(jnp.where(lanes == which, chosen, 0), axis=1, keepdims=True)
        far_pick.append(jnp.where((lanes == chosen) & (exists == 1), 1.0, 0.0))
    lift_pick = ones(iota((32, wide), 1) == owner_col * 8 + block_col)
    near_hang = spread(hanging, 0, lambda r: r // 8)
    plane_hang = spread(hanging, 4, lambda r: r // 16)
    near_hang = jnp.broadcast_to(near_hang.astype(F32), (32, LANES))
    plane_hang = jnp.broadcast_to(plane_hang.astype(F32), (32, LANES))
    return (
        thrice(unpack),
        request,
        thrice(plane_pick),
        thrice(lift_pick),
        far_pick,
        near_hang,
        plane_hang,
    )


def kernel(
    n_grp,
    n_mem,
    forcing_hbm,
    viscosity_hbm,
    solver_hbm,
    refinement_hbm,
    owner_hbm,
    block_hbm,
    plane_hbm,
    hanging_hbm,
    result,
    refinement,
    face_owner,
    face_block,
    plane_block,
    hanging,
    owner_scalar,
    block_scalar,
    velocity,
    residual,
    effective,
    solver,
    weight_k,
    weight_j,
    weight_i,
    ghost_k,
    ghost_j,
    diagonal,
    inverse,
    step_dir,
    ghosts,
    lifts,
    hang_near,
    hang_plane,
    unpack_mat,
    pack_mat,
    plane_mat,
    lift_mat,
    far_mat,
    solver_rows,
    in_solver,
    in_far_solver,
    near_rows,
    far_rows,
    out_vector,
    in_vector,
    out_face,
    in_face,
    out_request,
    in_request,
    out_plane,
    in_plane,
    send_request,
    recv_request,
    send_plane,
    recv_plane,
    send_face,
    recv_face,
    send_solver,
    recv_solver,
    send_far,
    recv_far,
    send_vector,
    recv_vector,
    load_sem,
    store_sem,
    *group_refs,
):
    grp, mem = lax.axis_index("grp"), lax.axis_index("mem")
    above = lax.rem(grp + 1, n_grp)
    below = lax.rem(grp + n_grp - 1, n_grp)
    n_coarse = n_mem * 24
    buffers = [group_refs[8 * g : 8 * g + 8] for g in range(len(GROUPS))]
    groups_of_lanes = n_coarse // LANES
    wide = n_mem * 8

    mem_y, mem_x = lax.div(mem, 4), lax.rem(mem, 4)
    peers = [
        lax.rem(mem_y + dy, n_mem // 4) * 4 + lax.rem(mem_x + dx, 4) for dy, dx in far_first(n_mem)
    ]
    barrier = pltpu.get_barrier_semaphore()
    for to in peers:
        pl.semaphore_signal(barrier, inc=1, device_id={"mem": to}, device_id_type=MESH)
    for other in (above, below):
        pl.semaphore_signal(barrier, inc=1, device_id={"grp": other}, device_id_type=MESH)

    loads = [
        pltpu.make_async_copy(viscosity_hbm, effective, load_sem.at[0]),
        pltpu.make_async_copy(forcing_hbm, residual, load_sem.at[1]),
        pltpu.make_async_copy(solver_hbm.at[0], solver, load_sem.at[2]),
    ]
    small = [
        (refinement_hbm, refinement),
        (owner_hbm, face_owner),
        (block_hbm, face_block),
        (plane_hbm, plane_block),
        (hanging_hbm, hanging),
        (owner_hbm, owner_scalar),
        (block_hbm, block_scalar),
    ]
    small = [
        pltpu.make_async_copy(source, target, load_sem.at[3 + place])
        for place, (source, target) in enumerate(small)
    ]
    for load in [*small, *loads]:
        load.start()

    def store(place):
        source = (velocity, residual)[place]
        return pltpu.make_async_copy(source, result.at[place], store_sem.at[place])

    lane = iota((8, LANES), 1)
    in_row = lane % EDGE
    row = lane // EDGE
    first_k, last_k = in_row == 0, in_row == EDGE - 1
    first_row, last_row = lane < EDGE, lane >= LANES - EDGE

    def send(outgoing, incoming, send_sem, recv_sem):
        for to in peers:
            pltpu.make_async_remote_copy(
                src_ref=outgoing.at[to],
                dst_ref=incoming.at[mem],
                send_sem=send_sem,
                recv_sem=recv_sem,
                device_id={"mem": to},
                device_id_type=MESH,
            ).start()

    def wait_for(buffer, sem, count=n_mem - 1):
        span = buffer.at[pl.ds(0, count)]
        pltpu.make_async_copy(span, span, sem).wait()

    def plane_copy(side, outgoing, incoming, send_sem, recv_sem):
        return pltpu.make_async_remote_copy(
            src_ref=outgoing.at[side],
            dst_ref=incoming.at[side],
            send_sem=send_sem.at[side],
            recv_sem=recv_sem.at[side],
            device_id={"grp": above if side == 0 else below},
            device_id_type=MESH,
        )

    def effective_plane(side):
        return plane_copy(side, out_plane, in_plane, send_plane, recv_plane)

    def step_plane(g, t, side):
        return plane_copy(side, *[ref.at[t] for ref in buffers[g][4:]])

    def far_solver(c, side):
        return pltpu.make_async_remote_copy(
            src_ref=solver_rows.at[c],
            dst_ref=in_far_solver.at[c, side],
            send_sem=send_far.at[c, side],
            recv_sem=recv_far.at[c, side],
            device_id={"grp": above if side == 0 else below},
            device_id_type=MESH,
        )

    for load in small:
        load.wait()

    block_row = iota((8, LANES), 0)
    level = jnp.sum(
        jnp.where(iota((8, 8), 0) == iota((8, 8), 1), refinement[...], 0), axis=1, keepdims=True
    )
    level = jnp.broadcast_to(level, (8, LANES))
    scale = 1.0 / jnp.left_shift(jnp.ones_like(level), level).astype(F32)
    loads[0].wait()
    for i in range(EDGE):
        for v in range(2):
            effective[:, part(i, v)] = effective[:, part(i, v)] * scale

    found = extract(lambda i, v: effective[:, part(i, v)])
    for (v, d), register in found.items():
        out_face[pl.ds(v * 32 + d * 8, 8), :] = register

    unpack, request, plane_pick, lift_pick, far_pick, near_hang, plane_hang = tables(
        face_owner[...],
        face_block[...],
        plane_block[...],
        hanging[...],
        n_mem,
        jnp.where(grp > 0, 1, 0),
        jnp.where(grp < n_grp - 1, 1, 0),
    )
    unpack_mat[...] = unpack
    plane_mat[...] = plane_pick
    lift_mat[...] = lift_pick
    for side in range(2):
        far_mat[side] = far_pick[side]
    hang_near[...] = near_hang
    hang_plane[...] = plane_hang
    out_request[...] = request.reshape(n_mem, 8, LANES)

    pl.semaphore_wait(barrier, n_mem - 1 + 2)

    send(out_request, in_request, send_request, recv_request)
    for to in peers:
        pltpu.make_async_remote_copy(
            src_ref=out_face,
            dst_ref=in_face.at[mem],
            send_sem=send_face,
            recv_sem=recv_face,
            device_id={"mem": to},
            device_id_type=MESH,
        ).start()
    for v in range(2):
        out_plane[0, pl.ds(8 * v, 8), :] = effective[:, part(EDGE - 1, v)]
        out_plane[1, pl.ds(8 * v, 8), :] = effective[:, part(0, v)]
    for side in range(2):
        effective_plane(side).start()
    in_face[mem] = out_face[...]
    in_request[mem] = out_request[mem]

    loads[1].wait()
    loads[2].wait()
    rows, columns = iota((24, 24), 0), iota((24, 24), 1)
    reorder = jnp.where(columns == 3 * (rows % 8) + rows // 8, 1.0, 0.0).astype(BF16)
    ordered = pick(thrice(reorder), solver[...])
    for c in range(3):
        solver_rows[c] = ordered[8 * c : 8 * c + 8]
    for c in range(3):
        for i in range(EDGE):
            for v in range(2):
                velocity[c, :, part(i, v)] = jnp.zeros((8, LANES), F32)
    for i in range(EDGE):
        own = [effective[:, part(i, v)] for v in range(2)]
        back = [turn(x, EDGE) for x in own]
        ahead = [turn(x, -EDGE) for x in own]
        for v in range(2):
            x = own[v]
            lower_k = jnp.where(first_k, 0.0, 0.5 * (x + turn(x, 1)))
            upper_k = jnp.where(last_k, 0.0, 0.5 * (x + turn(x, -1)))
            if v == 0:
                lower_j = jnp.where(first_row, 0.0, 0.5 * (x + back[0]))
                upper_j = 0.5 * (x + jnp.where(last_row, ahead[1], ahead[0]))
            else:
                lower_j = 0.5 * (x + jnp.where(first_row, back[0], back[1]))
                upper_j = jnp.where(last_row, 0.0, 0.5 * (x + ahead[1]))
            weight_k[0, :, part(i, v)] = lower_k
            weight_k[1, :, part(i, v)] = upper_k
            weight_j[0, :, part(i, v)] = lower_j
            weight_j[1, :, part(i, v)] = upper_j
            if i > 0:
                weight_i[:, part(i, v)] = 0.5 * (x + effective[:, part(i - 1, v)])
            diagonal[:, part(i, v)] = MASS_TERM * x + lower_k + upper_k + lower_j + upper_j

    def settle(values, hang):
        return jnp.where(hang == 1.0, coarsen(values), values)

    def side_by_side(pieces):
        return pieces[0] if len(pieces) == 1 else jnp.concatenate(pieces, axis=1)

    def columns(values, count):
        return [values[:, l * LANES : (l + 1) * LANES] for l in range(count)]

    def receive(g, t):
        count = len(GROUPS[g])
        incoming, recv_sem, planes = buffers[g][1], buffers[g][3], buffers[g][5]
        for side in range(2):
            step_plane(g, t, side).wait_recv()
        far = pick(
            plane_mat[...],
            side_by_side([planes[t, :, l].reshape(32, LANES) for l in range(count)]),
        )
        far = [settle(values, hang_plane[...]) for values in columns(far, count)]
        wait_for(incoming.at[t], recv_sem.at[t])
        near = pick(
            unpack_mat[...],
            side_by_side([incoming[t, :, l].reshape(wide, LANES) for l in range(count)]),
        )
        result = []
        for l, values in enumerate(columns(near, count)):
            halves = [settle(values[32 * v : 32 * v + 32], hang_near[...]) for v in range(2)]
            result.append(
                (
                    {(d, v): halves[v][8 * d : 8 * d + 8] for d in range(4) for v in range(2)},
                    {
                        (side, v): far[l][16 * side + 8 * v : 16 * side + 8 * v + 8]
                        for side in range(2)
                        for v in range(2)
                    },
                )
            )
        return result

    def near_ghosts(near):
        lower_k = [near[0, v] for v in range(2)]
        upper_k = [turn(near[1, v], EDGE - 1) for v in range(2)]
        lower_j = [near[2, v] for v in range(2)]
        upper_j = [turn(near[3, v], LANES - EDGE) for v in range(2)]

        def at_k(i, v):
            return turn(jnp.where(in_row == i, lower_k[v], upper_k[v]), -i)

        def at_j(i):
            both = jnp.where(row == i % 8, lower_j[i // 8], upper_j[i // 8])
            return turn(both, -(i % 8) * EDGE)

        return at_k, at_j

    for side in range(2):
        effective_plane(side).wait_recv()
    far = settle(pick(plane_mat[...], in_plane[...].reshape(32, LANES)), hang_plane[...])
    for v in range(2):
        weight_i[:, part(0, v)] = 0.5 * (effective[:, part(0, v)] + far[8 * v : 8 * v + 8])
        weight_i[:, part(EDGE, v)] = 0.5 * (
            effective[:, part(EDGE - 1, v)] + far[16 + 8 * v : 24 + 8 * v]
        )
    wait_for(in_face, recv_face)
    for d in range(4):
        for b in range(8):
            owner = owner_scalar[0, 4 * b + d]
            wanted = (d + 1 - 2 * (d % 2)) * 8 + block_scalar[d, b]
            for v in range(2):
                ghosts[pl.ds(v * 32 + d * 8 + b, 1), :] = in_face[
                    owner, pl.ds(v * 32 + wanted, 1), :
                ]
    halves = [settle(ghosts[pl.ds(32 * v, 32), :], hang_near[...]) for v in range(2)]
    k_ghost, j_ghost = near_ghosts(
        {(d, v): halves[v][8 * d : 8 * d + 8] for d in range(4) for v in range(2)}
    )
    for i in range(EDGE):
        beside_j = j_ghost(i)
        for v in range(2):
            x = effective[:, part(i, v)]
            at_k = jnp.where(first_k | last_k, 0.5 * (x + k_ghost(i, v)), 0.0)
            edge = first_row if v == 0 else last_row
            at_j = jnp.where(edge, 0.5 * (x + beside_j), 0.0)
            ghost_k[:, part(i, v)] = at_k
            ghost_j[:, part(i, v)] = at_j
            whole = (
                diagonal[:, part(i, v)]
                + (weight_i[:, part(i, v)] + weight_i[:, part(i + 1, v)])
                + (at_k + at_j)
            )
            diagonal[:, part(i, v)] = whole
            inverse[:, part(i, v)] = 1.0 / whole

    steps = chebyshev()
    wait_for(in_request, recv_request)
    request = in_request[...].reshape(wide, LANES)
    pack_mat[...] = jnp.concatenate([request, request[:, :64]], axis=1).astype(BF16)

    def across_faces(c, near, far):
        k_ghost, j_ghost = near_ghosts(near)

        def new(i):
            beside_j = j_ghost(i)
            result = []
            for v in range(2):
                change = ghost_k[:, part(i, v)] * k_ghost(i, v)
                change = change + ghost_j[:, part(i, v)] * beside_j
                if i == 0:
                    change = change + weight_i[:, part(0, v)] * far[0, v]
                if i == EDGE - 1:
                    change = change + weight_i[:, part(EDGE, v)] * far[1, v]
                result.append(residual[c, :, part(i, v)] + change)
            return result

        return new

    def coarse_level():
        totals = [None] * 3
        for g, group in enumerate(GROUPS):
            for c, arrived in zip(group, receive(g, DEG - 1)):
                total = jnp.zeros((8, LANES), F32)
                new = across_faces(c, *arrived)
                for i in range(EDGE):
                    for v, value in enumerate(new(i)):
                        residual[c, :, part(i, v)] = value
                        total = total + value
                totals[c] = jnp.sum(total, axis=1, keepdims=True) / math.sqrt(CELLS)
        chunks = []
        for q in range(groups_of_lanes):
            place = lane + q * LANES - 24 * mem - 3 * block_row
            mine = jnp.zeros((8, LANES), F32)
            for c in range(3):
                mine = jnp.where(place == c, totals[c], mine)
            chunks.append(jnp.sum(mine, axis=0, keepdims=True))
        tile = jnp.zeros((8, LANES), F32)
        for q in range(groups_of_lanes):
            tile = jnp.where(block_row == q, chunks[q], tile)
        out_vector[...] = tile

        def send_vector_to(other, to, slot):
            pltpu.make_async_remote_copy(
                src_ref=out_vector,
                dst_ref=in_vector.at[slot, mem],
                send_sem=send_vector.at[slot],
                recv_sem=recv_vector.at[slot],
                device_id={"grp": other, "mem": to},
                device_id_type=MESH,
            ).start()

        for to in peers:
            send_vector_to(above, to, 1)
            send_vector_to(below, to, 2)
            send_vector_to(grp, to, 0)
        send_vector_to(above, mem, 1)
        send_vector_to(below, mem, 2)
        in_vector[0, mem] = tile

        for c in range(3):
            wait_for(in_solver.at[c], recv_solver.at[c])
            in_solver[c, mem] = solver_rows[c]
            near_rows[c] = pick(lift_mat[...], in_solver[c].reshape(wide, n_coarse))
            for side in range(2):
                far_solver(c, side).wait_recv()
                source = in_far_solver[c, side]
                chosen = jnp.zeros((8, n_coarse), F32)
                for b in range(8):
                    wants = far_mat[side][:, b : b + 1]
                    chosen = jnp.where(wants == 1.0, source[b : b + 1], chosen)
                far_rows[c, side] = chosen

        def vector_of(slot):
            whole = in_vector[slot, 0]
            for m in range(1, n_mem):
                whole = whole + in_vector[slot, m]
            return [jnp.broadcast_to(whole[q : q + 1], (8, LANES)) for q in range(groups_of_lanes)]

        def correction(rows, vector):
            product = rows[:, :LANES] * vector[0]
            for q in range(1, groups_of_lanes):
                product = product + rows[:, q * LANES : (q + 1) * LANES] * vector[q]
            return jnp.broadcast_to(jnp.sum(product, axis=1, keepdims=True), (8, LANES))

        for side in range(2):
            wait_for(in_vector.at[1 + side], recv_vector.at[1 + side], n_mem)
        far_vectors = [vector_of(1), vector_of(2)]
        wait_for(in_vector.at[0], recv_vector.at[0])
        vector = vector_of(0)
        def lifted(c):
            mine = correction(solver_rows[c], vector)
            lifts[c] = mine
            gap = [mine - correction(near_rows[c, pl.ds(8 * d, 8), :], vector) for d in range(4)]
            gap_lower, gap_upper = [
                mine - correction(far_rows[c, side], far_vectors[side]) for side in range(2)
            ]
            gap_k = jnp.where(first_k, gap[0], gap[1])

            def new(i):
                result = []
                for v in range(2):
                    change = MASS_TERM * effective[:, part(i, v)] * mine
                    change = change + ghost_k[:, part(i, v)] * gap_k
                    change = change + ghost_j[:, part(i, v)] * gap[2 + v]
                    if i == 0:
                        change = change + weight_i[:, part(0, v)] * gap_lower
                    if i == EDGE - 1:
                        change = change + weight_i[:, part(EDGE, v)] * gap_upper
                    result.append(residual[c, :, part(i, v)] - change)
                return result

            return new

        return lifted

    def advance(g, t, news, keep, gain):
        outgoing, incoming, send_sem, recv_sem, planes = buffers[g][:5]
        group = GROUPS[g]
        columns_out = []
        for l, c in enumerate(group):
            moved = {}

            def step_of(i, v):
                if v == 0:
                    for half, value in enumerate(news[l](i)):
                        if keep is not None or t == DEG:
                            residual[c, :, part(i, half)] = value
                        ahead = gain * (value * inverse[:, part(i, half)])
                        if keep is not None:
                            ahead = keep * step_dir[c, :, part(i, half)] + ahead
                        step_dir[c, :, part(i, half)] = ahead
                        moved[i, half] = ahead
                return moved[i, v]

            found = extract(step_of)
            columns_out.append(
                jnp.concatenate([found[v, d] for v in range(2) for d in range(4)], axis=0)
            )
        packed = columns(pick(pack_mat[...], side_by_side(columns_out)), len(group))
        for l in range(len(group)):
            outgoing[t, :, l] = packed[l].reshape(n_mem, 8, LANES)
        send(outgoing.at[t], incoming.at[t], send_sem.at[t], recv_sem.at[t])
        for l, c in enumerate(group):
            for v in range(2):
                planes[t, 0, l, pl.ds(8 * v, 8), :] = step_dir[c, :, part(EDGE - 1, v)]
                planes[t, 1, l, pl.ds(8 * v, 8), :] = step_dir[c, :, part(0, v)]
        for side in range(2):
            step_plane(g, t, side).start()
        incoming[t, mem] = outgoing[t, mem]

    def send_solver_rows(c):
        for to in peers:
            pltpu.make_async_remote_copy(
                src_ref=solver_rows.at[c],
                dst_ref=in_solver.at[c, mem],
                send_sem=send_solver.at[c],
                recv_sem=recv_solver.at[c],
                device_id={"mem": to},
                device_id_type=MESH,
            ).start()
        for side in range(2):
            far_solver(c, side).start()

    def inside(lift):
        @pl.loop(0, 3)
        def _(c):
            for i in range(EDGE):
                own = [step_dir[c, :, part(i, v)] for v in range(2)]
                back = [turn(x, EDGE) for x in own]
                ahead = [turn(x, -EDGE) for x in own]
                for v in range(2):
                    x = own[v]
                    if v == 0:
                        lower_j, upper_j = back[0], jnp.where(last_row, ahead[1], ahead[0])
                    else:
                        lower_j, upper_j = jnp.where(first_row, back[0], back[1]), ahead[1]
                    change = weight_k[0, :, part(i, v)] * turn(x, 1)
                    change = change + weight_k[1, :, part(i, v)] * turn(x, -1)
                    change = change + weight_j[0, :, part(i, v)] * lower_j
                    change = change + weight_j[1, :, part(i, v)] * upper_j
                    if i > 0:
                        change = change + weight_i[:, part(i, v)] * step_dir[c, :, part(i - 1, v)]
                    if i < EDGE - 1:
                        change = change + weight_i[:, part(i + 1, v)] * step_dir[
                            c, :, part(i + 1, v)
                        ]
                    residual[c, :, part(i, v)] = residual[c, :, part(i, v)] - (
                        diagonal[:, part(i, v)] * x - change
                    )
                    if lift:
                        x = x + lifts[c]
                    velocity[c, :, part(i, v)] = velocity[c, :, part(i, v)] + x

    def as_is(c):
        return lambda i: [residual[c, :, part(i, v)] for v in range(2)]

    def later(first):
        def sweep(t, carry):
            keep = by_step(t - first, [value for value, _ in steps])
            gain = by_step(t - first, [value for _, value in steps])
            for g, group in enumerate(GROUPS):
                news = [
                    across_faces(c, *arrived) for c, arrived in zip(group, receive(g, t - 1))
                ]
                advance(g, t, news, keep, gain)
            if first == 0:
                send_solver_rows(t)
            inside(False)
            return carry

        lax.fori_loop(first + 1, first + DEG, sweep, 0)

    for g, group in enumerate(GROUPS):
        advance(g, 0, [as_is(c) for c in group], None, jnp.float32(steps[0][1]))
    send_solver_rows(0)
    inside(False)
    later(0)
    lifted = coarse_level()
    for g, group in enumerate(GROUPS):
        advance(g, DEG, [lifted(c) for c in group], None, jnp.float32(steps[0][1]))
    inside(True)
    later(DEG)
    store(0).start()
    for g, group in enumerate(GROUPS):
        for c, arrived in zip(group, receive(g, SWEEPS - 1)):
            new = across_faces(c, *arrived)
            for i in range(EDGE):
                for v, value in enumerate(new(i)):
                    residual[c, :, part(i, v)] = value

    store(1).start()
    wait_for(in_face, send_face)
    for g in range(len(GROUPS)):
        for t in range(SWEEPS):
            wait_for(buffers[g][0].at[t], buffers[g][2].at[t])
            for side in range(2):
                step_plane(g, t, side).wait_send()
    for t in range(DEG):
        wait_for(in_solver.at[t], send_solver.at[t])
        for side in range(2):
            far_solver(t, side).wait_send()
    wait_for(in_vector.at[0], send_vector.at[0])
    for side in range(2):
        wait_for(in_vector.at[1 + side], send_vector.at[1 + side], n_mem)
    wait_for(out_request, send_request)
    for side in range(2):
        effective_plane(side).wait_send()
    for place in range(2):
        store(place).wait()


def group_scratch(n_mem):
    shapes = []
    for group in GROUPS:
        near = pltpu.VMEM((SWEEPS, n_mem, len(group), 8, LANES), F32)
        far = pltpu.VMEM((SWEEPS, 2, len(group), 16, LANES), F32)
        dma = pltpu.SemaphoreType.DMA
        shapes += [near, near, dma((SWEEPS,)), dma((SWEEPS,))]
        shapes += [far, far, dma((SWEEPS, 2)), dma((SWEEPS, 2))]
    return shapes


def solution(mesh):
    n_grp, n_mem = mesh.shape["grp"], mesh.shape["mem"]
    wide = n_mem * 8

    def local(
        forcing,
        viscosity,
        refinement,
        face_owner,
        face_block,
        plane_block,
        hanging,
        coarse_solver,
    ):
        field = pltpu.VMEM((8, CELLS), F32)
        hbm = pl.BlockSpec(memory_space=pltpu.HBM)
        dma = pltpu.SemaphoreType.DMA
        both = pl.pallas_call(
            functools.partial(kernel, n_grp, n_mem),
            out_shape=jax.ShapeDtypeStruct((2, *forcing.shape), F32),
            in_specs=[hbm] * 8,
            out_specs=hbm,
            scratch_shapes=[
                pltpu.VMEM((1, 8), jnp.int32),
                pltpu.VMEM((1, 32), jnp.int32),
                pltpu.VMEM((4, 8), jnp.int32),
                pltpu.VMEM((2, 8), jnp.int32),
                pltpu.VMEM((8, 6), jnp.int32),
                pltpu.SMEM((1, 32), jnp.int32),
                pltpu.SMEM((4, 8), jnp.int32),
                pltpu.VMEM((3, 8, CELLS), F32),
                pltpu.VMEM((3, 8, CELLS), F32),
                field,
                pltpu.VMEM((24, n_mem * 24), F32),
                pltpu.VMEM((2, 8, CELLS), F32),
                pltpu.VMEM((2, 8, CELLS), F32),
                pltpu.VMEM((8, CELLS + FACE), F32),
                field,
                field,
                field,
                field,
                pltpu.VMEM((3, 8, CELLS), F32),
                pltpu.VMEM((64, LANES), F32),
                pltpu.VMEM((3, 8, LANES), F32),
                pltpu.VMEM((32, LANES), F32),
                pltpu.VMEM((32, LANES), F32),
                pltpu.VMEM((64, 3 * wide), BF16),
                pltpu.VMEM((wide, 192), BF16),
                pltpu.VMEM((32, 96), BF16),
                pltpu.VMEM((32, 3 * wide), BF16),
                pltpu.VMEM((2, 8, 8), F32),
                pltpu.VMEM((3, 8, n_mem * 24), F32),
                pltpu.VMEM((3, n_mem, 8, n_mem * 24), F32),
                pltpu.VMEM((3, 2, 8, n_mem * 24), F32),
                pltpu.VMEM((3, 32, n_mem * 24), F32),
                pltpu.VMEM((3, 2, 8, n_mem * 24), F32),
                pltpu.VMEM((8, LANES), F32),
                pltpu.VMEM((3, n_mem, 8, LANES), F32),
                pltpu.VMEM((64, LANES), F32),
                pltpu.VMEM((n_mem, 64, LANES), F32),
                pltpu.VMEM((n_mem, 8, LANES), F32),
                pltpu.VMEM((n_mem, 8, LANES), F32),
                pltpu.VMEM((2, 16, LANES), F32),
                pltpu.VMEM((2, 16, LANES), F32),
                dma,
                dma,
                dma((2,)),
                dma((2,)),
                dma,
                dma,
                dma((DEG,)),
                dma((DEG,)),
                dma((DEG, 2)),
                dma((DEG, 2)),
                dma((3,)),
                dma((3,)),
                dma((10,)),
                dma((2,)),
                *group_scratch(n_mem),
            ],
            compiler_params=pltpu.CompilerParams(
                collective_id=0, has_side_effects=True, vmem_limit_bytes=56 * 1024 * 1024
            ),
            name="vcycle",
        )(
            forcing,
            viscosity,
            coarse_solver,
            refinement.reshape(1, 8),
            face_owner.reshape(1, 32),
            face_block.T,
            plane_block.T,
            hanging,
        )
        return both[0], both[1]

    in_specs = (
        P(None, ("grp", "mem"), None),
        P(("grp", "mem"), None),
        P(("grp", "mem")),
        P(("grp", "mem"), None),
        P(("grp", "mem"), None),
        P(("grp", "mem"), None),
        P(("grp", "mem"), None),
        P("grp", "mem", None),
    )
    out_specs = (P(None, ("grp", "mem"), None), P(None, ("grp", "mem"), None))
    return jax.shard_map(local, mesh=mesh, in_specs=in_specs, out_specs=out_specs, check_vma=False)
```

```python
import functools
import math

import jax
import jax.numpy as jnp
from jax import lax
from jax.experimental import pallas as pl
from jax.experimental.pallas import tpu as pltpu
from jax.sharding import PartitionSpec as P

MESH = pl.DeviceIdType.MESH
EDGE = 16
DEG = 3
CELLS = 4096
FACE = 256
LANES = 128
CAP = 4
MASS_TERM = 1.0
LOWER_BOUND = 0.25
UPPER_BOUND = 2.0
SWEEPS = 2 * DEG
GROUPS = ((0,), (1, 2))
F32 = jnp.float32
BF16 = jnp.bfloat16


def chebyshev():
    theta = 0.5 * (UPPER_BOUND + LOWER_BOUND)
    delta = 0.5 * (UPPER_BOUND - LOWER_BOUND)
    sigma = theta / delta
    rho = 1.0 / sigma
    steps = [(0.0, 1.0 / theta)]
    for _ in range(DEG - 1):
        rho_next = 1.0 / (2.0 * sigma - rho)
        steps.append((rho_next * rho, 2.0 * rho_next / delta))
        rho = rho_next
    return steps


def far_first(members):
    tall = members // 4

    def hops(offset):
        dy, dx = offset
        return min(dy, tall - dy) + min(dx, 4 - dx)

    others = [(dy, dx) for dy in range(tall) for dx in range(4) if (dy, dx) != (0, 0)]
    return sorted(others, key=hops, reverse=True)


def by_step(step, values):
    result = jnp.float32(values[-1])
    for place in range(len(values) - 2, -1, -1):
        result = jnp.where(step == place, jnp.float32(values[place]), result)
    return result


def iota(shape, dim):
    return lax.broadcasted_iota(jnp.int32, shape, dim)


def turn(x, shift):
    shift = shift % LANES
    return x if shift == 0 else pltpu.roll(x, shift, 1)


def part(i, v):
    return pl.ds(i * FACE + v * LANES, LANES)


def parts(values):
    high = values.astype(BF16)
    rest = values - high.astype(F32)
    middle = rest.astype(BF16)
    low = (rest - middle.astype(F32)).astype(BF16)
    return jnp.concatenate([high, middle, low], axis=0)


def thrice(one_hot):
    return jnp.concatenate([one_hot] * 3, axis=1)


def pick(one_hot_thrice, values):
    return jnp.dot(one_hot_thrice, parts(values), preferred_element_type=F32)


def coarsen(x, start):
    lane = (iota(x.shape, 1) + (LANES - start)) % LANES
    x = x + jnp.where(lane % 2 == 0, turn(x, -1), turn(x, 1))
    x = x + jnp.where(lane // EDGE % 2 == 0, turn(x, -EDGE), turn(x, EDGE))
    return 0.25 * x


def extract(read):
    lane = iota((8, LANES), 1)
    in_row, row = lane % EDGE, lane // EDGE
    zero = jnp.zeros((8, LANES), F32)
    faces = {(v, d): zero for v in range(2) for d in range(4)}
    for i in range(EDGE):
        halves = (read(i, 0), read(i, 1))
        for v in range(2):
            moved = turn(halves[v], i)
            faces[v, 0] = jnp.where(in_row == i, moved, faces[v, 0])
            faces[v, 1] = jnp.where(in_row == (i - 1) % EDGE, moved, faces[v, 1])
        v = i // 8
        moved = turn(jnp.where(lane < EDGE, halves[0], halves[1]), i % 8 * EDGE)
        faces[v, 2] = jnp.where(row == i % 8, moved, faces[v, 2])
        faces[v, 3] = jnp.where(row == (i - 1) % 8, moved, faces[v, 3])
    for v in range(2):
        faces[v, 3] = turn(faces[v, 3], EDGE)
    return faces


def tables(owner, face_block, plane_block, hanging, members, has_lower, has_upper):
    wide = members * 8
    rows, columns = iota((32, 32), 0), iota((32, 32), 1)
    given = 4 * (rows % 8) + rows // 8
    given_t = 4 * (columns % 8) + columns // 8
    owner_col = jnp.sum(jnp.where(columns == given, owner, 0), axis=1, keepdims=True)
    own_col = jnp.sum(jnp.where(rows == columns, owner, 0), axis=1, keepdims=True)
    owner_row = jnp.sum(jnp.where(rows == given_t, own_col, 0), axis=0, keepdims=True)
    same = owner_col == owner_row
    rank_col = jnp.sum(jnp.where(same & (columns < rows), 1, 0), axis=1, keepdims=True)
    rank_row = jnp.sum(jnp.where(same & (rows < columns), 1, 0), axis=0, keepdims=True)

    def spread(table, first, of_row):
        tall = jnp.concatenate([table] * 4, axis=0)
        mask = iota(tall.shape, 1) == first + of_row(iota(tall.shape, 0))
        return jnp.sum(jnp.where(mask, tall, 0), axis=1, keepdims=True)

    def spread_t(table, per):
        lanes, which = iota((32, 8), 1), iota((32, 8), 0)
        tall = jnp.zeros((32, 8), jnp.int32)
        for d in range(table.shape[0]):
            tall = jnp.where(which // per == d, table[d : d + 1], tall)
        return jnp.sum(jnp.where(lanes == which % 8, tall, 0), axis=1, keepdims=True)

    block_col = spread_t(face_block, 8)
    side = iota((32, 1), 0) // 8
    wanted = (side + 1 - 2 * (side % 2)) * 8 + block_col
    slot_col = owner_col * 8 + rank_col
    slot_row = owner_row * 8 + rank_row

    def ones(mask):
        return jnp.where(mask, 1.0, 0.0).astype(BF16)

    lanes = iota((32, wide), 1)
    unpack = jnp.concatenate([ones(lanes == slot_col + CAP * v) for v in range(2)], axis=0)
    slots = iota((wide, 32), 0)
    unpack_t = jnp.concatenate([ones(slots == slot_row + CAP * v) for v in range(2)], axis=1)
    lanes = iota((32, LANES), 1)
    source = jnp.concatenate([ones(lanes % 64 == wanted + 32 * v) for v in range(2)], axis=0)
    request = jnp.dot(unpack_t, source, preferred_element_type=F32)
    plane_col = spread_t(plane_block, 16)
    which = iota((32, 32), 0) // 16
    inside = jnp.where(which == 0, has_lower, has_upper) == 1
    plane_pick = ones((columns == rows // 8 * 8 + plane_col) & inside)
    lanes, which = iota((8, 8), 1), iota((8, 8), 0)
    far_pick = []
    for d, exists in enumerate((has_lower, has_upper)):
        chosen = plane_block[d : d + 1]
        chosen = jnp.sum(jnp.where(lanes == which, chosen, 0), axis=1, keepdims=True)
        far_pick.append(jnp.where((lanes == chosen) & (exists == 1), 1.0, 0.0))
    lift_pick = ones(iota((32, wide), 1) == owner_col * 8 + block_col)
    near_hang = spread(hanging, 0, lambda r: r // 8)
    plane_hang = spread(hanging, 4, lambda r: r // 16)
    near_hang = jnp.broadcast_to(near_hang.astype(F32), (32, LANES))
    plane_hang = jnp.broadcast_to(plane_hang.astype(F32), (32, LANES))
    return (
        thrice(unpack),
        request,
        thrice(plane_pick),
        thrice(lift_pick),
        far_pick,
        near_hang,
        plane_hang,
    )


def kernel(
    n_grp,
    n_mem,
    forcing_hbm,
    viscosity_hbm,
    solver_hbm,
    refinement_hbm,
    owner_hbm,
    block_hbm,
    plane_hbm,
    hanging_hbm,
    result,
    refinement,
    face_owner,
    face_block,
    plane_block,
    hanging,
    owner_scalar,
    block_scalar,
    velocity,
    residual,
    effective,
    solver,
    weight_k,
    weight_j,
    weight_i,
    ghost_k,
    ghost_j,
    diagonal,
    inverse,
    step_dir,
    ghosts,
    lifts,
    hang_near,
    hang_plane,
    unpack_mat,
    pack_mat,
    plane_mat,
    lift_mat,
    far_mat,
    solver_rows,
    in_solver,
    in_far_solver,
    near_rows,
    far_rows,
    out_vector,
    in_vector,
    out_face,
    in_face,
    out_request,
    in_request,
    out_plane,
    in_plane,
    send_request,
    recv_request,
    send_plane,
    recv_plane,
    send_face,
    recv_face,
    send_solver,
    recv_solver,
    send_far,
    recv_far,
    send_vector,
    recv_vector,
    load_sem,
    store_sem,
    *group_refs,
):
    grp, mem = lax.axis_index("grp"), lax.axis_index("mem")
    above = lax.rem(grp + 1, n_grp)
    below = lax.rem(grp + n_grp - 1, n_grp)
    n_coarse = n_mem * 24
    buffers = [group_refs[8 * g : 8 * g + 8] for g in range(len(GROUPS))]
    groups_of_lanes = n_coarse // LANES
    wide = n_mem * 8

    mem_y, mem_x = lax.div(mem, 4), lax.rem(mem, 4)
    peers = [
        lax.rem(mem_y + dy, n_mem // 4) * 4 + lax.rem(mem_x + dx, 4) for dy, dx in far_first(n_mem)
    ]
    barrier = pltpu.get_barrier_semaphore()
    for to in peers:
        pl.semaphore_signal(barrier, inc=1, device_id={"mem": to}, device_id_type=MESH)
    for other in (above, below):
        pl.semaphore_signal(barrier, inc=1, device_id={"grp": other}, device_id_type=MESH)

    loads = [
        pltpu.make_async_copy(viscosity_hbm, effective, load_sem.at[0]),
        pltpu.make_async_copy(forcing_hbm, residual, load_sem.at[1]),
        pltpu.make_async_copy(solver_hbm.at[0], solver, load_sem.at[2]),
    ]
    small = [
        (refinement_hbm, refinement),
        (owner_hbm, face_owner),
        (block_hbm, face_block),
        (plane_hbm, plane_block),
        (hanging_hbm, hanging),
        (owner_hbm, owner_scalar),
        (block_hbm, block_scalar),
    ]
    small = [
        pltpu.make_async_copy(source, target, load_sem.at[3 + place])
        for place, (source, target) in enumerate(small)
    ]
    for load in [*small, *loads]:
        load.start()

    def store(place, c):
        source = (velocity, residual)[place]
        return pltpu.make_async_copy(
            source.at[c], result.at[place, c], store_sem.at[place, c]
        )

    lane = iota((8, LANES), 1)
    in_row = lane % EDGE
    row = lane // EDGE
    first_k, last_k = in_row == 0, in_row == EDGE - 1
    first_row, last_row = lane < EDGE, lane >= LANES - EDGE

    def send(outgoing, incoming, send_sem, recv_sem):
        for to in peers:
            pltpu.make_async_remote_copy(
                src_ref=outgoing.at[to],
                dst_ref=incoming.at[mem],
                send_sem=send_sem,
                recv_sem=recv_sem,
                device_id={"mem": to},
                device_id_type=MESH,
            ).start()

    def wait_for(buffer, sem, count=n_mem - 1):
        span = buffer.at[pl.ds(0, count)]
        pltpu.make_async_copy(span, span, sem).wait()

    def plane_copy(side, outgoing, incoming, send_sem, recv_sem):
        return pltpu.make_async_remote_copy(
            src_ref=outgoing.at[side],
            dst_ref=incoming.at[side],
            send_sem=send_sem.at[side],
            recv_sem=recv_sem.at[side],
            device_id={"grp": above if side == 0 else below},
            device_id_type=MESH,
        )

    def effective_plane(side):
        return plane_copy(side, out_plane, in_plane, send_plane, recv_plane)

    def step_plane(g, t, side):
        return plane_copy(side, *[ref.at[t] for ref in buffers[g][4:]])

    def far_solver(c, side):
        return pltpu.make_async_remote_copy(
            src_ref=solver_rows.at[c],
            dst_ref=in_far_solver.at[c, side],
            send_sem=send_far.at[c, side],
            recv_sem=recv_far.at[c, side],
            device_id={"grp": above if side == 0 else below},
            device_id_type=MESH,
        )

    for load in small:
        load.wait()

    block_row = iota((8, LANES), 0)
    level = jnp.sum(
        jnp.where(iota((8, 8), 0) == iota((8, 8), 1), refinement[...], 0), axis=1, keepdims=True
    )
    level = jnp.broadcast_to(level, (8, LANES))
    scale = 1.0 / jnp.left_shift(jnp.ones_like(level), level).astype(F32)
    loads[0].wait()
    for i in range(EDGE):
        for v in range(2):
            effective[:, part(i, v)] = effective[:, part(i, v)] * scale

    found = extract(lambda i, v: effective[:, part(i, v)])
    for (v, d), register in found.items():
        out_face[pl.ds(v * 32 + d * 8, 8), :] = register

    unpack, request, plane_pick, lift_pick, far_pick, near_hang, plane_hang = tables(
        face_owner[...],
        face_block[...],
        plane_block[...],
        hanging[...],
        n_mem,
        jnp.where(grp > 0, 1, 0),
        jnp.where(grp < n_grp - 1, 1, 0),
    )
    unpack_mat[...] = unpack
    plane_mat[...] = plane_pick
    lift_mat[...] = lift_pick
    for side in range(2):
        far_mat[side] = far_pick[side]
    hang_near[...] = near_hang
    hang_plane[...] = plane_hang
    out_request[...] = request.reshape(n_mem, 8, LANES)

    pl.semaphore_wait(barrier, n_mem - 1 + 2)

    send(out_request, in_request, send_request, recv_request)
    for to in peers:
        pltpu.make_async_remote_copy(
            src_ref=out_face,
            dst_ref=in_face.at[mem],
            send_sem=send_face,
            recv_sem=recv_face,
            device_id={"mem": to},
            device_id_type=MESH,
        ).start()
    for v in range(2):
        out_plane[0, pl.ds(8 * v, 8), :] = effective[:, part(EDGE - 1, v)]
        out_plane[1, pl.ds(8 * v, 8), :] = effective[:, part(0, v)]
    for side in range(2):
        effective_plane(side).start()
    in_face[mem] = out_face[...]
    in_request[mem] = out_request[mem]

    loads[1].wait()
    loads[2].wait()
    rows, columns = iota((24, 24), 0), iota((24, 24), 1)
    reorder = jnp.where(columns == 3 * (rows % 8) + rows // 8, 1.0, 0.0).astype(BF16)
    ordered = pick(thrice(reorder), solver[...])
    for c in range(3):
        solver_rows[c] = ordered[8 * c : 8 * c + 8]
    for c in range(3):
        for i in range(EDGE):
            for v in range(2):
                velocity[c, :, part(i, v)] = jnp.zeros((8, LANES), F32)
    for i in range(EDGE):
        own = [effective[:, part(i, v)] for v in range(2)]
        back = [turn(x, EDGE) for x in own]
        ahead = [turn(x, -EDGE) for x in own]
        for v in range(2):
            x = own[v]
            lower_k = jnp.where(first_k, 0.0, 0.5 * (x + turn(x, 1)))
            upper_k = jnp.where(last_k, 0.0, 0.5 * (x + turn(x, -1)))
            if v == 0:
                lower_j = jnp.where(first_row, 0.0, 0.5 * (x + back[0]))
                upper_j = 0.5 * (x + jnp.where(last_row, ahead[1], ahead[0]))
            else:
                lower_j = 0.5 * (x + jnp.where(first_row, back[0], back[1]))
                upper_j = jnp.where(last_row, 0.0, 0.5 * (x + ahead[1]))
            weight_k[0, :, part(i, v)] = lower_k
            weight_k[1, :, part(i, v)] = upper_k
            weight_j[0, :, part(i, v)] = lower_j
            weight_j[1, :, part(i, v)] = upper_j
            if i > 0:
                weight_i[:, part(i, v)] = 0.5 * (x + effective[:, part(i - 1, v)])
            diagonal[:, part(i, v)] = MASS_TERM * x + lower_k + upper_k + lower_j + upper_j

    def settle(values, hang, start=0):
        return jnp.where(hang == 1.0, coarsen(values, start), values)

    first_side = jnp.where(iota((32, LANES), 0) < 8, EDGE - 1, 0)

    def side_by_side(pieces):
        return pieces[0] if len(pieces) == 1 else jnp.concatenate(pieces, axis=1)

    def columns(values, count):
        return [values[:, l * LANES : (l + 1) * LANES] for l in range(count)]

    def receive(g, t):
        count = len(GROUPS[g])
        incoming, recv_sem, planes = buffers[g][1], buffers[g][3], buffers[g][5]
        for side in range(2):
            step_plane(g, t, side).wait_recv()
        far = pick(
            plane_mat[...],
            side_by_side([planes[t, :, l].reshape(32, LANES) for l in range(count)]),
        )
        far = [settle(values, hang_plane[...]) for values in columns(far, count)]
        wait_for(incoming.at[t], recv_sem.at[t])
        near = pick(
            unpack_mat[...],
            side_by_side([incoming[t, :, l].reshape(wide, LANES) for l in range(count)]),
        )
        result = []
        for l, values in enumerate(columns(near, count)):
            halves = [settle(values[32 * v : 32 * v + 32], hang_near[...], first_side) for v in range(2)]
            result.append(
                (
                    {(d, v): halves[v][8 * d : 8 * d + 8] for d in range(4) for v in range(2)},
                    {
                        (side, v): far[l][16 * side + 8 * v : 16 * side + 8 * v + 8]
                        for side in range(2)
                        for v in range(2)
                    },
                )
            )
        return result

    def near_ghosts(near):
        lower_k = [turn(near[0, v], -2 * (EDGE - 1)) for v in range(2)]
        upper_k = [near[1, v] for v in range(2)]
        lower_j = [near[2, v] for v in range(2)]
        upper_j = [turn(near[3, v], LANES - EDGE) for v in range(2)]

        def at_k(i, v):
            return turn(jnp.where(in_row == i, upper_k[v], lower_k[v]), EDGE - 1 - i)

        def at_j(i):
            both = jnp.where(row == i % 8, lower_j[i // 8], upper_j[i // 8])
            return turn(both, -(i % 8) * EDGE)

        return at_k, at_j

    for side in range(2):
        effective_plane(side).wait_recv()
    far = settle(pick(plane_mat[...], in_plane[...].reshape(32, LANES)), hang_plane[...])
    for v in range(2):
        weight_i[:, part(0, v)] = 0.5 * (effective[:, part(0, v)] + far[8 * v : 8 * v + 8])
        weight_i[:, part(EDGE, v)] = 0.5 * (
            effective[:, part(EDGE - 1, v)] + far[16 + 8 * v : 24 + 8 * v]
        )
    wait_for(in_face, recv_face)
    for d in range(4):
        for b in range(8):
            owner = owner_scalar[0, 4 * b + d]
            wanted = (d + 1 - 2 * (d % 2)) * 8 + block_scalar[d, b]
            for v in range(2):
                ghosts[pl.ds(v * 32 + d * 8 + b, 1), :] = in_face[
                    owner, pl.ds(v * 32 + wanted, 1), :
                ]
    halves = [settle(ghosts[pl.ds(32 * v, 32), :], hang_near[...], first_side) for v in range(2)]
    k_ghost, j_ghost = near_ghosts(
        {(d, v): halves[v][8 * d : 8 * d + 8] for d in range(4) for v in range(2)}
    )
    for i in range(EDGE):
        beside_j = j_ghost(i)
        for v in range(2):
            x = effective[:, part(i, v)]
            at_k = jnp.where(first_k | last_k, 0.5 * (x + k_ghost(i, v)), 0.0)
            edge = first_row if v == 0 else last_row
            at_j = jnp.where(edge, 0.5 * (x + beside_j), 0.0)
            ghost_k[:, part(i, v)] = at_k
            ghost_j[:, part(i, v)] = at_j
            whole = (
                diagonal[:, part(i, v)]
                + (weight_i[:, part(i, v)] + weight_i[:, part(i + 1, v)])
                + (at_k + at_j)
            )
            diagonal[:, part(i, v)] = whole
            inverse[:, part(i, v)] = 1.0 / whole

    steps = chebyshev()
    wait_for(in_request, recv_request)
    request = in_request[...].reshape(wide, LANES)
    pack_mat[...] = jnp.concatenate([request, request[:, :64]], axis=1).astype(BF16)

    def across_faces(c, near, far):
        k_ghost, j_ghost = near_ghosts(near)

        def new(i):
            beside_j = j_ghost(i)
            result = []
            for v in range(2):
                change = ghost_k[:, part(i, v)] * k_ghost(i, v)
                change = change + ghost_j[:, part(i, v)] * beside_j
                if i == 0:
                    change = change + weight_i[:, part(0, v)] * far[0, v]
                if i == EDGE - 1:
                    change = change + weight_i[:, part(EDGE, v)] * far[1, v]
                result.append(residual[c, :, part(i, v)] + change)
            return result

        return new

    def coarse_level():
        totals = [None] * 3
        for g, group in enumerate(GROUPS):
            for c, arrived in zip(group, receive(g, DEG - 1)):
                total = jnp.zeros((8, LANES), F32)
                new = across_faces(c, *arrived)
                for i in range(EDGE):
                    for v, value in enumerate(new(i)):
                        residual[c, :, part(i, v)] = value
                        total = total + value
                totals[c] = jnp.sum(total, axis=1, keepdims=True) / math.sqrt(CELLS)
        chunks = []
        for q in range(groups_of_lanes):
            place = lane + q * LANES - 24 * mem - 3 * block_row
            mine = jnp.zeros((8, LANES), F32)
            for c in range(3):
                mine = jnp.where(place == c, totals[c], mine)
            chunks.append(jnp.sum(mine, axis=0, keepdims=True))
        tile = jnp.zeros((8, LANES), F32)
        for q in range(groups_of_lanes):
            tile = jnp.where(block_row == q, chunks[q], tile)
        out_vector[...] = tile

        def send_vector_to(other, to, slot):
            pltpu.make_async_remote_copy(
                src_ref=out_vector,
                dst_ref=in_vector.at[slot, mem],
                send_sem=send_vector.at[slot],
                recv_sem=recv_vector.at[slot],
                device_id={"grp": other, "mem": to},
                device_id_type=MESH,
            ).start()

        for to in peers:
            send_vector_to(above, to, 1)
            send_vector_to(below, to, 2)
            send_vector_to(grp, to, 0)
        send_vector_to(above, mem, 1)
        send_vector_to(below, mem, 2)
        in_vector[0, mem] = tile

        for c in range(3):
            wait_for(in_solver.at[c], recv_solver.at[c])
            in_solver[c, mem] = solver_rows[c]
            near_rows[c] = pick(lift_mat[...], in_solver[c].reshape(wide, n_coarse))
            for side in range(2):
                far_solver(c, side).wait_recv()
                source = in_far_solver[c, side]
                chosen = jnp.zeros((8, n_coarse), F32)
                for b in range(8):
                    wants = far_mat[side][:, b : b + 1]
                    chosen = jnp.where(wants == 1.0, source[b : b + 1], chosen)
                far_rows[c, side] = chosen

        def vector_of(slot):
            whole = in_vector[slot, 0]
            for m in range(1, n_mem):
                whole = whole + in_vector[slot, m]
            return [jnp.broadcast_to(whole[q : q + 1], (8, LANES)) for q in range(groups_of_lanes)]

        def correction(rows, vector):
            product = rows[:, :LANES] * vector[0]
            for q in range(1, groups_of_lanes):
                product = product + rows[:, q * LANES : (q + 1) * LANES] * vector[q]
            return jnp.broadcast_to(jnp.sum(product, axis=1, keepdims=True), (8, LANES))

        for side in range(2):
            wait_for(in_vector.at[1 + side], recv_vector.at[1 + side], n_mem)
        far_vectors = [vector_of(1), vector_of(2)]
        wait_for(in_vector.at[0], recv_vector.at[0])
        vector = vector_of(0)
        def lifted(c):
            mine = correction(solver_rows[c], vector)
            lifts[c] = mine
            gap = [mine - correction(near_rows[c, pl.ds(8 * d, 8), :], vector) for d in range(4)]
            gap_lower, gap_upper = [
                mine - correction(far_rows[c, side], far_vectors[side]) for side in range(2)
            ]
            gap_k = jnp.where(first_k, gap[0], gap[1])

            def new(i):
                result = []
                for v in range(2):
                    change = MASS_TERM * effective[:, part(i, v)] * mine
                    change = change + ghost_k[:, part(i, v)] * gap_k
                    change = change + ghost_j[:, part(i, v)] * gap[2 + v]
                    if i == 0:
                        change = change + weight_i[:, part(0, v)] * gap_lower
                    if i == EDGE - 1:
                        change = change + weight_i[:, part(EDGE, v)] * gap_upper
                    result.append(residual[c, :, part(i, v)] - change)
                return result

            return new

        return lifted

    def advance(g, t, news, keep, gain):
        outgoing, incoming, send_sem, recv_sem, planes = buffers[g][:5]
        group = GROUPS[g]
        columns_out = []
        for l, c in enumerate(group):
            moved = {}

            def step_of(i, v):
                if v == 0:
                    for half, value in enumerate(news[l](i)):
                        if keep is not None or t == DEG:
                            residual[c, :, part(i, half)] = value
                        ahead = gain * (value * inverse[:, part(i, half)])
                        if keep is not None:
                            ahead = keep * step_dir[c, :, part(i, half)] + ahead
                        step_dir[c, :, part(i, half)] = ahead
                        moved[i, half] = ahead
                return moved[i, v]

            found = extract(step_of)
            columns_out.append(
                jnp.concatenate([found[v, d] for v in range(2) for d in range(4)], axis=0)
            )
        packed = columns(pick(pack_mat[...], side_by_side(columns_out)), len(group))
        for l in range(len(group)):
            outgoing[t, :, l] = packed[l].reshape(n_mem, 8, LANES)
        send(outgoing.at[t], incoming.at[t], send_sem.at[t], recv_sem.at[t])
        for l, c in enumerate(group):
            for v in range(2):
                planes[t, 0, l, pl.ds(8 * v, 8), :] = step_dir[c, :, part(EDGE - 1, v)]
                planes[t, 1, l, pl.ds(8 * v, 8), :] = step_dir[c, :, part(0, v)]
        for side in range(2):
            step_plane(g, t, side).start()
        incoming[t, mem] = outgoing[t, mem]

    def send_solver_rows(c):
        for to in peers:
            pltpu.make_async_remote_copy(
                src_ref=solver_rows.at[c],
                dst_ref=in_solver.at[c, mem],
                send_sem=send_solver.at[c],
                recv_sem=recv_solver.at[c],
                device_id={"mem": to},
                device_id_type=MESH,
            ).start()
        for side in range(2):
            far_solver(c, side).start()

    def inside(lift):
        @pl.loop(0, 3)
        def _(c):
            for i in range(EDGE):
                own = [step_dir[c, :, part(i, v)] for v in range(2)]
                back = [turn(x, EDGE) for x in own]
                ahead = [turn(x, -EDGE) for x in own]
                for v in range(2):
                    x = own[v]
                    if v == 0:
                        lower_j, upper_j = back[0], jnp.where(last_row, ahead[1], ahead[0])
                    else:
                        lower_j, upper_j = jnp.where(first_row, back[0], back[1]), ahead[1]
                    change = weight_k[0, :, part(i, v)] * turn(x, 1)
                    change = change + weight_k[1, :, part(i, v)] * turn(x, -1)
                    change = change + weight_j[0, :, part(i, v)] * lower_j
                    change = change + weight_j[1, :, part(i, v)] * upper_j
                    if i > 0:
                        change = change + weight_i[:, part(i, v)] * step_dir[c, :, part(i - 1, v)]
                    if i < EDGE - 1:
                        change = change + weight_i[:, part(i + 1, v)] * step_dir[
                            c, :, part(i + 1, v)
                        ]
                    residual[c, :, part(i, v)] = residual[c, :, part(i, v)] - (
                        diagonal[:, part(i, v)] * x - change
                    )
                    if lift:
                        x = x + lifts[c]
                    velocity[c, :, part(i, v)] = velocity[c, :, part(i, v)] + x

    def as_is(c):
        return lambda i: [residual[c, :, part(i, v)] for v in range(2)]

    def later(first):
        def sweep(t, carry):
            keep = by_step(t - first, [value for value, _ in steps])
            gain = by_step(t - first, [value for _, value in steps])
            for g, group in enumerate(GROUPS):
                news = [
                    across_faces(c, *arrived) for c, arrived in zip(group, receive(g, t - 1))
                ]
                advance(g, t, news, keep, gain)
            inside(False)
            if first == 0:
                send_solver_rows(t)
            return carry

        lax.fori_loop(first + 1, first + DEG, sweep, 0)

    for g, group in enumerate(GROUPS):
        advance(g, 0, [as_is(c) for c in group], None, jnp.float32(steps[0][1]))
    inside(False)
    send_solver_rows(0)
    later(0)
    lifted = coarse_level()
    for g, group in enumerate(GROUPS):
        advance(g, DEG, [lifted(c) for c in group], None, jnp.float32(steps[0][1]))
    inside(True)
    later(DEG)
    for c in range(3):
        store(0, c).start()
    for g, group in enumerate(GROUPS):
        for c, arrived in zip(group, receive(g, SWEEPS - 1)):
            new = across_faces(c, *arrived)
            for i in range(EDGE):
                for v, value in enumerate(new(i)):
                    residual[c, :, part(i, v)] = value
            store(1, c).start()

    wait_for(in_face, send_face)
    for g in range(len(GROUPS)):
        for t in range(SWEEPS):
            wait_for(buffers[g][0].at[t], buffers[g][2].at[t])
            for side in range(2):
                step_plane(g, t, side).wait_send()
    for t in range(DEG):
        wait_for(in_solver.at[t], send_solver.at[t])
        for side in range(2):
            far_solver(t, side).wait_send()
    wait_for(in_vector.at[0], send_vector.at[0])
    for side in range(2):
        wait_for(in_vector.at[1 + side], send_vector.at[1 + side], n_mem)
    wait_for(out_request, send_request)
    for side in range(2):
        effective_plane(side).wait_send()
    for place in range(2):
        for c in range(3):
            store(place, c).wait()


def group_scratch(n_mem):
    shapes = []
    for group in GROUPS:
        near = pltpu.VMEM((SWEEPS, n_mem, len(group), 8, LANES), F32)
        far = pltpu.VMEM((SWEEPS, 2, len(group), 16, LANES), F32)
        dma = pltpu.SemaphoreType.DMA
        shapes += [near, near, dma((SWEEPS,)), dma((SWEEPS,))]
        shapes += [far, far, dma((SWEEPS, 2)), dma((SWEEPS, 2))]
    return shapes


def solution(mesh):
    n_grp, n_mem = mesh.shape["grp"], mesh.shape["mem"]
    wide = n_mem * 8

    def local(
        forcing,
        viscosity,
        refinement,
        face_owner,
        face_block,
        plane_block,
        hanging,
        coarse_solver,
    ):
        field = pltpu.VMEM((8, CELLS), F32)
        hbm = pl.BlockSpec(memory_space=pltpu.HBM)
        dma = pltpu.SemaphoreType.DMA
        both = pl.pallas_call(
            functools.partial(kernel, n_grp, n_mem),
            out_shape=jax.ShapeDtypeStruct((2, *forcing.shape), F32),
            in_specs=[hbm] * 8,
            out_specs=hbm,
            scratch_shapes=[
                pltpu.VMEM((1, 8), jnp.int32),
                pltpu.VMEM((1, 32), jnp.int32),
                pltpu.VMEM((4, 8), jnp.int32),
                pltpu.VMEM((2, 8), jnp.int32),
                pltpu.VMEM((8, 6), jnp.int32),
                pltpu.SMEM((1, 32), jnp.int32),
                pltpu.SMEM((4, 8), jnp.int32),
                pltpu.VMEM((3, 8, CELLS), F32),
                pltpu.VMEM((3, 8, CELLS), F32),
                field,
                pltpu.VMEM((24, n_mem * 24), F32),
                pltpu.VMEM((2, 8, CELLS), F32),
                pltpu.VMEM((2, 8, CELLS), F32),
                pltpu.VMEM((8, CELLS + FACE), F32),
                field,
                field,
                field,
                field,
                pltpu.VMEM((3, 8, CELLS), F32),
                pltpu.VMEM((64, LANES), F32),
                pltpu.VMEM((3, 8, LANES), F32),
                pltpu.VMEM((32, LANES), F32),
                pltpu.VMEM((32, LANES), F32),
                pltpu.VMEM((64, 3 * wide), BF16),
                pltpu.VMEM((wide, 192), BF16),
                pltpu.VMEM((32, 96), BF16),
                pltpu.VMEM((32, 3 * wide), BF16),
                pltpu.VMEM((2, 8, 8), F32),
                pltpu.VMEM((3, 8, n_mem * 24), F32),
                pltpu.VMEM((3, n_mem, 8, n_mem * 24), F32),
                pltpu.VMEM((3, 2, 8, n_mem * 24), F32),
                pltpu.VMEM((3, 32, n_mem * 24), F32),
                pltpu.VMEM((3, 2, 8, n_mem * 24), F32),
                pltpu.VMEM((8, LANES), F32),
                pltpu.VMEM((3, n_mem, 8, LANES), F32),
                pltpu.VMEM((64, LANES), F32),
                pltpu.VMEM((n_mem, 64, LANES), F32),
                pltpu.VMEM((n_mem, 8, LANES), F32),
                pltpu.VMEM((n_mem, 8, LANES), F32),
                pltpu.VMEM((2, 16, LANES), F32),
                pltpu.VMEM((2, 16, LANES), F32),
                dma,
                dma,
                dma((2,)),
                dma((2,)),
                dma,
                dma,
                dma((DEG,)),
                dma((DEG,)),
                dma((DEG, 2)),
                dma((DEG, 2)),
                dma((3,)),
                dma((3,)),
                dma((10,)),
                dma((2, 3)),
                *group_scratch(n_mem),
            ],
            compiler_params=pltpu.CompilerParams(
                collective_id=0, has_side_effects=True, vmem_limit_bytes=56 * 1024 * 1024
            ),
            name="vcycle",
        )(
            forcing,
            viscosity,
            coarse_solver,
            refinement.reshape(1, 8),
            face_owner.reshape(1, 32),
            face_block.T,
            plane_block.T,
            hanging,
        )
        return both[0], both[1]

    in_specs = (
        P(None, ("grp", "mem"), None),
        P(("grp", "mem"), None),
        P(("grp", "mem")),
        P(("grp", "mem"), None),
        P(("grp", "mem"), None),
        P(("grp", "mem"), None),
        P(("grp", "mem"), None),
        P("grp", "mem", None),
    )
    out_specs = (P(None, ("grp", "mem"), None), P(None, ("grp", "mem"), None))
    return jax.shard_map(local, mesh=mesh, in_specs=in_specs, out_specs=out_specs, check_vma=False)
```

```python
import functools
import math

import jax
import jax.numpy as jnp
from jax import lax
from jax.experimental import pallas as pl
from jax.experimental.pallas import tpu as pltpu
from jax.sharding import PartitionSpec as P

MESH = pl.DeviceIdType.MESH
EDGE = 16
DEG = 3
CELLS = 4096
FACE = 256
LANES = 128
CAP = 4
MASS_TERM = 1.0
LOWER_BOUND = 0.25
UPPER_BOUND = 2.0
SWEEPS = 2 * DEG
GROUPS = ((0,), (1, 2))
F32 = jnp.float32
BF16 = jnp.bfloat16


def chebyshev():
    theta = 0.5 * (UPPER_BOUND + LOWER_BOUND)
    delta = 0.5 * (UPPER_BOUND - LOWER_BOUND)
    sigma = theta / delta
    rho = 1.0 / sigma
    steps = [(0.0, 1.0 / theta)]
    for _ in range(DEG - 1):
        rho_next = 1.0 / (2.0 * sigma - rho)
        steps.append((rho_next * rho, 2.0 * rho_next / delta))
        rho = rho_next
    return steps


def far_first(members):
    tall = members // 4

    def hops(offset):
        dy, dx = offset
        return min(dy, tall - dy) + min(dx, 4 - dx)

    others = [(dy, dx) for dy in range(tall) for dx in range(4) if (dy, dx) != (0, 0)]
    return sorted(others, key=hops, reverse=True)


def by_step(step, values):
    result = jnp.float32(values[-1])
    for place in range(len(values) - 2, -1, -1):
        result = jnp.where(step == place, jnp.float32(values[place]), result)
    return result


def iota(shape, dim):
    return lax.broadcasted_iota(jnp.int32, shape, dim)


def turn(x, shift):
    shift = shift % LANES
    return x if shift == 0 else pltpu.roll(x, shift, 1)


def part(i, v):
    return pl.ds(i * FACE + v * LANES, LANES)


def parts(values):
    high = values.astype(BF16)
    rest = values - high.astype(F32)
    middle = rest.astype(BF16)
    low = (rest - middle.astype(F32)).astype(BF16)
    return jnp.concatenate([high, middle, low], axis=0)


def thrice(one_hot):
    return jnp.concatenate([one_hot] * 3, axis=1)


def pick(one_hot_thrice, values):
    return jnp.dot(one_hot_thrice, parts(values), preferred_element_type=F32)


def coarsen(x, start):
    lane = (iota(x.shape, 1) + (LANES - start)) % LANES
    x = x + jnp.where(lane % 2 == 0, turn(x, -1), turn(x, 1))
    x = x + jnp.where(lane // EDGE % 2 == 0, turn(x, -EDGE), turn(x, EDGE))
    return 0.25 * x


def extract(read):
    lane = iota((8, LANES), 1)
    in_row, row = lane % EDGE, lane // EDGE
    zero = jnp.zeros((8, LANES), F32)
    faces = {(v, d): zero for v in range(2) for d in range(4)}
    for i in range(EDGE):
        halves = (read(i, 0), read(i, 1))
        for v in range(2):
            moved = turn(halves[v], i)
            faces[v, 0] = jnp.where(in_row == i, moved, faces[v, 0])
            faces[v, 1] = jnp.where(in_row == (i - 1) % EDGE, moved, faces[v, 1])
        v = i // 8
        moved = turn(jnp.where(lane < EDGE, halves[0], halves[1]), i % 8 * EDGE)
        faces[v, 2] = jnp.where(row == i % 8, moved, faces[v, 2])
        faces[v, 3] = jnp.where(row == (i - 1) % 8, moved, faces[v, 3])
    for v in range(2):
        faces[v, 3] = turn(faces[v, 3], EDGE)
    return faces


def tables(owner, face_block, plane_block, hanging, members, has_lower, has_upper):
    wide = members * 8
    rows, columns = iota((32, 32), 0), iota((32, 32), 1)
    given = 4 * (rows % 8) + rows // 8
    given_t = 4 * (columns % 8) + columns // 8
    owner_col = jnp.sum(jnp.where(columns == given, owner, 0), axis=1, keepdims=True)
    own_col = jnp.sum(jnp.where(rows == columns, owner, 0), axis=1, keepdims=True)
    owner_row = jnp.sum(jnp.where(rows == given_t, own_col, 0), axis=0, keepdims=True)
    same = owner_col == owner_row
    rank_col = jnp.sum(jnp.where(same & (columns < rows), 1, 0), axis=1, keepdims=True)
    rank_row = jnp.sum(jnp.where(same & (rows < columns), 1, 0), axis=0, keepdims=True)

    def spread(table, first, of_row):
        tall = jnp.concatenate([table] * 4, axis=0)
        mask = iota(tall.shape, 1) == first + of_row(iota(tall.shape, 0))
        return jnp.sum(jnp.where(mask, tall, 0), axis=1, keepdims=True)

    def spread_t(table, per):
        lanes, which = iota((32, 8), 1), iota((32, 8), 0)
        tall = jnp.zeros((32, 8), jnp.int32)
        for d in range(table.shape[0]):
            tall = jnp.where(which // per == d, table[d : d + 1], tall)
        return jnp.sum(jnp.where(lanes == which % 8, tall, 0), axis=1, keepdims=True)

    block_col = spread_t(face_block, 8)
    side = iota((32, 1), 0) // 8
    wanted = (side + 1 - 2 * (side % 2)) * 8 + block_col
    slot_col = owner_col * 8 + rank_col
    slot_row = owner_row * 8 + rank_row

    def ones(mask):
        return jnp.where(mask, 1.0, 0.0).astype(BF16)

    lanes = iota((32, wide), 1)
    unpack = jnp.concatenate([ones(lanes == slot_col + CAP * v) for v in range(2)], axis=0)
    slots = iota((wide, 32), 0)
    unpack_t = jnp.concatenate([ones(slots == slot_row + CAP * v) for v in range(2)], axis=1)
    lanes = iota((32, LANES), 1)
    source = jnp.concatenate([ones(lanes % 64 == wanted + 32 * v) for v in range(2)], axis=0)
    request = jnp.dot(unpack_t, source, preferred_element_type=F32)
    plane_col = spread_t(plane_block, 16)
    which = iota((32, 32), 0) // 16
    inside = jnp.where(which == 0, has_lower, has_upper) == 1
    plane_pick = ones((columns == rows // 8 * 8 + plane_col) & inside)
    lanes, which = iota((8, 8), 1), iota((8, 8), 0)
    far_pick = []
    for d, exists in enumerate((has_lower, has_upper)):
        chosen = plane_block[d : d + 1]
        chosen = jnp.sum(jnp.where(lanes == which, chosen, 0), axis=1, keepdims=True)
        far_pick.append(jnp.where((lanes == chosen) & (exists == 1), 1.0, 0.0))
    lift_pick = ones(iota((32, wide), 1) == owner_col * 8 + block_col)
    near_hang = spread(hanging, 0, lambda r: r // 8)
    plane_hang = spread(hanging, 4, lambda r: r // 16)
    near_hang = jnp.broadcast_to(near_hang.astype(F32), (32, LANES))
    plane_hang = jnp.broadcast_to(plane_hang.astype(F32), (32, LANES))
    return (
        thrice(unpack),
        request,
        thrice(plane_pick),
        thrice(lift_pick),
        far_pick,
        near_hang,
        plane_hang,
    )


def kernel(
    n_grp,
    n_mem,
    forcing_hbm,
    viscosity_hbm,
    solver_hbm,
    refinement_hbm,
    owner_hbm,
    block_hbm,
    plane_hbm,
    hanging_hbm,
    result,
    refinement,
    face_owner,
    face_block,
    plane_block,
    hanging,
    owner_scalar,
    block_scalar,
    velocity,
    residual,
    effective,
    solver,
    weight_k,
    weight_j,
    weight_i,
    ghost_k,
    ghost_j,
    diagonal,
    inverse,
    step_dir,
    ghosts,
    lifts,
    hang_near,
    hang_plane,
    unpack_mat,
    pack_mat,
    plane_mat,
    lift_mat,
    far_mat,
    solver_rows,
    in_solver,
    in_far_solver,
    near_rows,
    far_rows,
    out_vector,
    in_vector,
    out_face,
    in_face,
    out_request,
    in_request,
    out_plane,
    in_plane,
    send_request,
    recv_request,
    send_plane,
    recv_plane,
    send_face,
    recv_face,
    send_solver,
    recv_solver,
    send_far,
    recv_far,
    send_vector,
    recv_vector,
    load_sem,
    store_sem,
    *group_refs,
):
    grp, mem = lax.axis_index("grp"), lax.axis_index("mem")
    above = lax.rem(grp + 1, n_grp)
    below = lax.rem(grp + n_grp - 1, n_grp)
    n_coarse = n_mem * 24
    buffers = [group_refs[8 * g : 8 * g + 8] for g in range(len(GROUPS))]
    groups_of_lanes = n_coarse // LANES
    wide = n_mem * 8

    mem_y, mem_x = lax.div(mem, 4), lax.rem(mem, 4)
    peers = [
        lax.rem(mem_y + dy, n_mem // 4) * 4 + lax.rem(mem_x + dx, 4) for dy, dx in far_first(n_mem)
    ]
    barrier = pltpu.get_barrier_semaphore()
    for to in peers:
        pl.semaphore_signal(barrier, inc=1, device_id={"mem": to}, device_id_type=MESH)
    for other in (above, below):
        pl.semaphore_signal(barrier, inc=1, device_id={"grp": other}, device_id_type=MESH)

    loads = [
        pltpu.make_async_copy(viscosity_hbm, effective, load_sem.at[0]),
        pltpu.make_async_copy(forcing_hbm, residual, load_sem.at[1]),
        pltpu.make_async_copy(solver_hbm.at[0], solver, load_sem.at[2]),
    ]
    small = [
        (refinement_hbm, refinement),
        (owner_hbm, face_owner),
        (block_hbm, face_block),
        (plane_hbm, plane_block),
        (hanging_hbm, hanging),
        (owner_hbm, owner_scalar),
        (block_hbm, block_scalar),
    ]
    small = [
        pltpu.make_async_copy(source, target, load_sem.at[3 + place])
        for place, (source, target) in enumerate(small)
    ]
    for load in [*small, *loads]:
        load.start()

    def store(place, c):
        source = (velocity, residual)[place]
        return pltpu.make_async_copy(
            source.at[c], result.at[place, c], store_sem.at[place, c]
        )

    lane = iota((8, LANES), 1)
    in_row = lane % EDGE
    row = lane // EDGE
    first_k, last_k = in_row == 0, in_row == EDGE - 1
    first_row, last_row = lane < EDGE, lane >= LANES - EDGE

    def send(outgoing, incoming, send_sem, recv_sem):
        for to in peers:
            pltpu.make_async_remote_copy(
                src_ref=outgoing.at[to],
                dst_ref=incoming.at[mem],
                send_sem=send_sem,
                recv_sem=recv_sem,
                device_id={"mem": to},
                device_id_type=MESH,
            ).start()

    def wait_for(buffer, sem, count=n_mem - 1):
        span = buffer.at[pl.ds(0, count)]
        pltpu.make_async_copy(span, span, sem).wait()

    def plane_copy(side, outgoing, incoming, send_sem, recv_sem):
        return pltpu.make_async_remote_copy(
            src_ref=outgoing.at[side],
            dst_ref=incoming.at[side],
            send_sem=send_sem.at[side],
            recv_sem=recv_sem.at[side],
            device_id={"grp": above if side == 0 else below},
            device_id_type=MESH,
        )

    def effective_plane(side):
        return plane_copy(side, out_plane, in_plane, send_plane, recv_plane)

    def step_plane(g, t, side):
        return plane_copy(side, *[ref.at[t] for ref in buffers[g][4:]])

    def far_solver(c, side):
        return pltpu.make_async_remote_copy(
            src_ref=solver_rows.at[c],
            dst_ref=in_far_solver.at[c, side],
            send_sem=send_far.at[c, side],
            recv_sem=recv_far.at[c, side],
            device_id={"grp": above if side == 0 else below},
            device_id_type=MESH,
        )

    for load in small:
        load.wait()

    block_row = iota((8, LANES), 0)
    level = jnp.sum(
        jnp.where(iota((8, 8), 0) == iota((8, 8), 1), refinement[...], 0), axis=1, keepdims=True
    )
    level = jnp.broadcast_to(level, (8, LANES))
    scale = 1.0 / jnp.left_shift(jnp.ones_like(level), level).astype(F32)
    loads[0].wait()
    for i in range(EDGE):
        for v in range(2):
            effective[:, part(i, v)] = effective[:, part(i, v)] * scale

    found = extract(lambda i, v: effective[:, part(i, v)])
    for (v, d), register in found.items():
        out_face[pl.ds(v * 32 + d * 8, 8), :] = register

    unpack, request, plane_pick, lift_pick, far_pick, near_hang, plane_hang = tables(
        face_owner[...],
        face_block[...],
        plane_block[...],
        hanging[...],
        n_mem,
        jnp.where(grp > 0, 1, 0),
        jnp.where(grp < n_grp - 1, 1, 0),
    )
    unpack_mat[...] = unpack
    plane_mat[...] = plane_pick
    lift_mat[...] = lift_pick
    for side in range(2):
        far_mat[side] = far_pick[side]
    hang_near[...] = near_hang
    hang_plane[...] = plane_hang
    out_request[...] = request.reshape(n_mem, 8, LANES)

    pl.semaphore_wait(barrier, n_mem - 1 + 2)

    for to in peers:
        pltpu.make_async_remote_copy(
            src_ref=out_face,
            dst_ref=in_face.at[mem],
            send_sem=send_face,
            recv_sem=recv_face,
            device_id={"mem": to},
            device_id_type=MESH,
        ).start()
    for v in range(2):
        out_plane[0, pl.ds(8 * v, 8), :] = effective[:, part(EDGE - 1, v)]
        out_plane[1, pl.ds(8 * v, 8), :] = effective[:, part(0, v)]
    for side in range(2):
        effective_plane(side).start()
    send(out_request, in_request, send_request, recv_request)
    in_face[mem] = out_face[...]
    in_request[mem] = out_request[mem]

    loads[1].wait()
    loads[2].wait()
    rows, columns = iota((24, 24), 0), iota((24, 24), 1)
    reorder = jnp.where(columns == 3 * (rows % 8) + rows // 8, 1.0, 0.0).astype(BF16)
    ordered = pick(thrice(reorder), solver[...])
    for c in range(3):
        solver_rows[c] = ordered[8 * c : 8 * c + 8]
    for c in range(3):
        for i in range(EDGE):
            for v in range(2):
                velocity[c, :, part(i, v)] = jnp.zeros((8, LANES), F32)
    for i in range(EDGE):
        own = [effective[:, part(i, v)] for v in range(2)]
        back = [turn(x, EDGE) for x in own]
        ahead = [turn(x, -EDGE) for x in own]
        for v in range(2):
            x = own[v]
            lower_k = jnp.where(first_k, 0.0, 0.5 * (x + turn(x, 1)))
            upper_k = jnp.where(last_k, 0.0, 0.5 * (x + turn(x, -1)))
            if v == 0:
                lower_j = jnp.where(first_row, 0.0, 0.5 * (x + back[0]))
                upper_j = 0.5 * (x + jnp.where(last_row, ahead[1], ahead[0]))
            else:
                lower_j = 0.5 * (x + jnp.where(first_row, back[0], back[1]))
                upper_j = jnp.where(last_row, 0.0, 0.5 * (x + ahead[1]))
            weight_k[0, :, part(i, v)] = lower_k
            weight_k[1, :, part(i, v)] = upper_k
            weight_j[0, :, part(i, v)] = lower_j
            weight_j[1, :, part(i, v)] = upper_j
            if i > 0:
                weight_i[:, part(i, v)] = 0.5 * (x + effective[:, part(i - 1, v)])
            diagonal[:, part(i, v)] = MASS_TERM * x + lower_k + upper_k + lower_j + upper_j

    def settle(values, hang, start=0):
        return jnp.where(hang == 1.0, coarsen(values, start), values)

    first_side = jnp.where(iota((32, LANES), 0) < 8, EDGE - 1, 0)

    def side_by_side(pieces):
        return pieces[0] if len(pieces) == 1 else jnp.concatenate(pieces, axis=1)

    def columns(values, count):
        return [values[:, l * LANES : (l + 1) * LANES] for l in range(count)]

    def receive(g, t):
        count = len(GROUPS[g])
        incoming, recv_sem, planes = buffers[g][1], buffers[g][3], buffers[g][5]
        for side in range(2):
            step_plane(g, t, side).wait_recv()
        far = pick(
            plane_mat[...],
            side_by_side([planes[t, :, l].reshape(32, LANES) for l in range(count)]),
        )
        far = [settle(values, hang_plane[...]) for values in columns(far, count)]
        wait_for(incoming.at[t], recv_sem.at[t])
        near = pick(
            unpack_mat[...],
            side_by_side([incoming[t, :, l].reshape(wide, LANES) for l in range(count)]),
        )
        result = []
        for l, values in enumerate(columns(near, count)):
            halves = [settle(values[32 * v : 32 * v + 32], hang_near[...], first_side) for v in range(2)]
            result.append(
                (
                    {(d, v): halves[v][8 * d : 8 * d + 8] for d in range(4) for v in range(2)},
                    {
                        (side, v): far[l][16 * side + 8 * v : 16 * side + 8 * v + 8]
                        for side in range(2)
                        for v in range(2)
                    },
                )
            )
        return result

    def near_ghosts(near):
        lower_k = [turn(near[0, v], -2 * (EDGE - 1)) for v in range(2)]
        upper_k = [near[1, v] for v in range(2)]
        lower_j = [near[2, v] for v in range(2)]
        upper_j = [turn(near[3, v], LANES - EDGE) for v in range(2)]

        def at_k(i, v):
            return turn(jnp.where(in_row == i, upper_k[v], lower_k[v]), EDGE - 1 - i)

        def at_j(i):
            both = jnp.where(row == i % 8, lower_j[i // 8], upper_j[i // 8])
            return turn(both, -(i % 8) * EDGE)

        return at_k, at_j

    for side in range(2):
        effective_plane(side).wait_recv()
    far = settle(pick(plane_mat[...], in_plane[...].reshape(32, LANES)), hang_plane[...])
    for v in range(2):
        weight_i[:, part(0, v)] = 0.5 * (effective[:, part(0, v)] + far[8 * v : 8 * v + 8])
        weight_i[:, part(EDGE, v)] = 0.5 * (
            effective[:, part(EDGE - 1, v)] + far[16 + 8 * v : 24 + 8 * v]
        )
    wait_for(in_face, recv_face)
    for d in range(4):
        for b in range(8):
            owner = owner_scalar[0, 4 * b + d]
            wanted = (d + 1 - 2 * (d % 2)) * 8 + block_scalar[d, b]
            for v in range(2):
                ghosts[pl.ds(v * 32 + d * 8 + b, 1), :] = in_face[
                    owner, pl.ds(v * 32 + wanted, 1), :
                ]
    halves = [settle(ghosts[pl.ds(32 * v, 32), :], hang_near[...], first_side) for v in range(2)]
    k_ghost, j_ghost = near_ghosts(
        {(d, v): halves[v][8 * d : 8 * d + 8] for d in range(4) for v in range(2)}
    )
    for i in range(EDGE):
        beside_j = j_ghost(i)
        for v in range(2):
            x = effective[:, part(i, v)]
            at_k = jnp.where(first_k | last_k, 0.5 * (x + k_ghost(i, v)), 0.0)
            edge = first_row if v == 0 else last_row
            at_j = jnp.where(edge, 0.5 * (x + beside_j), 0.0)
            ghost_k[:, part(i, v)] = at_k
            ghost_j[:, part(i, v)] = at_j
            whole = (
                diagonal[:, part(i, v)]
                + (weight_i[:, part(i, v)] + weight_i[:, part(i + 1, v)])
                + (at_k + at_j)
            )
            diagonal[:, part(i, v)] = whole
            inverse[:, part(i, v)] = 1.0 / whole

    steps = chebyshev()
    wait_for(in_request, recv_request)
    request = in_request[...].reshape(wide, LANES)
    pack_mat[...] = jnp.concatenate([request, request[:, :64]], axis=1).astype(BF16)

    def across_faces(c, near, far):
        k_ghost, j_ghost = near_ghosts(near)

        def new(i):
            beside_j = j_ghost(i)
            result = []
            for v in range(2):
                change = ghost_k[:, part(i, v)] * k_ghost(i, v)
                change = change + ghost_j[:, part(i, v)] * beside_j
                if i == 0:
                    change = change + weight_i[:, part(0, v)] * far[0, v]
                if i == EDGE - 1:
                    change = change + weight_i[:, part(EDGE, v)] * far[1, v]
                result.append(residual[c, :, part(i, v)] + change)
            return result

        return new

    def coarse_level():
        totals = [None] * 3
        for g, group in enumerate(GROUPS):
            for c, arrived in zip(group, receive(g, DEG - 1)):
                total = jnp.zeros((8, LANES), F32)
                new = across_faces(c, *arrived)
                for i in range(EDGE):
                    for v, value in enumerate(new(i)):
                        residual[c, :, part(i, v)] = value
                        total = total + value
                totals[c] = jnp.sum(total, axis=1, keepdims=True) / math.sqrt(CELLS)
        chunks = []
        for q in range(groups_of_lanes):
            place = lane + q * LANES - 24 * mem - 3 * block_row
            mine = jnp.zeros((8, LANES), F32)
            for c in range(3):
                mine = jnp.where(place == c, totals[c], mine)
            chunks.append(jnp.sum(mine, axis=0, keepdims=True))
        tile = jnp.zeros((8, LANES), F32)
        for q in range(groups_of_lanes):
            tile = jnp.where(block_row == q, chunks[q], tile)
        out_vector[...] = tile

        def send_vector_to(other, to, slot):
            pltpu.make_async_remote_copy(
                src_ref=out_vector,
                dst_ref=in_vector.at[slot, mem],
                send_sem=send_vector.at[slot],
                recv_sem=recv_vector.at[slot],
                device_id={"grp": other, "mem": to},
                device_id_type=MESH,
            ).start()

        for to in peers:
            send_vector_to(above, to, 1)
            send_vector_to(below, to, 2)
            send_vector_to(grp, to, 0)
        send_vector_to(above, mem, 1)
        send_vector_to(below, mem, 2)
        in_vector[0, mem] = tile

        for c in range(3):
            wait_for(in_solver.at[c], recv_solver.at[c])
            in_solver[c, mem] = solver_rows[c]
            near_rows[c] = pick(lift_mat[...], in_solver[c].reshape(wide, n_coarse))
            for side in range(2):
                far_solver(c, side).wait_recv()
                source = in_far_solver[c, side]
                chosen = jnp.zeros((8, n_coarse), F32)
                for b in range(8):
                    wants = far_mat[side][:, b : b + 1]
                    chosen = jnp.where(wants == 1.0, source[b : b + 1], chosen)
                far_rows[c, side] = chosen

        def vector_of(slot):
            whole = in_vector[slot, 0]
            for m in range(1, n_mem):
                whole = whole + in_vector[slot, m]
            return [jnp.broadcast_to(whole[q : q + 1], (8, LANES)) for q in range(groups_of_lanes)]

        def correction(rows, vector):
            product = rows[:, :LANES] * vector[0]
            for q in range(1, groups_of_lanes):
                product = product + rows[:, q * LANES : (q + 1) * LANES] * vector[q]
            return jnp.broadcast_to(jnp.sum(product, axis=1, keepdims=True), (8, LANES))

        for side in range(2):
            wait_for(in_vector.at[1 + side], recv_vector.at[1 + side], n_mem)
        far_vectors = [vector_of(1), vector_of(2)]
        wait_for(in_vector.at[0], recv_vector.at[0])
        vector = vector_of(0)
        def lifted(c):
            mine = correction(solver_rows[c], vector)
            lifts[c] = mine
            gap = [mine - correction(near_rows[c, pl.ds(8 * d, 8), :], vector) for d in range(4)]
            gap_lower, gap_upper = [
                mine - correction(far_rows[c, side], far_vectors[side]) for side in range(2)
            ]
            gap_k = jnp.where(first_k, gap[0], gap[1])

            def new(i):
                result = []
                for v in range(2):
                    change = MASS_TERM * effective[:, part(i, v)] * mine
                    change = change + ghost_k[:, part(i, v)] * gap_k
                    change = change + ghost_j[:, part(i, v)] * gap[2 + v]
                    if i == 0:
                        change = change + weight_i[:, part(0, v)] * gap_lower
                    if i == EDGE - 1:
                        change = change + weight_i[:, part(EDGE, v)] * gap_upper
                    result.append(residual[c, :, part(i, v)] - change)
                return result

            return new

        return lifted

    def advance(g, t, news, keep, gain):
        outgoing, incoming, send_sem, recv_sem, planes = buffers[g][:5]
        group = GROUPS[g]
        columns_out = []
        for l, c in enumerate(group):
            moved = {}

            def step_of(i, v):
                if v == 0:
                    for half, value in enumerate(news[l](i)):
                        if keep is not None or t == DEG:
                            residual[c, :, part(i, half)] = value
                        ahead = gain * (value * inverse[:, part(i, half)])
                        if keep is not None:
                            ahead = keep * step_dir[c, :, part(i, half)] + ahead
                        step_dir[c, :, part(i, half)] = ahead
                        moved[i, half] = ahead
                return moved[i, v]

            found = extract(step_of)
            columns_out.append(
                jnp.concatenate([found[v, d] for v in range(2) for d in range(4)], axis=0)
            )
        packed = columns(pick(pack_mat[...], side_by_side(columns_out)), len(group))
        for l in range(len(group)):
            outgoing[t, :, l] = packed[l].reshape(n_mem, 8, LANES)
        send(outgoing.at[t], incoming.at[t], send_sem.at[t], recv_sem.at[t])
        for l, c in enumerate(group):
            for v in range(2):
                planes[t, 0, l, pl.ds(8 * v, 8), :] = step_dir[c, :, part(EDGE - 1, v)]
                planes[t, 1, l, pl.ds(8 * v, 8), :] = step_dir[c, :, part(0, v)]
        for side in range(2):
            step_plane(g, t, side).start()
        incoming[t, mem] = outgoing[t, mem]

    def send_solver_rows(c):
        for to in peers:
            pltpu.make_async_remote_copy(
                src_ref=solver_rows.at[c],
                dst_ref=in_solver.at[c, mem],
                send_sem=send_solver.at[c],
                recv_sem=recv_solver.at[c],
                device_id={"mem": to},
                device_id_type=MESH,
            ).start()
        for side in range(2):
            far_solver(c, side).start()

    def inside(lift):
        @pl.loop(0, 3)
        def _(c):
            for i in range(EDGE):
                own = [step_dir[c, :, part(i, v)] for v in range(2)]
                back = [turn(x, EDGE) for x in own]
                ahead = [turn(x, -EDGE) for x in own]
                for v in range(2):
                    x = own[v]
                    if v == 0:
                        lower_j, upper_j = back[0], jnp.where(last_row, ahead[1], ahead[0])
                    else:
                        lower_j, upper_j = jnp.where(first_row, back[0], back[1]), ahead[1]
                    change = weight_k[0, :, part(i, v)] * turn(x, 1)
                    change = change + weight_k[1, :, part(i, v)] * turn(x, -1)
                    change = change + weight_j[0, :, part(i, v)] * lower_j
                    change = change + weight_j[1, :, part(i, v)] * upper_j
                    if i > 0:
                        change = change + weight_i[:, part(i, v)] * step_dir[c, :, part(i - 1, v)]
                    if i < EDGE - 1:
                        change = change + weight_i[:, part(i + 1, v)] * step_dir[
                            c, :, part(i + 1, v)
                        ]
                    residual[c, :, part(i, v)] = residual[c, :, part(i, v)] - (
                        diagonal[:, part(i, v)] * x - change
                    )
                    if lift:
                        x = x + lifts[c]
                    velocity[c, :, part(i, v)] = velocity[c, :, part(i, v)] + x

    def as_is(c):
        return lambda i: [residual[c, :, part(i, v)] for v in range(2)]

    def later(first):
        def sweep(t, carry):
            keep = by_step(t - first, [value for value, _ in steps])
            gain = by_step(t - first, [value for _, value in steps])
            for g, group in enumerate(GROUPS):
                news = [
                    across_faces(c, *arrived) for c, arrived in zip(group, receive(g, t - 1))
                ]
                advance(g, t, news, keep, gain)
            inside(False)
            if first == 0:
                send_solver_rows(t)
            return carry

        lax.fori_loop(first + 1, first + DEG, sweep, 0)

    for g, group in enumerate(GROUPS):
        advance(g, 0, [as_is(c) for c in group], None, jnp.float32(steps[0][1]))
    inside(False)
    send_solver_rows(0)
    later(0)
    lifted = coarse_level()
    for g, group in enumerate(GROUPS):
        advance(g, DEG, [lifted(c) for c in group], None, jnp.float32(steps[0][1]))
    inside(True)
    later(DEG)
    for c in range(3):
        store(0, c).start()
    for g, group in enumerate(GROUPS):
        for c, arrived in zip(group, receive(g, SWEEPS - 1)):
            new = across_faces(c, *arrived)
            for i in range(EDGE):
                for v, value in enumerate(new(i)):
                    residual[c, :, part(i, v)] = value
            store(1, c).start()

    wait_for(in_face, send_face)
    for g in range(len(GROUPS)):
        for t in range(SWEEPS):
            wait_for(buffers[g][0].at[t], buffers[g][2].at[t])
            for side in range(2):
                step_plane(g, t, side).wait_send()
    for t in range(DEG):
        wait_for(in_solver.at[t], send_solver.at[t])
        for side in range(2):
            far_solver(t, side).wait_send()
    wait_for(in_vector.at[0], send_vector.at[0])
    for side in range(2):
        wait_for(in_vector.at[1 + side], send_vector.at[1 + side], n_mem)
    wait_for(out_request, send_request)
    for side in range(2):
        effective_plane(side).wait_send()
    for place in range(2):
        for c in range(3):
            store(place, c).wait()


def group_scratch(n_mem):
    shapes = []
    for group in GROUPS:
        near = pltpu.VMEM((SWEEPS, n_mem, len(group), 8, LANES), F32)
        far = pltpu.VMEM((SWEEPS, 2, len(group), 16, LANES), F32)
        dma = pltpu.SemaphoreType.DMA
        shapes += [near, near, dma((SWEEPS,)), dma((SWEEPS,))]
        shapes += [far, far, dma((SWEEPS, 2)), dma((SWEEPS, 2))]
    return shapes


def solution(mesh):
    n_grp, n_mem = mesh.shape["grp"], mesh.shape["mem"]
    wide = n_mem * 8

    def local(
        forcing,
        viscosity,
        refinement,
        face_owner,
        face_block,
        plane_block,
        hanging,
        coarse_solver,
    ):
        field = pltpu.VMEM((8, CELLS), F32)
        hbm = pl.BlockSpec(memory_space=pltpu.HBM)
        dma = pltpu.SemaphoreType.DMA
        both = pl.pallas_call(
            functools.partial(kernel, n_grp, n_mem),
            out_shape=jax.ShapeDtypeStruct((2, *forcing.shape), F32),
            in_specs=[hbm] * 8,
            out_specs=hbm,
            scratch_shapes=[
                pltpu.VMEM((1, 8), jnp.int32),
                pltpu.VMEM((1, 32), jnp.int32),
                pltpu.VMEM((4, 8), jnp.int32),
                pltpu.VMEM((2, 8), jnp.int32),
                pltpu.VMEM((8, 6), jnp.int32),
                pltpu.SMEM((1, 32), jnp.int32),
                pltpu.SMEM((4, 8), jnp.int32),
                pltpu.VMEM((3, 8, CELLS), F32),
                pltpu.VMEM((3, 8, CELLS), F32),
                field,
                pltpu.VMEM((24, n_mem * 24), F32),
                pltpu.VMEM((2, 8, CELLS), F32),
                pltpu.VMEM((2, 8, CELLS), F32),
                pltpu.VMEM((8, CELLS + FACE), F32),
                field,
                field,
                field,
                field,
                pltpu.VMEM((3, 8, CELLS), F32),
                pltpu.VMEM((64, LANES), F32),
                pltpu.VMEM((3, 8, LANES), F32),
                pltpu.VMEM((32, LANES), F32),
                pltpu.VMEM((32, LANES), F32),
                pltpu.VMEM((64, 3 * wide), BF16),
                pltpu.VMEM((wide, 192), BF16),
                pltpu.VMEM((32, 96), BF16),
                pltpu.VMEM((32, 3 * wide), BF16),
                pltpu.VMEM((2, 8, 8), F32),
                pltpu.VMEM((3, 8, n_mem * 24), F32),
                pltpu.VMEM((3, n_mem, 8, n_mem * 24), F32),
                pltpu.VMEM((3, 2, 8, n_mem * 24), F32),
                pltpu.VMEM((3, 32, n_mem * 24), F32),
                pltpu.VMEM((3, 2, 8, n_mem * 24), F32),
                pltpu.VMEM((8, LANES), F32),
                pltpu.VMEM((3, n_mem, 8, LANES), F32),
                pltpu.VMEM((64, LANES), F32),
                pltpu.VMEM((n_mem, 64, LANES), F32),
                pltpu.VMEM((n_mem, 8, LANES), F32),
                pltpu.VMEM((n_mem, 8, LANES), F32),
                pltpu.VMEM((2, 16, LANES), F32),
                pltpu.VMEM((2, 16, LANES), F32),
                dma,
                dma,
                dma((2,)),
                dma((2,)),
                dma,
                dma,
                dma((DEG,)),
                dma((DEG,)),
                dma((DEG, 2)),
                dma((DEG, 2)),
                dma((3,)),
                dma((3,)),
                dma((10,)),
                dma((2, 3)),
                *group_scratch(n_mem),
            ],
            compiler_params=pltpu.CompilerParams(
                collective_id=0, has_side_effects=True, vmem_limit_bytes=56 * 1024 * 1024
            ),
            name="vcycle",
        )(
            forcing,
            viscosity,
            coarse_solver,
            refinement.reshape(1, 8),
            face_owner.reshape(1, 32),
            face_block.T,
            plane_block.T,
            hanging,
        )
        return both[0], both[1]

    in_specs = (
        P(None, ("grp", "mem"), None),
        P(("grp", "mem"), None),
        P(("grp", "mem")),
        P(("grp", "mem"), None),
        P(("grp", "mem"), None),
        P(("grp", "mem"), None),
        P(("grp", "mem"), None),
        P("grp", "mem", None),
    )
    out_specs = (P(None, ("grp", "mem"), None), P(None, ("grp", "mem"), None))
    return jax.shard_map(local, mesh=mesh, in_specs=in_specs, out_specs=out_specs, check_vma=False)
```
